128 devices in a mesh: tm: 32 (over z, x_hi, y), rows: 4 (over x_lo, core).
Axes of the slice: x: 4 (x_hi: 2, x_lo: 2; x = x_hi * 2 + x_lo), y: 4, z: 4, core: 2. Of those that a mesh axis runs over, the one named last changes fastest.
Arguments:
- video_clip: bfloat16 [256, 56, 7, 512], P('tm', 'rows'), may hold values from -6 to 6
- cotangent: bfloat16 [256, 56, 7, 512], P('tm', 'rows'), may hold values from -6 to 6
- gain_first: float32 [512], replicated, may hold values from 0.1 to 1.9
- bias_first: float32 [512], replicated, may hold values from -3 to 3
- qkv_first: bfloat16 [512, 1536], replicated
- out_first: bfloat16 [512, 512], replicated, may hold values from -0.25 to 0.25
- gain_second: float32 [512], replicated, may hold values from 0.1 to 1.9
- bias_second: float32 [512], replicated, may hold values from -3 to 3
- qkv_second: bfloat16 [512, 1536], replicated
- out_second: bfloat16 [512, 512], replicated, may hold values from -0.25 to 0.25
Outputs:
- grad_clip: bfloat16 [256, 56, 7, 512], P('tm', 'rows')
- grad_qkv_first: float32 [512, 1536], P(('tm', 'rows'))
- grad_out_first: float32 [512, 512], P(('tm', 'rows'))
- grad_qkv_second: float32 [512, 1536], P(('tm', 'rows'))
- grad_out_second: float32 [512, 512], P(('tm', 'rows'))
The draws below stay inside these ranges and needn't reach their ends.
All inputs are finite; a program needn't handle non-finite values.
Results may differ from the reference program's by a relative error of at most 0.03.
Values may be sent and summed in bfloat16 or wider, within the bound.
A program may use at most 256 MiB of HBM per device.

```python
import math
import jax
import jax.numpy as jnp
from jax import lax

C = 512
HEADS = 16
WT = 8
WH = 7
WW = 7
H = 56
W = 7
FRAMES = 256


def projection_entries(key, column_factor):
    entries = jax.random.normal(key, (C, 3 * C), jnp.float32) * C ** (-0.5)
    column_index = jnp.arange(3 * C)
    return entries * jnp.where(column_index < 2 * C, column_factor, 1.0)[None, :]


def draw_qkv_first(key, part):
    key = jax.random.fold_in(key, 11)
    entries = projection_entries(key, 1.0)
    return entries.astype(jnp.bfloat16)


def draw_qkv_second(key, part):
    key = jax.random.fold_in(key, 23)
    entries = projection_entries(key, 1.0)
    return entries.astype(jnp.bfloat16)


def levels(rng, shape, split, low, high):
    level = 1.0
    for dim, blocks in split:
        steps = jax.random.uniform(jax.random.fold_in(jax.random.fold_in(rng, 6), dim), (blocks,), jnp.float32, low / len(split), high / len(split))
        level = level * jnp.repeat(jnp.exp(steps), shape[dim] // blocks).reshape((-1,) + (1,) * (len(shape) - 1 - dim))
    return level


def gaussian(key, dims, scale, most, shards=(), kind=jnp.bfloat16):
    values = scale * jax.random.normal(key, dims, jnp.float32)
    if shards:
        values = values * levels(key, dims, shards, -0.22, 0.18)
    return jnp.clip(values, -most, most).astype(kind)


def setup_inputs(seed: int = 0) -> dict:
    streams_of = jax.random.split(jax.random.key(seed), 11)
    video_clip = gaussian(streams_of[0], (FRAMES, H, W, C), 1.0, 6.0, ((0, 32), (1, 4)))
    cotangent = gaussian(streams_of[1], (FRAMES, H, W, C), 1.0, 6.0, ((0, 32), (1, 4)))
    gain_first = jnp.clip(1.0 + 0.18 * jax.random.normal(streams_of[2], (C,), jnp.float32), 0.1, 1.9)
    bias_first = gaussian(streams_of[3], (C,), 0.5, 3.0, (), jnp.float32)
    qkv_first = draw_qkv_first(jax.random.fold_in(streams_of[10], 71), 0)
    out_first = gaussian(streams_of[5], (C, C), C ** -0.5, 0.25)
    gain_second = jnp.clip(1.0 + 0.18 * jax.random.normal(streams_of[6], (C,), jnp.float32), 0.1, 1.9)
    bias_second = gaussian(streams_of[7], (C,), 0.5, 3.0, (), jnp.float32)
    qkv_second = draw_qkv_second(jax.random.fold_in(streams_of[10], 71), 0)
    out_second = gaussian(streams_of[9], (C, C), C ** -0.5, 0.25)
    return {"video_clip": video_clip, "cotangent": cotangent, "gain_first": gain_first, "bias_first": bias_first, "qkv_first": qkv_first, "out_first": out_first, "gain_second": gain_second, "bias_second": bias_second, "qkv_second": qkv_second, "out_second": out_second}


def to_windows(volume):
    frames, rows_here, columns, channels = volume.shape
    blocked = volume.reshape(frames // WT, WT, rows_here // WH, WH, columns // WW, WW, channels)
    blocked = blocked.transpose(0, 2, 4, 1, 3, 5, 6)
    return blocked.reshape(-1, WT * WH * WW, channels)

def from_windows(windowed, frames, rows_here, columns):
    channels = windowed.shape[-1]
    blocked = windowed.reshape(frames // WT, rows_here // WH, columns // WW, WT, WH, WW, channels)
    return blocked.transpose(0, 3, 1, 4, 2, 5, 6).reshape(frames, rows_here, columns, channels)

def region(position, length, extent):
    return jnp.where(position < length - extent, 0, jnp.where(position < length - extent // 2, 1, 2)).astype(jnp.int32)

def region_labels(time_pos, time_len, row_pos, row_len, columns):
    col_pos = jnp.arange(columns, dtype=jnp.int32)
    labels = region(time_pos, time_len, WT)[:, None, None] * 9 + region(row_pos, row_len, WH)[None, :, None] * 3 + region(col_pos, columns, WW)[None, None, :]
    return to_windows(labels[..., None])[..., 0]

def normalize(values_in, norm_gain, norm_bias):
    center = values_in - lax.optimization_barrier(jnp.mean(values_in, axis=-1, keepdims=True))
    spread = lax.optimization_barrier(jnp.mean(center * center, axis=-1, keepdims=True))
    return (center * lax.rsqrt(spread + 1e-05) * norm_gain + norm_bias).astype(jnp.bfloat16)

def attend(projected, same_region):
    windows, length, triple = projected.shape
    channels = triple // 3
    head_size = channels // HEADS
    packed = lax.optimization_barrier(projected.astype(jnp.bfloat16))
    packed = packed.astype(jnp.float32).reshape(windows, length, 3, HEADS, head_size)
    query_rows = packed[:, :, 0]
    key_rows = packed[:, :, 1]
    value_rows = packed[:, :, 2]
    scores = jnp.einsum('nqhd,nkhd->nhqk', query_rows, key_rows) * head_size ** (-0.5)
    scores = jnp.where(same_region[:, None], scores, -1000000000.0)
    weights = lax.optimization_barrier(jax.nn.softmax(scores, axis=-1).astype(jnp.bfloat16))
    mixed = jnp.einsum('nhqk,nkhd->nqhd', weights.astype(jnp.float32), value_rows)
    return mixed.astype(jnp.bfloat16).reshape(windows, length, channels)

def forward_block(windows_in, norm_gain, norm_bias, w_qkv, same_region):
    windows, length, channels = windows_in.shape
    input_float = windows_in.astype(jnp.float32)
    normed, pull_norm = jax.vjp(lambda values_in: normalize(values_in, norm_gain, norm_bias), input_float)
    normed_rows = normed.reshape(-1, channels)
    projected = jnp.dot(normed_rows, w_qkv, preferred_element_type=jnp.float32).reshape(windows, length, 3 * channels)
    mixed, pull_attend = jax.vjp(lambda inner: attend(inner, same_region), projected)
    return (input_float, normed_rows, mixed, pull_norm, pull_attend)

def block_output(saved, w_out):
    input_float, normed_rows, mixed, pull_norm, pull_attend = saved
    channels = mixed.shape[-1]
    added = jnp.dot(mixed.reshape(-1, channels), w_out, preferred_element_type=jnp.float32)
    return (input_float + added.reshape(input_float.shape)).astype(jnp.bfloat16)

def backward_block(saved, grads_in, w_qkv, w_out):
    input_float, normed_rows, mixed, pull_norm, pull_attend = saved
    channels = mixed.shape[-1]
    grad_rows = grads_in.reshape(-1, channels)
    mixed_rows = mixed.reshape(-1, channels)
    grad_out = jnp.dot(mixed_rows.T, grad_rows, preferred_element_type=jnp.float32)
    d_mixed = jnp.dot(grad_rows, w_out.T, preferred_element_type=jnp.float32).astype(jnp.bfloat16)
    d_projected, = pull_attend(d_mixed.reshape(mixed.shape))
    d_projected = d_projected.astype(jnp.bfloat16).reshape(-1, 3 * channels)
    grad_qkv = jnp.dot(normed_rows.T, d_projected, preferred_element_type=jnp.float32)
    d_normed = jnp.dot(d_projected, w_qkv.T, preferred_element_type=jnp.float32).astype(jnp.bfloat16)
    d_input, = pull_norm(d_normed.reshape(input_float.shape))
    d_total = (grads_in.astype(jnp.float32) + d_input).astype(jnp.bfloat16)
    return (d_total, grad_qkv, grad_out)

def grouped(arrays):
    window_total = arrays[0].shape[0]
    per_group = math.gcd(window_total, 4)
    return tuple((item.reshape((window_total // per_group, per_group) + item.shape[1:]) for item in arrays))

def forward_grouped(windows_in, labels, norm_gain, norm_bias, w_qkv, w_out):

    def one_group(pieces):
        same_region = pieces[1][:, :, None] == pieces[1][:, None, :]
        return block_output(forward_block(pieces[0], norm_gain, norm_bias, w_qkv, same_region), w_out)
    result = lax.map(one_group, grouped((windows_in, labels)))
    return result.reshape(windows_in.shape)

def run_grouped(windows_in, grads_in, labels, norm_gain, norm_bias, w_qkv, w_out):

    def one_group(running, pieces):
        same_region = pieces[2][:, :, None] == pieces[2][:, None, :]
        saved = forward_block(pieces[0], norm_gain, norm_bias, w_qkv, same_region)
        d_piece, q_piece, o_piece = backward_block(saved, pieces[1], w_qkv, w_out)
        return ((running[0] + q_piece, running[1] + o_piece), d_piece)
    start = (jnp.zeros(w_qkv.shape, jnp.float32), jnp.zeros(w_out.shape, jnp.float32))
    (grad_qkv, grad_out), d_windows = lax.scan(one_group, start, grouped((windows_in, grads_in, labels)))
    return (d_windows.reshape(windows_in.shape), grad_qkv, grad_out)

def reference(video_clip, cotangent, gain_first, bias_first, qkv_first, out_first, gain_second, bias_second, qkv_second, out_second):
    frames, rows_all, columns, channels = video_clip.shape
    clip_windows = to_windows(video_clip)
    plain_labels = jnp.zeros(clip_windows.shape[:2], jnp.int32)
    first_out = from_windows(forward_grouped(clip_windows, plain_labels, gain_first, bias_first, qkv_first, out_first), frames, rows_all, columns)
    offsets = (-(WT // 2), -(WH // 2), -(WW // 2))
    shifted = jnp.roll(first_out, offsets, axis=(0, 1, 2))
    cot_second = jnp.roll(cotangent, offsets, axis=(0, 1, 2))
    labels = region_labels(jnp.arange(frames, dtype=jnp.int32), frames, jnp.arange(rows_all, dtype=jnp.int32), rows_all, columns)
    d_shifted, grad_qkv_second, grad_out_second = run_grouped(to_windows(shifted), to_windows(cot_second), labels, gain_second, bias_second, qkv_second, out_second)
    cot_first = jnp.roll(from_windows(d_shifted, frames, rows_all, columns), (WT // 2, WH // 2, WW // 2), axis=(0, 1, 2))
    d_clip, grad_qkv_first, grad_out_first = run_grouped(clip_windows, to_windows(cot_first), plain_labels, gain_first, bias_first, qkv_first, out_first)
    grad_scale = 1.0 / math.sqrt(frames * rows_all * columns)
    return (from_windows(d_clip, frames, rows_all, columns), grad_qkv_first * grad_scale, grad_out_first * grad_scale, grad_qkv_second * grad_scale, grad_out_second * grad_scale)
```

```python
import functools
import math

import jax
import jax.numpy as jnp
from jax import lax
from jax.experimental import pallas as pl
from jax.experimental.pallas import tpu as pltpu
from jax.sharding import PartitionSpec as P

F32, BF16 = jnp.float32, jnp.bfloat16
C, HEADS, HD = 512, 16, 32
TOK = 392
GROUP = 4
VROWS = 48
LOG2E = math.log2(math.e)
QSCALE = HD ** (-0.5) * LOG2E
MASKED = -1000000000.0 * LOG2E
LOW, HIGH = 2.0**-60, 2.0**100
WHOLE = ((0, 392, 0),)
SPLIT = ((0, 224, 0), (224, 392, 256))
VMEM_LIMIT = 56 * 1024 * 1024


def mm(a, b):
    return lax.dot_general(a, b, (((1,), (0,)), ((), ())), preferred_element_type=F32)


def mm_nt(a, b):
    return lax.dot_general(a, b, (((1,), (1,)), ((), ())), preferred_element_type=F32)


def mm_tn(a, b):
    return lax.dot_general(a, b, (((0,), (0,)), ((), ())), preferred_element_type=F32)


def standardized(values):
    center = values - jnp.mean(values, axis=-1, keepdims=True)
    rstd = lax.rsqrt(jnp.mean(center * center, axis=-1, keepdims=True) + 1e-05)
    return center * rstd, rstd


def tiles(block):
    return block.astype(F32).reshape(-1, C)


def head_rows(j, block):
    row = lax.broadcasted_iota(jnp.int32, block.shape, 0) // HD
    return jnp.where(row == j, block, jnp.zeros_like(block))


def head_lanes(j, block):
    lane = lax.broadcasted_iota(jnp.int32, block.shape, 1) // HD
    return jnp.where(lane == j, block, jnp.zeros_like(block))


def store_transposed(ref, block, segments, row0=0):
    for start, stop, lane in segments:
        ref[row0 : row0 + block.shape[1], lane : lane + stop - start] = block[start:stop].T


def store_values(vt, block, segments):
    for start, stop, lane in segments:
        turned = block[start:stop].T
        count = stop - start
        for head in range(HEADS):
            vt[VROWS * head : VROWS * head + HD, lane : lane + count] = turned[
                HD * head : HD * (head + 1)
            ]
            vt[VROWS * head + HD : VROWS * (head + 1), lane : lane + count] = jnp.ones(
                (VROWS - HD, count), BF16
            )


def out_of_range(sums):
    return jnp.where((sums > LOW) & (sums < HIGH), 0.0, 1.0)


def forward_kernel(
    x_ref, gain_ref, bias_ref, wqkv_ref, wout_ref,
    e_ref, mixt_ref, inv_ref, own_ref, row_ref, tm_ref, corner_ref,
    qt, k, vt,
):
    w, g = pl.program_id(0), pl.program_id(1)

    @pl.when(g == 0)
    def _():
        xhat, _ = standardized(tiles(x_ref[...]))
        normed = (xhat * gain_ref[...] + bias_ref[...]).astype(BF16)
        store_transposed(qt, (mm(normed, wqkv_ref[:, 0:C]) * QSCALE).astype(BF16), WHOLE)
        k[...] = mm(normed, wqkv_ref[:, C : 2 * C]).astype(BF16)
        store_values(vt, mm(normed, wqkv_ref[:, 2 * C :]).astype(BF16), WHOLE)

    base = pl.multiple_of(g * 128, 128)
    kg = k[:, pl.ds(base, 128)]
    qtg = qt[pl.ds(base, 128), :]

    def head(j, shifted):
        scores = mm(kg, head_rows(j, qtg))
        if shifted:
            scores = scores - jnp.max(scores, axis=0, keepdims=True)
        e = jnp.exp2(scores).astype(BF16)
        e_ref[0, j] = e
        mixed = mm(vt[pl.ds(pl.multiple_of(g * 4 * VROWS + j * VROWS, 16), VROWS), :], e)
        sums = mixed[HD : HD + 1]
        inv = 1.0 / sums
        inv_ref[0, 0, pl.ds(j, 1), :] = inv
        mixt_ref[0, pl.ds(pl.multiple_of(base + j * HD, HD), HD), :] = (mixed[:HD] * inv).astype(BF16)
        return out_of_range(sums)

    bad = head(0, False)
    for j in range(1, GROUP):
        bad = bad + head(j, False)

    @pl.when(jnp.max(bad) > 0.0)
    def _():
        def step(j, carry):
            head(j, True)
            return carry

        lax.fori_loop(0, GROUP, step, 0)

    @pl.when(g == GROUP - 1)
    def _():
        y = tiles(x_ref[...]) + mm_tn(mixt_ref[0], wout_ref[...])
        y = y.reshape(7, 7, 8, C).astype(BF16)
        low = y.astype(F32)[:, :, 0:4].astype(BF16)
        own_ref[...] = y

        @pl.when(w == 0)
        def _():
            row_ref[...] = y[0:3]
            corner_ref[...] = low[0:3]
            tm_ref[0:4] = low[3:7]

        @pl.when(w == 1)
        def _():
            tm_ref[4:11] = low


def norm_backward(dnormed, xhat, rstd, gain):
    d = dnormed.astype(BF16).astype(F32) * gain
    return rstd * (
        d
        - jnp.mean(d, axis=-1, keepdims=True)
        - xhat * jnp.mean(d * xhat, axis=-1, keepdims=True)
    )


def backward_first_kernel(
    scale,
    x_ref, gain_ref, bias_ref, wqkv_ref, wout_ref, e_ref, mixt_ref, inv_ref,
    own_ref, row_ref, tm_ref, corner_ref,
    grad_ref, gqkv_ref, gout_ref,
    xhat_s, rstd_s, normed_s, cot_s, q, kt, v, dot_s, dopt, dqt, dproj,
):
    w, g = pl.program_id(0), pl.program_id(1)

    @pl.when(g == 0)
    def _():
        xhat, rstd = standardized(tiles(x_ref[...]))
        xhat_s[...] = xhat
        rstd_s[...] = rstd
        normed = (xhat * gain_ref[...] + bias_ref[...]).astype(BF16)
        normed_s[...] = normed
        q[...] = mm(normed, wqkv_ref[:, 0:C]).astype(BF16)
        store_transposed(kt, mm(normed, wqkv_ref[:, C : 2 * C]).astype(BF16), WHOLE)
        v[...] = mm(normed, wqkv_ref[:, 2 * C :]).astype(BF16)

        def put(row, count, low, high):
            whole = jnp.concatenate([low.astype(F32), high.astype(F32)[:, :, 4:8]], axis=2)
            cot_s[56 * row : 56 * (row + count)] = whole.reshape(-1, C)

        @pl.when(w == 0)
        def _():
            put(0, 3, corner_ref[...], row_ref[...])
            put(3, 4, tm_ref[0:4], own_ref[3:7])

        @pl.when(w == 1)
        def _():
            put(0, 7, tm_ref[4:11], own_ref[7:14])

        dot_s[...] = mm_nt(wout_ref[...], cot_s[...].astype(BF16)).astype(BF16)

    base = pl.multiple_of(g * 128, 128)
    vg = v[:, pl.ds(base, 128)]
    qg = q[:, pl.ds(base, 128)]
    ds_all = []
    for j in range(GROUP):
        rows = pl.ds(pl.multiple_of(base + HD * j, HD), HD)
        inv = inv_ref[0, 0, j : j + 1, :]
        do = dot_s[rows, :].astype(F32) * inv
        dsum = jnp.sum(mixt_ref[0, rows, :].astype(F32) * do, axis=0, keepdims=True)
        dopt[HD * j : HD * (j + 1), :] = do.astype(BF16)
        ds_all.append(dsum)
    dopg = dopt[...]
    dopn = dopg.T
    dv = dk = None
    for j in range(GROUP):
        e = e_ref[0, j]
        dp = mm(vg, head_rows(j, dopg)) - ds_all[j]
        ds = (e.astype(F32) * dp).astype(BF16)
        rows = pl.ds(pl.multiple_of(base + HD * j, HD), HD)
        dqt[HD * j : HD * (j + 1), :] = (mm(kt[rows, :], ds) * HD ** (-0.5)).astype(BF16)
        dv_j = mm(e, head_lanes(j, dopn))
        dk_j = mm(ds, head_lanes(j, qg))
        dv = dv_j if dv is None else dv + dv_j
        dk = dk_j if dk is None else dk + dk_j
    dproj[:, pl.ds(base, 128)] = dqt[...].T
    dproj[:, pl.ds(pl.multiple_of(base + C, 128), 128)] = (dk * HD ** (-0.5)).astype(BF16)
    dproj[:, pl.ds(pl.multiple_of(base + 2 * C, 128), 128)] = dv.astype(BF16)

    @pl.when(g == GROUP - 1)
    def _():
        gout = mm(mixt_ref[0], cot_s[...].astype(BF16)) * scale
        gqkv = mm_tn(normed_s[...], dproj[...]) * scale

        @pl.when(w == 0)
        def _():
            gout_ref[...] = gout
            gqkv_ref[...] = gqkv

        @pl.when(w == 1)
        def _():
            gout_ref[...] += gout
            gqkv_ref[...] += gqkv

        dnormed = mm_nt(dproj[...], wqkv_ref[...])
        total = cot_s[...] + norm_backward(dnormed, xhat_s[...], rstd_s[...], gain_ref[...])
        grad_ref[...] = total.reshape(7, 7, 8, C).astype(BF16)


def second_kernel(
    scale,
    y_own, y_row, y_tm, y_corner, c_own, c_row, c_tm, c_corner,
    gain_ref, bias_ref, wqkv_ref, wout_ref,
    own_ref, row_ref, tm_ref, corner_ref, gqkv_ref, gout_ref,
    x_s, rstd_s, normed_s, cot_s, q, qt, k, kt, v, vt, dot_s, mixt, dopt, dqt, dproj, pen, e_s, dk_s, dv_s,
):
    w, g = pl.program_id(0), pl.program_id(1)
    last_frames = lax.axis_index("tm") == lax.axis_size("tm") - 1
    last_rows = (lax.axis_index("rows") == lax.axis_size("rows") - 1) & (w == 1)

    def region_of(token, segment):
        columns = 4 if segment == 0 else 3
        late = jnp.where(last_frames & (token % 8 < 4), 1, 0)
        below = jnp.where(last_rows & (token // 8 // columns >= 4), 2, 0)
        return late + below

    @pl.when(g == 0)
    def _():
        def gather(into, own, row, tm, corner):
            def put(rho, count, low, high):
                whole = jnp.concatenate([low.astype(F32), high.astype(F32)[:, :, 4:8]], axis=2)
                into[32 * rho : 32 * (rho + count)] = whole[:, 3:7].reshape(-1, C)
                into[224 + 24 * rho : 224 + 24 * (rho + count)] = whole[:, 0:3].reshape(-1, C)

            @pl.when(w == 0)
            def _():
                put(0, 7, tm[0:7], own[3:10])

            @pl.when(w == 1)
            def _():
                put(0, 4, tm[7:11], own[10:14])
                put(4, 3, corner[...], row[...])

        gather(x_s, y_own, y_row, y_tm, y_corner)
        gather(cot_s, c_own, c_row, c_tm, c_corner)
        xhat, rstd = standardized(x_s[...])
        x_s[...] = xhat
        rstd_s[...] = rstd
        normed = (xhat * gain_ref[...] + bias_ref[...]).astype(BF16)
        normed_s[...] = normed
        queries = mm(normed, wqkv_ref[:, 0:C])
        q[...] = queries.astype(BF16)
        store_transposed(qt, (queries * QSCALE).astype(BF16), SPLIT)
        keys = mm(normed, wqkv_ref[:, C : 2 * C]).astype(BF16)
        k[...] = keys
        store_transposed(kt, keys, SPLIT)
        values = mm(normed, wqkv_ref[:, 2 * C :]).astype(BF16)
        v[...] = values
        store_values(vt, values, SPLIT)
        for s, (start, stop, lane) in enumerate(SPLIT):
            dot_s[:, lane : lane + stop - start] = mm_nt(
                wout_ref[...], cot_s[start:stop].astype(BF16)
            ).astype(BF16)
            shape = (stop - start, stop - start)
            key = region_of(lax.broadcasted_iota(jnp.int32, shape, 0), s)
            query = region_of(lax.broadcasted_iota(jnp.int32, shape, 1), s)
            pen[start:stop, 0 : stop - start] = jnp.where(key == query, 0.0, MASKED)

    base = pl.multiple_of(g * 128, 128)

    def head(j, s, general):
        start, stop, lane = SPLIT[s]
        count = stop - start
        keys = slice(0, TOK) if general else slice(start, stop)
        lanes = slice(lane, lane + count)
        qtg = qt[pl.ds(base, 128), lanes]
        scores = mm(k[keys, pl.ds(base, 128)], head_rows(j, qtg))
        if general:
            shape = (TOK, count)
            token = lax.broadcasted_iota(jnp.int32, shape, 0)
            key = jnp.where(token < 224, region_of(token, 0), region_of(token - 224, 1) + 4)
            query = region_of(lax.broadcasted_iota(jnp.int32, shape, 1), s) + 4 * s
            same = key == query
            scores = jnp.where(same, scores, MASKED)
            scores = scores - jnp.max(scores, axis=0, keepdims=True)
        else:
            scores = scores + pen[start:stop, 0:count]
        e = jnp.exp2(scores).astype(BF16)
        e_s[0 if general else start : TOK if general else stop, 0:count] = e
        vrows = pl.ds(pl.multiple_of(g * 4 * VROWS + j * VROWS, 16), VROWS)
        if general:
            mixed = mm(vt[vrows, 0:224], e[0:224]) + mm(vt[vrows, 256:424], e[224:392])
        else:
            mixed = mm(vt[vrows, lanes], e)
        sums = mixed[HD : HD + 1]
        inv = 1.0 / sums
        mixed = mixed[:HD] * inv
        rows = pl.ds(pl.multiple_of(base + j * HD, HD), HD)
        mixt[rows, lanes] = mixed.astype(BF16)
        do = dot_s[rows, lanes].astype(F32) * inv
        dsum = jnp.sum(mixed * do, axis=0, keepdims=True)
        do = do.astype(BF16)
        jrow = j * HD if isinstance(j, int) else pl.multiple_of(j * HD, HD)
        dopt[...] = jnp.zeros_like(dopt)
        dopt[pl.ds(jrow, HD), lanes] = do
        dop = dopt[:, lanes]
        dp = mm(v[keys, pl.ds(base, 128)], dop) - dsum
        ds = e.astype(F32) * dp
        if general:
            ds = jnp.where(same, ds, 0.0)
        ds = ds.astype(BF16)
        if general:
            dq = mm(kt[rows, 0:224], ds[0:224]) + mm(kt[rows, 256:424], ds[224:392])
        else:
            dq = mm(kt[rows, lanes], ds)
        dqt[pl.ds(jrow, HD), lanes] = (dq * HD ** (-0.5)).astype(BF16)
        dv_s[keys] += mm(e, dop.T)
        dk_s[keys] += mm(ds, head_lanes(j, q[start:stop, pl.ds(base, 128)]))
        return out_of_range(sums)

    dv_s[...] = jnp.zeros_like(dv_s)
    dk_s[...] = jnp.zeros_like(dk_s)
    bad = jnp.zeros((), F32)
    for s in range(2):
        for j in range(GROUP):
            bad = bad + jnp.max(head(j, s, False))

    @pl.when(bad > 0.0)
    def _():
        dv_s[...] = jnp.zeros_like(dv_s)
        dk_s[...] = jnp.zeros_like(dk_s)

        def step(j, carry):
            head(j, 0, True)
            head(j, 1, True)
            return carry

        lax.fori_loop(0, GROUP, step, 0)

    for start, stop, lane in SPLIT:
        dproj[start:stop, pl.ds(base, 128)] = dqt[:, lane : lane + stop - start].T
    dproj[:, pl.ds(pl.multiple_of(base + C, 128), 128)] = (dk_s[...] * HD ** (-0.5)).astype(BF16)
    dproj[:, pl.ds(pl.multiple_of(base + 2 * C, 128), 128)] = dv_s[...].astype(BF16)

    @pl.when(g == GROUP - 1)
    def _():
        gout = None
        for start, stop, lane in SPLIT:
            part = mm(mixt[:, lane : lane + stop - start], cot_s[start:stop].astype(BF16))
            gout = part if gout is None else gout + part
        gout = gout * scale
        gqkv = mm_tn(normed_s[...], dproj[...]) * scale

        @pl.when(w == 0)
        def _():
            gout_ref[...] = gout
            gqkv_ref[...] = gqkv

        @pl.when(w == 1)
        def _():
            gout_ref[...] += gout
            gqkv_ref[...] += gqkv

        dnormed = mm_nt(dproj[...], wqkv_ref[...])
        total = cot_s[...] + norm_backward(dnormed, x_s[...], rstd_s[...], gain_ref[...])
        first = total[0:224].reshape(7, 4, 8, C)
        second = total[224:392].reshape(7, 3, 8, C)
        whole = jnp.concatenate([second, first], axis=1)
        low = whole[:, :, 0:4].astype(BF16)
        whole = whole.astype(BF16)

        @pl.when(w == 0)
        def _():
            own_ref[0:3] = whole[0:3]
            own_ref[3:10] = whole
            tm_ref[0:7] = low

        @pl.when(w == 1)
        def _():
            own_ref[10:14] = whole[0:4]
            tm_ref[7:11] = low[0:4]
            row_ref[...] = whole[4:7]
            corner_ref[...] = low[4:7]


def whole_block(shape):
    zeros = (0,) * len(shape)
    return pl.BlockSpec(shape, lambda w, g: zeros)


def piece_shapes():
    return [(14, 7, 8, C), (3, 7, 8, C), (11, 7, 4, C), (3, 7, 4, C)]


WINDOW = pl.BlockSpec((7, 7, 8, C), lambda w, g: (w, 0, 0, 0))
WEIGHTS = [(1, C), (1, C), (C, 3 * C), (C, C)]
SAVED = [
    pl.BlockSpec((1, GROUP, TOK, TOK), lambda w, g: (w, g, 0, 0)),
    pl.BlockSpec((1, C, TOK), lambda w, g: (w, 0, 0)),
    pl.BlockSpec((1, 1, GROUP, TOK), lambda w, g: (w, g, 0, 0)),
]
SAVED_SHAPES = [
    jax.ShapeDtypeStruct((2, HEADS, TOK, TOK), BF16),
    jax.ShapeDtypeStruct((2, C, TOK), BF16),
    jax.ShapeDtypeStruct((2, HEADS // GROUP, GROUP, TOK), F32),
]


def params():
    return pltpu.CompilerParams(
        dimension_semantics=("arbitrary", "arbitrary"), vmem_limit_bytes=VMEM_LIMIT
    )


def forward_first(x, weights):
    pieces = piece_shapes()
    return pl.pallas_call(
        forward_kernel,
        grid=(2, GROUP),
        in_specs=[WINDOW] + [whole_block(s) for s in WEIGHTS],
        out_specs=SAVED + [WINDOW] + [whole_block(s) for s in pieces[1:]],
        out_shape=SAVED_SHAPES + [jax.ShapeDtypeStruct(s, BF16) for s in pieces],
        scratch_shapes=[
            pltpu.VMEM((C, TOK), BF16),
            pltpu.VMEM((TOK, C), BF16),
            pltpu.VMEM((HEADS * VROWS, TOK), BF16),
        ],
        compiler_params=params(),
        name="forward_first",
    )(x, *weights)


def backward_first(scale, x, weights, saved, pieces):
    return pl.pallas_call(
        functools.partial(backward_first_kernel, scale),
        grid=(2, GROUP),
        in_specs=[WINDOW]
        + [whole_block(s) for s in WEIGHTS]
        + SAVED
        + [whole_block(s) for s in piece_shapes()],
        out_specs=[WINDOW, whole_block((C, 3 * C)), whole_block((C, C))],
        out_shape=[
            jax.ShapeDtypeStruct((14, 7, 8, C), BF16),
            jax.ShapeDtypeStruct((C, 3 * C), F32),
            jax.ShapeDtypeStruct((C, C), F32),
        ],
        scratch_shapes=[
            pltpu.VMEM((TOK, C), F32),
            pltpu.VMEM((TOK, 1), F32),
            pltpu.VMEM((TOK, C), BF16),
            pltpu.VMEM((TOK, C), F32),
            pltpu.VMEM((TOK, C), BF16),
            pltpu.VMEM((C, TOK), BF16),
            pltpu.VMEM((TOK, C), BF16),
            pltpu.VMEM((C, TOK), BF16),
            pltpu.VMEM((128, TOK), BF16),
            pltpu.VMEM((128, TOK), BF16),
            pltpu.VMEM((TOK, 3 * C), BF16),
        ],
        compiler_params=params(),
        name="backward_first",
    )(x, *weights, *saved, *pieces)


def second_block(scale, y_pieces, c_pieces, weights):
    pieces = piece_shapes()
    return pl.pallas_call(
        functools.partial(second_kernel, scale),
        grid=(2, GROUP),
        in_specs=[whole_block(s) for s in pieces + pieces + WEIGHTS],
        out_specs=[whole_block(s) for s in pieces + [(C, 3 * C), (C, C)]],
        out_shape=[jax.ShapeDtypeStruct(s, BF16) for s in pieces]
        + [jax.ShapeDtypeStruct((C, 3 * C), F32), jax.ShapeDtypeStruct((C, C), F32)],
        scratch_shapes=[
            pltpu.VMEM((TOK, C), F32),
            pltpu.VMEM((TOK, 1), F32),
            pltpu.VMEM((TOK, C), BF16),
            pltpu.VMEM((TOK, C), F32),
            pltpu.VMEM((TOK, C), BF16),
            pltpu.VMEM((C, 512), BF16),
            pltpu.VMEM((TOK, C), BF16),
            pltpu.VMEM((C, 512), BF16),
            pltpu.VMEM((TOK, C), BF16),
            pltpu.VMEM((HEADS * VROWS, 512), BF16),
            pltpu.VMEM((C, 512), BF16),
            pltpu.VMEM((C, 512), BF16),
            pltpu.VMEM((128, 512), BF16),
            pltpu.VMEM((128, 512), BF16),
            pltpu.VMEM((TOK, 3 * C), BF16),
            pltpu.VMEM((TOK, 256), F32),
            pltpu.VMEM((TOK, 256), BF16),
            pltpu.VMEM((TOK, 128), F32),
            pltpu.VMEM((TOK, 128), F32),
        ],
        compiler_params=params(),
        name="second_block",
    )(*y_pieces, *c_pieces, *weights)


def moved(block, axes, steps):
    sizes = [lax.axis_size(a) for a in axes]
    total = math.prod(sizes)

    def place(index):
        out = []
        for size in reversed(sizes):
            out.append(index % size)
            index //= size
        return out[::-1]

    def number(places):
        index = 0
        for p, size in zip(places, sizes):
            index = index * size + p % size
        return index

    route = [
        (number([p + s for p, s in zip(place(i), steps)]), i) for i in range(total)
    ]
    return lax.ppermute(block, axes if len(axes) > 1 else axes[0], route)


def exchanged(row, tm, corner, step):
    return (
        moved(row, ("rows",), (step,)),
        moved(tm, ("tm",), (step,)),
        moved(corner, ("tm", "rows"), (step, step)),
    )


def per_device(
    video_clip, cotangent,
    gain_first, bias_first, qkv_first, out_first,
    gain_second, bias_second, qkv_second, out_second,
):
    frames, rows_here, columns, channels = video_clip.shape
    devices = lax.axis_size("tm") * lax.axis_size("rows")
    scale = 1.0 / math.sqrt(frames * rows_here * columns * devices)
    x = video_clip.transpose(1, 2, 0, 3)
    cot = cotangent.transpose(1, 2, 0, 3)
    first = (gain_first.reshape(1, C), bias_first.reshape(1, C), qkv_first, out_first)
    second = (gain_second.reshape(1, C), bias_second.reshape(1, C), qkv_second, out_second)
    c_pieces = (cot,) + exchanged(cot[0:3], cot[3:14, :, 0:4], cot[0:3, :, 0:4], 1)
    *saved, own, row, tm, corner = forward_first(x, first)
    y_pieces = (own,) + exchanged(row, tm, corner, 1)
    own, row, tm, corner, gqkv2, gout2 = second_block(scale, y_pieces, c_pieces, second)
    d_pieces = (own,) + exchanged(row, tm, corner, -1)
    grad, gqkv1, gout1 = backward_first(scale, x, first, saved, d_pieces)

    def scattered(block):
        return lax.psum_scatter(block, ("tm", "rows"), scatter_dimension=0, tiled=True)

    return (
        grad.transpose(2, 0, 1, 3),
        scattered(gqkv1), scattered(gout1), scattered(gqkv2), scattered(gout2),
    )


def solution(mesh):
    clip = P("tm", "rows", None, None)
    scattered = P(("tm", "rows"), None)
    return jax.shard_map(
        per_device,
        mesh=mesh,
        in_specs=(clip, clip) + (P(),) * 8,
        out_specs=(clip,) + (scattered,) * 4,
        check_vma=False,
    )
```

```python
import functools
import math

import jax
import jax.numpy as jnp
from jax import lax
from jax.experimental import pallas as pl
from jax.experimental.pallas import tpu as pltpu
from jax.sharding import PartitionSpec as P

F32, BF16 = jnp.float32, jnp.bfloat16
C, HEADS, HD = 512, 16, 32
TOK = 392
GROUP = 4
VROWS = 48
LOG2E = math.log2(math.e)
QSCALE = HD ** (-0.5) * LOG2E
MASKED = -1000000000.0 * LOG2E
LOW, HIGH = 2.0**-60, 2.0**100
WHOLE = ((0, 392, 0),)
SPLIT = ((0, 224, 0), (224, 392, 256))
VMEM_LIMIT = 56 * 1024 * 1024


def mm(a, b):
    return lax.dot_general(a, b, (((1,), (0,)), ((), ())), preferred_element_type=F32)


def mm_nt(a, b):
    return lax.dot_general(a, b, (((1,), (1,)), ((), ())), preferred_element_type=F32)


def mm_tn(a, b):
    return lax.dot_general(a, b, (((0,), (0,)), ((), ())), preferred_element_type=F32)


def standardized(values):
    center = values - jnp.mean(values, axis=-1, keepdims=True)
    rstd = lax.rsqrt(jnp.mean(center * center, axis=-1, keepdims=True) + 1e-05)
    return center * rstd, rstd


def tiles(block):
    return block.astype(F32).reshape(-1, C)


def head_rows(j, block):
    row = lax.broadcasted_iota(jnp.int32, block.shape, 0) // HD
    return jnp.where(row == j, block, jnp.zeros_like(block))


def head_lanes(j, block):
    lane = lax.broadcasted_iota(jnp.int32, block.shape, 1) // HD
    return jnp.where(lane == j, block, jnp.zeros_like(block))


def store_transposed(ref, block, segments, row0=0):
    for start, stop, lane in segments:
        ref[row0 : row0 + block.shape[1], lane : lane + stop - start] = block[start:stop].T


def store_values(vt, block, segments):
    for start, stop, lane in segments:
        turned = block[start:stop].T
        count = stop - start
        for head in range(HEADS):
            vt[VROWS * head : VROWS * head + HD, lane : lane + count] = turned[
                HD * head : HD * (head + 1)
            ]
            vt[VROWS * head + HD : VROWS * (head + 1), lane : lane + count] = jnp.ones(
                (VROWS - HD, count), BF16
            )


def out_of_range(sums):
    return jnp.where((sums > LOW) & (sums < HIGH), 0.0, 1.0)


def forward_kernel(
    x_ref, gain_ref, bias_ref, wqkv_ref, wout_ref,
    e_ref, mixt_ref, inv_ref, own_ref, row_ref, tm_ref, corner_ref,
    qt, k, vt,
):
    w, g = pl.program_id(0), pl.program_id(1)

    @pl.when(g == 0)
    def _():
        xhat, _ = standardized(tiles(x_ref[...]))
        normed = (xhat * gain_ref[...] + bias_ref[...]).astype(BF16)
        store_transposed(qt, (mm(normed, wqkv_ref[:, 0:C]) * QSCALE).astype(BF16), WHOLE)
        k[...] = mm(normed, wqkv_ref[:, C : 2 * C]).astype(BF16)
        store_values(vt, mm(normed, wqkv_ref[:, 2 * C :]).astype(BF16), WHOLE)

    base = pl.multiple_of(g * 128, 128)
    kg = k[:, pl.ds(base, 128)]
    qtg = qt[pl.ds(base, 128), :]

    def head(j, shifted):
        scores = mm(kg, head_rows(j, qtg))
        if shifted:
            scores = scores - jnp.max(scores, axis=0, keepdims=True)
        e = jnp.exp2(scores).astype(BF16)
        e_ref[0, j] = e
        mixed = mm(vt[pl.ds(pl.multiple_of(g * 4 * VROWS + j * VROWS, 16), VROWS), :], e)
        sums = mixed[HD : HD + 1]
        inv = 1.0 / sums
        inv_ref[0, 0, pl.ds(j, 1), :] = inv
        mixt_ref[0, pl.ds(pl.multiple_of(base + j * HD, HD), HD), :] = (mixed[:HD] * inv).astype(BF16)
        return out_of_range(sums)

    bad = head(0, False)
    for j in range(1, GROUP):
        bad = bad + head(j, False)

    @pl.when(jnp.max(bad) > 0.0)
    def _():
        def step(j, carry):
            head(j, True)
            return carry

        lax.fori_loop(0, GROUP, step, 0)

    @pl.when(g == GROUP - 1)
    def _():
        y = tiles(x_ref[...]) + mm_tn(mixt_ref[0], wout_ref[...])
        y = y.reshape(7, 7, 8, C).astype(BF16)
        low = y.astype(F32)[:, :, 0:4].astype(BF16)
        own_ref[...] = y

        @pl.when(w == 0)
        def _():
            row_ref[...] = y[0:3]
            corner_ref[...] = low[0:3]
            tm_ref[0:4] = low[3:7]

        @pl.when(w == 1)
        def _():
            tm_ref[4:11] = low


def write_parts(gqkv, gout, parts):
    def layer(z, carry):
        for xy in range(16):
            x, y = xy // 4, xy % 4
            rows = pl.ds(pl.multiple_of((z * 16 + x // 2 * 8 + y * 2 + x % 2) * 8, 8), 8)
            blocks = (
                gqkv[rows, 0:640],
                gqkv[rows, 640:1280],
                jnp.concatenate([gqkv[rows, 1280:1536], gout[rows, :]], axis=1),
            )
            for part, block, place in zip(parts, blocks, ((x, y, z), (y, z, x), (z, x, y))):
                part[(0,) + place] = block[0:4].astype(BF16)
                part[(1,) + place] = block[4:8].astype(BF16)
        return carry

    lax.fori_loop(0, 4, layer, 0)


def norm_backward(dnormed, xhat, rstd, gain):
    d = dnormed.astype(BF16).astype(F32) * gain
    return rstd * (
        d
        - jnp.mean(d, axis=-1, keepdims=True)
        - xhat * jnp.mean(d * xhat, axis=-1, keepdims=True)
    )


def backward_first_kernel(
    scale,
    x_ref, gain_ref, bias_ref, wqkv_ref, wout_ref, e_ref, mixt_ref, inv_ref,
    own_ref, row_ref, tm_ref, corner_ref,
    grad_ref, part0_ref, part1_ref, part2_ref,
    xhat_s, rstd_s, normed_s, cot_s, q, kt, v, dot_s, dopt, dqt, dproj, gqkv_s, gout_s,
):
    part_refs = (part0_ref, part1_ref, part2_ref)
    w, g = pl.program_id(0), pl.program_id(1)

    @pl.when(g == 0)
    def _():
        xhat, rstd = standardized(tiles(x_ref[...]))
        xhat_s[...] = xhat
        rstd_s[...] = rstd
        normed = (xhat * gain_ref[...] + bias_ref[...]).astype(BF16)
        normed_s[...] = normed
        q[...] = mm(normed, wqkv_ref[:, 0:C]).astype(BF16)
        store_transposed(kt, mm(normed, wqkv_ref[:, C : 2 * C]).astype(BF16), WHOLE)
        v[...] = mm(normed, wqkv_ref[:, 2 * C :]).astype(BF16)

        def put(row, count, low, high):
            whole = jnp.concatenate([low.astype(F32), high.astype(F32)[:, :, 4:8]], axis=2)
            cot_s[56 * row : 56 * (row + count)] = whole.reshape(-1, C)

        @pl.when(w == 0)
        def _():
            put(0, 3, corner_ref[...], row_ref[...])
            put(3, 4, tm_ref[0:4], own_ref[3:7])

        @pl.when(w == 1)
        def _():
            put(0, 7, tm_ref[4:11], own_ref[7:14])

        dot_s[...] = mm_nt(wout_ref[...], cot_s[...].astype(BF16)).astype(BF16)

    base = pl.multiple_of(g * 128, 128)
    vg = v[:, pl.ds(base, 128)]
    qg = q[:, pl.ds(base, 128)]
    ds_all = []
    for j in range(GROUP):
        rows = pl.ds(pl.multiple_of(base + HD * j, HD), HD)
        inv = inv_ref[0, 0, j : j + 1, :]
        do = dot_s[rows, :].astype(F32) * inv
        dsum = jnp.sum(mixt_ref[0, rows, :].astype(F32) * do, axis=0, keepdims=True)
        dopt[HD * j : HD * (j + 1), :] = do.astype(BF16)
        ds_all.append(dsum)
    dopg = dopt[...]
    dopn = dopg.T
    dv = dk = None
    for j in range(GROUP):
        e = e_ref[0, j]
        dp = mm(vg, head_rows(j, dopg)) - ds_all[j]
        ds = (e.astype(F32) * dp).astype(BF16)
        rows = pl.ds(pl.multiple_of(base + HD * j, HD), HD)
        dqt[HD * j : HD * (j + 1), :] = (mm(kt[rows, :], ds) * HD ** (-0.5)).astype(BF16)
        dv_j = mm(e, head_lanes(j, dopn))
        dk_j = mm(ds, head_lanes(j, qg))
        dv = dv_j if dv is None else dv + dv_j
        dk = dk_j if dk is None else dk + dk_j
    dproj[:, pl.ds(base, 128)] = dqt[...].T
    dproj[:, pl.ds(pl.multiple_of(base + C, 128), 128)] = (dk * HD ** (-0.5)).astype(BF16)
    dproj[:, pl.ds(pl.multiple_of(base + 2 * C, 128), 128)] = dv.astype(BF16)

    @pl.when(g == GROUP - 1)
    def _():
        gout = mm(mixt_ref[0], cot_s[...].astype(BF16)) * scale
        gqkv = mm_tn(normed_s[...], dproj[...]) * scale

        @pl.when(w == 0)
        def _():
            gout_s[...] = gout
            gqkv_s[...] = gqkv

        @pl.when(w == 1)
        def _():
            gout_s[...] += gout
            gqkv_s[...] += gqkv
            write_parts(gqkv_s, gout_s, part_refs)

        dnormed = mm_nt(dproj[...], wqkv_ref[...])
        total = cot_s[...] + norm_backward(dnormed, xhat_s[...], rstd_s[...], gain_ref[...])
        grad_ref[...] = total.reshape(7, 7, 8, C).astype(BF16)


def second_kernel(
    scale,
    y_own, y_row, y_tm, y_corner, c_own, c_row, c_tm, c_corner,
    gain_ref, bias_ref, wqkv_ref, wout_ref,
    own_ref, row_ref, tm_ref, corner_ref, part0_ref, part1_ref, part2_ref,
    x_s, rstd_s, normed_s, cot_s, q, qt, k, kt, v, vt, dot_s, mixt, dopt, dqt, dproj, pen, e_s, dk_s, dv_s,
    gqkv_s, gout_s,
):
    part_refs = (part0_ref, part1_ref, part2_ref)
    w, g = pl.program_id(0), pl.program_id(1)
    last_frames = lax.axis_index("tm") == lax.axis_size("tm") - 1
    last_rows = (lax.axis_index("rows") == lax.axis_size("rows") - 1) & (w == 1)

    def region_of(token, segment):
        columns = 4 if segment == 0 else 3
        late = jnp.where(last_frames & (token % 8 < 4), 1, 0)
        below = jnp.where(last_rows & (token // 8 // columns >= 4), 2, 0)
        return late + below

    @pl.when(g == 0)
    def _():
        def gather(into, own, row, tm, corner):
            def put(rho, count, low, high):
                whole = jnp.concatenate([low.astype(F32), high.astype(F32)[:, :, 4:8]], axis=2)
                into[32 * rho : 32 * (rho + count)] = whole[:, 3:7].reshape(-1, C)
                into[224 + 24 * rho : 224 + 24 * (rho + count)] = whole[:, 0:3].reshape(-1, C)

            @pl.when(w == 0)
            def _():
                put(0, 7, tm[0:7], own[3:10])

            @pl.when(w == 1)
            def _():
                put(0, 4, tm[7:11], own[10:14])
                put(4, 3, corner[...], row[...])

        gather(x_s, y_own, y_row, y_tm, y_corner)
        gather(cot_s, c_own, c_row, c_tm, c_corner)
        xhat, rstd = standardized(x_s[...])
        x_s[...] = xhat
        rstd_s[...] = rstd
        normed = (xhat * gain_ref[...] + bias_ref[...]).astype(BF16)
        normed_s[...] = normed
        queries = mm(normed, wqkv_ref[:, 0:C])
        q[...] = queries.astype(BF16)
        store_transposed(qt, (queries * QSCALE).astype(BF16), SPLIT)
        keys = mm(normed, wqkv_ref[:, C : 2 * C]).astype(BF16)
        k[...] = keys
        store_transposed(kt, keys, SPLIT)
        values = mm(normed, wqkv_ref[:, 2 * C :]).astype(BF16)
        v[...] = values
        store_values(vt, values, SPLIT)
        for s, (start, stop, lane) in enumerate(SPLIT):
            dot_s[:, lane : lane + stop - start] = mm_nt(
                wout_ref[...], cot_s[start:stop].astype(BF16)
            ).astype(BF16)
            shape = (stop - start, stop - start)
            key = region_of(lax.broadcasted_iota(jnp.int32, shape, 0), s)
            query = region_of(lax.broadcasted_iota(jnp.int32, shape, 1), s)
            pen[start:stop, 0 : stop - start] = jnp.where(key == query, 0.0, MASKED)

    base = pl.multiple_of(g * 128, 128)

    def head(j, s, general):
        start, stop, lane = SPLIT[s]
        count = stop - start
        keys = slice(0, TOK) if general else slice(start, stop)
        lanes = slice(lane, lane + count)
        qtg = qt[pl.ds(base, 128), lanes]
        scores = mm(k[keys, pl.ds(base, 128)], head_rows(j, qtg))
        if general:
            shape = (TOK, count)
            token = lax.broadcasted_iota(jnp.int32, shape, 0)
            key = jnp.where(token < 224, region_of(token, 0), region_of(token - 224, 1) + 4)
            query = region_of(lax.broadcasted_iota(jnp.int32, shape, 1), s) + 4 * s
            same = key == query
            scores = jnp.where(same, scores, MASKED)
            scores = scores - jnp.max(scores, axis=0, keepdims=True)
        else:
            scores = scores + pen[start:stop, 0:count]
        e = jnp.exp2(scores).astype(BF16)
        e_s[0 if general else start : TOK if general else stop, 0:count] = e
        vrows = pl.ds(pl.multiple_of(g * 4 * VROWS + j * VROWS, 16), VROWS)
        if general:
            mixed = mm(vt[vrows, 0:224], e[0:224]) + mm(vt[vrows, 256:424], e[224:392])
        else:
            mixed = mm(vt[vrows, lanes], e)
        sums = mixed[HD : HD + 1]
        inv = 1.0 / sums
        mixed = mixed[:HD] * inv
        rows = pl.ds(pl.multiple_of(base + j * HD, HD), HD)
        mixt[rows, lanes] = mixed.astype(BF16)
        do = dot_s[rows, lanes].astype(F32) * inv
        dsum = jnp.sum(mixed * do, axis=0, keepdims=True)
        do = do.astype(BF16)
        jrow = j * HD if isinstance(j, int) else pl.multiple_of(j * HD, HD)
        dopt[...] = jnp.zeros_like(dopt)
        dopt[pl.ds(jrow, HD), lanes] = do
        dop = dopt[:, lanes]
        dp = mm(v[keys, pl.ds(base, 128)], dop) - dsum
        ds = e.astype(F32) * dp
        if general:
            ds = jnp.where(same, ds, 0.0)
        ds = ds.astype(BF16)
        if general:
            dq = mm(kt[rows, 0:224], ds[0:224]) + mm(kt[rows, 256:424], ds[224:392])
        else:
            dq = mm(kt[rows, lanes], ds)
        dqt[pl.ds(jrow, HD), lanes] = (dq * HD ** (-0.5)).astype(BF16)
        dv_s[keys] += mm(e, dop.T)
        dk_s[keys] += mm(ds, head_lanes(j, q[start:stop, pl.ds(base, 128)]))
        return out_of_range(sums)

    dv_s[...] = jnp.zeros_like(dv_s)
    dk_s[...] = jnp.zeros_like(dk_s)
    bad = jnp.zeros((), F32)
    for s in range(2):
        for j in range(GROUP):
            bad = bad + jnp.max(head(j, s, False))

    @pl.when(bad > 0.0)
    def _():
        dv_s[...] = jnp.zeros_like(dv_s)
        dk_s[...] = jnp.zeros_like(dk_s)

        def step(j, carry):
            head(j, 0, True)
            head(j, 1, True)
            return carry

        lax.fori_loop(0, GROUP, step, 0)

    for start, stop, lane in SPLIT:
        dproj[start:stop, pl.ds(base, 128)] = dqt[:, lane : lane + stop - start].T
    dproj[:, pl.ds(pl.multiple_of(base + C, 128), 128)] = (dk_s[...] * HD ** (-0.5)).astype(BF16)
    dproj[:, pl.ds(pl.multiple_of(base + 2 * C, 128), 128)] = dv_s[...].astype(BF16)

    @pl.when(g == GROUP - 1)
    def _():
        gout = None
        for start, stop, lane in SPLIT:
            part = mm(mixt[:, lane : lane + stop - start], cot_s[start:stop].astype(BF16))
            gout = part if gout is None else gout + part
        gout = gout * scale
        gqkv = mm_tn(normed_s[...], dproj[...]) * scale

        @pl.when(w == 0)
        def _():
            gout_s[...] = gout
            gqkv_s[...] = gqkv

        @pl.when(w == 1)
        def _():
            gout_s[...] += gout
            gqkv_s[...] += gqkv
            write_parts(gqkv_s, gout_s, part_refs)

        dnormed = mm_nt(dproj[...], wqkv_ref[...])
        total = cot_s[...] + norm_backward(dnormed, x_s[...], rstd_s[...], gain_ref[...])
        first = total[0:224].reshape(7, 4, 8, C)
        second = total[224:392].reshape(7, 3, 8, C)
        whole = jnp.concatenate([second, first], axis=1)
        low = whole[:, :, 0:4].astype(BF16)
        whole = whole.astype(BF16)

        @pl.when(w == 0)
        def _():
            own_ref[0:3] = whole[0:3]
            own_ref[3:10] = whole
            tm_ref[0:7] = low

        @pl.when(w == 1)
        def _():
            own_ref[10:14] = whole[0:4]
            tm_ref[7:11] = low[0:4]
            row_ref[...] = whole[4:7]
            corner_ref[...] = low[4:7]


def whole_block(shape):
    zeros = (0,) * len(shape)
    return pl.BlockSpec(shape, lambda w, g: zeros)


def piece_shapes():
    return [(14, 7, 8, C), (3, 7, 8, C), (11, 7, 4, C), (3, 7, 4, C)]


WIDTHS = (640, 640, 768)
PARTS = [(2, 4, 4, 4, 4, width) for width in WIDTHS]
WINDOW = pl.BlockSpec((7, 7, 8, C), lambda w, g: (w, 0, 0, 0))
WEIGHTS = [(1, C), (1, C), (C, 3 * C), (C, C)]
SAVED = [
    pl.BlockSpec((1, GROUP, TOK, TOK), lambda w, g: (w, g, 0, 0)),
    pl.BlockSpec((1, C, TOK), lambda w, g: (w, 0, 0)),
    pl.BlockSpec((1, 1, GROUP, TOK), lambda w, g: (w, g, 0, 0)),
]
SAVED_SHAPES = [
    jax.ShapeDtypeStruct((2, HEADS, TOK, TOK), BF16),
    jax.ShapeDtypeStruct((2, C, TOK), BF16),
    jax.ShapeDtypeStruct((2, HEADS // GROUP, GROUP, TOK), F32),
]


def params():
    return pltpu.CompilerParams(
        dimension_semantics=("arbitrary", "arbitrary"), vmem_limit_bytes=VMEM_LIMIT
    )


def forward_first(x, weights):
    pieces = piece_shapes()
    return pl.pallas_call(
        forward_kernel,
        grid=(2, GROUP),
        in_specs=[WINDOW] + [whole_block(s) for s in WEIGHTS],
        out_specs=SAVED + [WINDOW] + [whole_block(s) for s in pieces[1:]],
        out_shape=SAVED_SHAPES + [jax.ShapeDtypeStruct(s, BF16) for s in pieces],
        scratch_shapes=[
            pltpu.VMEM((C, TOK), BF16),
            pltpu.VMEM((TOK, C), BF16),
            pltpu.VMEM((HEADS * VROWS, TOK), BF16),
        ],
        compiler_params=params(),
        name="forward_first",
    )(x, *weights)


def backward_first(scale, x, weights, saved, pieces):
    return pl.pallas_call(
        functools.partial(backward_first_kernel, scale),
        grid=(2, GROUP),
        in_specs=[WINDOW]
        + [whole_block(s) for s in WEIGHTS]
        + SAVED
        + [whole_block(s) for s in piece_shapes()],
        out_specs=[WINDOW] + [whole_block(s) for s in PARTS],
        out_shape=[jax.ShapeDtypeStruct(s, BF16) for s in [(14, 7, 8, C)] + PARTS],
        scratch_shapes=[
            pltpu.VMEM((TOK, C), F32),
            pltpu.VMEM((TOK, 1), F32),
            pltpu.VMEM((TOK, C), BF16),
            pltpu.VMEM((TOK, C), F32),
            pltpu.VMEM((TOK, C), BF16),
            pltpu.VMEM((C, TOK), BF16),
            pltpu.VMEM((TOK, C), BF16),
            pltpu.VMEM((C, TOK), BF16),
            pltpu.VMEM((128, TOK), BF16),
            pltpu.VMEM((128, TOK), BF16),
            pltpu.VMEM((TOK, 3 * C), BF16),
            pltpu.VMEM((C, 3 * C), F32),
            pltpu.VMEM((C, C), F32),
        ],
        compiler_params=params(),
        name="backward_first",
    )(x, *weights, *saved, *pieces)


def second_block(scale, y_pieces, c_pieces, weights):
    pieces = piece_shapes()
    return pl.pallas_call(
        functools.partial(second_kernel, scale),
        grid=(2, GROUP),
        in_specs=[whole_block(s) for s in pieces + pieces + WEIGHTS],
        out_specs=[whole_block(s) for s in pieces + PARTS],
        out_shape=[jax.ShapeDtypeStruct(s, BF16) for s in pieces + PARTS],
        scratch_shapes=[
            pltpu.VMEM((TOK, C), F32),
            pltpu.VMEM((TOK, 1), F32),
            pltpu.VMEM((TOK, C), BF16),
            pltpu.VMEM((TOK, C), F32),
            pltpu.VMEM((TOK, C), BF16),
            pltpu.VMEM((C, 512), BF16),
            pltpu.VMEM((TOK, C), BF16),
            pltpu.VMEM((C, 512), BF16),
            pltpu.VMEM((TOK, C), BF16),
            pltpu.VMEM((HEADS * VROWS, 512), BF16),
            pltpu.VMEM((C, 512), BF16),
            pltpu.VMEM((C, 512), BF16),
            pltpu.VMEM((128, 512), BF16),
            pltpu.VMEM((128, 512), BF16),
            pltpu.VMEM((TOK, 3 * C), BF16),
            pltpu.VMEM((TOK, 256), F32),
            pltpu.VMEM((TOK, 256), BF16),
            pltpu.VMEM((TOK, 128), F32),
            pltpu.VMEM((TOK, 128), F32),
            pltpu.VMEM((C, 3 * C), F32),
            pltpu.VMEM((C, C), F32),
        ],
        compiler_params=params(),
        name="second_block",
    )(*y_pieces, *c_pieces, *weights)


def coordinates():
    tm, rows = lax.axis_index("tm"), lax.axis_index("rows")
    return {
        "x": tm // 4 % 2 * 2 + rows // 2,
        "y": tm % 4,
        "z": tm // 8,
        "core": rows % 2,
    }


def device_at(place):
    tm = place["z"] * 8 + place["x"] // 2 * 4 + place["y"]
    return (tm, place["x"] % 2 * 2 + place["core"])


def beside(here, axis, steps):
    return device_at({**here, axis: (here[axis] + steps) % (2 if axis == "core" else 4)})


ORDERS = ("xyz", "yzx", "zxy")
MESH = pl.DeviceIdType.MESH


def reduce_kernel(jobs, *refs):
    parts, outs = refs[:jobs], refs[jobs : 2 * jobs]
    scratch = refs[2 * jobs : 7 * jobs]
    held = [scratch[5 * i : 5 * i + 2] for i in range(jobs)]
    slots = [scratch[5 * i + 2 : 5 * i + 5] for i in range(jobs)]
    send_sem, recv_sem, local_sem = refs[7 * jobs :]
    here = coordinates()
    partners = [beside(here, "core", 1)] + [
        beside(here, axis, steps) for axis in "xyz" for steps in (1, 2, 3)
    ]
    barrier = pltpu.get_barrier_semaphore()
    for partner in partners:
        pl.semaphore_signal(barrier, inc=1, device_id=partner, device_id_type=MESH)

    local = []
    for i in range(jobs):
        copy = pltpu.make_async_copy(parts[i].at[here["core"]], held[i][0], local_sem.at[i])
        copy.start()
        local.append(copy)
    pl.semaphore_wait(barrier, len(partners))

    flying = []
    for i in range(jobs):
        copy = pltpu.make_async_remote_copy(
            src_ref=parts[i].at[1 - here["core"]],
            dst_ref=held[i][1],
            send_sem=send_sem.at[i, 0],
            recv_sem=recv_sem.at[i, 0],
            device_id=partners[0],
            device_id_type=MESH,
        )
        copy.start()
        flying.append([copy])

    sent = list(flying)
    sums = [None] * jobs
    for stage in range(4):
        for i in range(jobs):
            order = ORDERS[i % 3]
            for copy in flying[i]:
                copy.wait_recv()
            if stage == 0:
                local[i].wait()
                for a in range(4):
                    total = held[i][0][a].astype(F32) + held[i][1][a].astype(F32)
                    held[i][0][a] = total.astype(BF16)
                source = held[i][0]
            else:
                total = sums[i]
                for slot in range(3):
                    total = total + slots[i][stage - 1][slot].astype(F32)
                if stage == 3:
                    outs[i][...] = total
                    continue
                source = slots[i][stage - 1].at[3]
                source[...] = total.astype(BF16)
            axis = order[stage]
            copies = []
            for steps in (1, 2, 3):
                copy = pltpu.make_async_remote_copy(
                    src_ref=source.at[(here[axis] + steps) % 4],
                    dst_ref=slots[i][stage].at[steps - 1],
                    send_sem=send_sem.at[i, 3 * stage + steps],
                    recv_sem=recv_sem.at[i, 3 * stage + steps],
                    device_id=beside(here, axis, steps),
                    device_id_type=MESH,
                )
                copy.start()
                copies.append(copy)
            sums[i] = source[here[axis]].astype(F32)
            flying[i] = copies
            sent.append(copies)
    for copies in sent:
        for copy in copies:
            copy.wait_send()


def reduced(parts):
    jobs = len(parts)
    scratch = []
    for part in parts:
        width = part.shape[-1]
        scratch += [
            pltpu.VMEM((4, 4, 4, 4, width), BF16),
            pltpu.VMEM((4, 4, 4, 4, width), BF16),
            pltpu.VMEM((4, 4, 4, 4, width), BF16),
            pltpu.VMEM((4, 4, 4, width), BF16),
            pltpu.VMEM((4, 4, width), BF16),
        ]
    return pl.pallas_call(
        functools.partial(reduce_kernel, jobs),
        in_specs=[pl.BlockSpec(memory_space=pl.ANY)] * jobs,
        out_specs=[pl.BlockSpec(memory_space=pltpu.VMEM)] * jobs,
        out_shape=[jax.ShapeDtypeStruct((4, part.shape[-1]), F32) for part in parts],
        scratch_shapes=scratch
        + [
            pltpu.SemaphoreType.DMA((jobs, 10)),
            pltpu.SemaphoreType.DMA((jobs, 10)),
            pltpu.SemaphoreType.DMA((jobs,)),
        ],
        compiler_params=pltpu.CompilerParams(
            collective_id=0, has_side_effects=True, vmem_limit_bytes=VMEM_LIMIT
        ),
        name="reduce_gradients",
    )(*parts)


def moved(block, axes, steps):
    sizes = [lax.axis_size(a) for a in axes]
    total = math.prod(sizes)

    def place(index):
        out = []
        for size in reversed(sizes):
            out.append(index % size)
            index //= size
        return out[::-1]

    def number(places):
        index = 0
        for p, size in zip(places, sizes):
            index = index * size + p % size
        return index

    route = [
        (number([p + s for p, s in zip(place(i), steps)]), i) for i in range(total)
    ]
    return lax.ppermute(block, axes if len(axes) > 1 else axes[0], route)


def exchanged(row, tm, corner, step):
    return (
        moved(row, ("rows",), (step,)),
        moved(tm, ("tm",), (step,)),
        moved(corner, ("tm", "rows"), (step, step)),
    )


def per_device(
    video_clip, cotangent,
    gain_first, bias_first, qkv_first, out_first,
    gain_second, bias_second, qkv_second, out_second,
):
    frames, rows_here, columns, channels = video_clip.shape
    devices = lax.axis_size("tm") * lax.axis_size("rows")
    scale = 1.0 / math.sqrt(frames * rows_here * columns * devices)
    x = video_clip.transpose(1, 2, 0, 3)
    cot = cotangent.transpose(1, 2, 0, 3)
    first = (gain_first.reshape(1, C), bias_first.reshape(1, C), qkv_first, out_first)
    second = (gain_second.reshape(1, C), bias_second.reshape(1, C), qkv_second, out_second)
    c_pieces = (cot,) + exchanged(cot[0:3], cot[3:14, :, 0:4], cot[0:3, :, 0:4], 1)
    *saved, own, row, tm, corner = forward_first(x, first)
    y_pieces = (own,) + exchanged(row, tm, corner, 1)
    own, row, tm, corner, *parts2 = second_block(scale, y_pieces, c_pieces, second)
    d_pieces = (own,) + exchanged(row, tm, corner, -1)
    grad, *parts1 = backward_first(scale, x, first, saved, d_pieces)
    sums = reduced(parts1 + parts2)

    def matrices(sums):
        gqkv = jnp.concatenate([sums[0], sums[1], sums[2][:, :256]], axis=1)
        return gqkv, sums[2][:, 256:]

    return (grad.transpose(2, 0, 1, 3), *matrices(sums[:3]), *matrices(sums[3:]))


def solution(mesh):
    clip = P("tm", "rows", None, None)
    scattered = P(("tm", "rows"), None)
    return jax.shard_map(
        per_device,
        mesh=mesh,
        in_specs=(clip, clip) + (P(),) * 8,
        out_specs=(clip,) + (scattered,) * 4,
        check_vma=False,
    )
```

```python
import functools
import math

import jax
import jax.numpy as jnp
from jax import lax
from jax.experimental import pallas as pl
from jax.experimental.pallas import tpu as pltpu
from jax.sharding import PartitionSpec as P

F32, BF16 = jnp.float32, jnp.bfloat16
C, HEADS, HD = 512, 16, 32
TOK = 392
GROUP = 4
VROWS = 48
LOG2E = math.log2(math.e)
QSCALE = HD ** (-0.5) * LOG2E
MASKED = -1000000000.0 * LOG2E
LOW, HIGH = 2.0**-60, 2.0**100
WHOLE = ((0, 392, 0),)
SPLIT = ((0, 224, 0), (224, 392, 256))
VMEM_LIMIT = 56 * 1024 * 1024


def mm(a, b):
    return lax.dot_general(a, b, (((1,), (0,)), ((), ())), preferred_element_type=F32)


def mm_nt(a, b):
    return lax.dot_general(a, b, (((1,), (1,)), ((), ())), preferred_element_type=F32)


def mm_tn(a, b):
    return lax.dot_general(a, b, (((0,), (0,)), ((), ())), preferred_element_type=F32)


def standardized(values):
    center = values - jnp.mean(values, axis=-1, keepdims=True)
    rstd = lax.rsqrt(jnp.mean(center * center, axis=-1, keepdims=True) + 1e-05)
    return center * rstd, rstd


def tiles(block):
    return block.astype(F32).reshape(-1, C)


def head_rows(j, block):
    row = lax.broadcasted_iota(jnp.int32, block.shape, 0) // HD
    return jnp.where(row == j, block, jnp.zeros_like(block))


def head_lanes(j, block):
    lane = lax.broadcasted_iota(jnp.int32, block.shape, 1) // HD
    return jnp.where(lane == j, block, jnp.zeros_like(block))


def store_transposed(ref, block, segments, row0=0):
    for start, stop, lane in segments:
        ref[row0 : row0 + block.shape[1], lane : lane + stop - start] = block[start:stop].T


def store_values(vt, block, segments):
    for start, stop, lane in segments:
        turned = block[start:stop].T
        count = stop - start
        for head in range(HEADS):
            vt[VROWS * head : VROWS * head + HD, lane : lane + count] = turned[
                HD * head : HD * (head + 1)
            ]
            vt[VROWS * head + HD : VROWS * (head + 1), lane : lane + count] = jnp.ones(
                (VROWS - HD, count), BF16
            )


def out_of_range(sums):
    return jnp.where((sums > LOW) & (sums < HIGH), 0.0, 1.0)


def forward_kernel(
    x_ref, cot_ref, gain_ref, bias_ref, wqkv_ref, wout_ref,
    e_ref, mixt_ref, inv_ref, *refs,
):
    y_pieces, c_pieces, (qt, k, vt) = refs[0:5], refs[5:10], refs[10:]
    w, g = pl.program_id(0), pl.program_id(1)

    @pl.when(g == 0)
    def _():
        xhat, _ = standardized(tiles(x_ref[...]))
        normed = (xhat * gain_ref[...] + bias_ref[...]).astype(BF16)
        store_transposed(qt, (mm(normed, wqkv_ref[:, 0:C]) * QSCALE).astype(BF16), WHOLE)
        k[...] = mm(normed, wqkv_ref[:, C : 2 * C]).astype(BF16)
        store_values(vt, mm(normed, wqkv_ref[:, 2 * C :]).astype(BF16), WHOLE)

    base = pl.multiple_of(g * 128, 128)
    kg = k[:, pl.ds(base, 128)]
    qtg = qt[pl.ds(base, 128), :]

    def head(j, shifted):
        scores = mm(kg, head_rows(j, qtg))
        if shifted:
            scores = scores - jnp.max(scores, axis=0, keepdims=True)
        e = jnp.exp2(scores).astype(BF16)
        e_ref[0, j] = e
        mixed = mm(vt[pl.ds(pl.multiple_of(g * 4 * VROWS + j * VROWS, 16), VROWS), :], e)
        sums = mixed[HD : HD + 1]
        inv = 1.0 / sums
        inv_ref[0, 0, pl.ds(j, 1), :] = inv
        mixt_ref[0, pl.ds(pl.multiple_of(base + j * HD, HD), HD), :] = (mixed[:HD] * inv).astype(BF16)
        return out_of_range(sums)

    bad = head(0, False)
    for j in range(1, GROUP):
        bad = bad + head(j, False)

    @pl.when(jnp.max(bad) > 0.0)
    def _():
        def step(j, carry):
            head(j, True)
            return carry

        lax.fori_loop(0, GROUP, step, 0)

    @pl.when(g == GROUP - 1)
    def _():
        y = tiles(x_ref[...]) + mm_tn(mixt_ref[0], wout_ref[...])
        for whole, pieces in (
            (y.reshape(7, 7, 8, C), y_pieces),
            (cot_ref[...].astype(F32), c_pieces),
        ):
            own, ahead, behind, above, corner = pieces

            @pl.when(w == 0)
            def _():
                above[...] = whole[0:3, :, 0:4].astype(BF16)
                corner[...] = whole[0:3, :, 4:8].astype(BF16)
                ahead[0:4] = whole[3:7, :, 0:4].astype(BF16)
                own[0:4] = whole[3:7, :, 4:8].astype(BF16)

            @pl.when(w == 1)
            def _():
                ahead[4:7] = whole[0:3, :, 0:4].astype(BF16)
                own[4:7] = whole[0:3, :, 4:8].astype(BF16)
                behind[...] = whole[3:7, :, 4:8].astype(BF16)
                own[7:11] = whole[3:7, :, 0:4].astype(BF16)


def write_parts(gqkv, gout, parts):
    def layer(z, carry):
        for xy in range(16):
            x, y = xy // 4, xy % 4
            rows = pl.ds(pl.multiple_of((z * 16 + x // 2 * 8 + y * 2 + x % 2) * 8, 8), 8)
            blocks = (
                gqkv[rows, 0:640],
                gqkv[rows, 640:1280],
                jnp.concatenate([gqkv[rows, 1280:1536], gout[rows, :]], axis=1),
            )
            for part, block, place in zip(parts, blocks, ((x, y, z), (y, z, x), (z, x, y))):
                part[(0,) + place] = block[0:4].astype(BF16)
                part[(1,) + place] = block[4:8].astype(BF16)
        return carry

    lax.fori_loop(0, 4, layer, 0)


def norm_backward(dnormed, xhat, rstd, gain):
    d = dnormed.astype(BF16).astype(F32) * gain
    return rstd * (
        d
        - jnp.mean(d, axis=-1, keepdims=True)
        - xhat * jnp.mean(d * xhat, axis=-1, keepdims=True)
    )


def backward_first_kernel(
    scale,
    x_ref, gain_ref, bias_ref, wqkv_ref, wout_ref, e_ref, mixt_ref, inv_ref,
    own, ahead, behind, above, corner,
    grad_ref, part0_ref, part1_ref, part2_ref,
    xhat_s, rstd_s, normed_s, cot_s, q, kt, v, dot_s, dopt, dqt, dproj, gqkv_s, gout_s,
):
    part_refs = (part0_ref, part1_ref, part2_ref)
    w, g = pl.program_id(0), pl.program_id(1)

    @pl.when(g == 0)
    def _():
        xhat, rstd = standardized(tiles(x_ref[...]))
        xhat_s[...] = xhat
        rstd_s[...] = rstd
        normed = (xhat * gain_ref[...] + bias_ref[...]).astype(BF16)
        normed_s[...] = normed
        q[...] = mm(normed, wqkv_ref[:, 0:C]).astype(BF16)
        store_transposed(kt, mm(normed, wqkv_ref[:, C : 2 * C]).astype(BF16), WHOLE)
        v[...] = mm(normed, wqkv_ref[:, 2 * C :]).astype(BF16)

        def put(row, count, low, high):
            whole = jnp.concatenate([low.astype(F32), high.astype(F32)], axis=2)
            cot_s[56 * row : 56 * (row + count)] = whole.reshape(-1, C)

        @pl.when(w == 0)
        def _():
            put(0, 3, above[...], corner[...])
            put(3, 4, ahead[0:4], own[0:4])

        @pl.when(w == 1)
        def _():
            put(0, 3, ahead[4:7], own[4:7])
            put(3, 4, own[7:11], behind[...])

        dot_s[...] = mm_nt(wout_ref[...], cot_s[...].astype(BF16)).astype(BF16)

    base = pl.multiple_of(g * 128, 128)
    vg = v[:, pl.ds(base, 128)]
    qg = q[:, pl.ds(base, 128)]
    ds_all = []
    for j in range(GROUP):
        rows = pl.ds(pl.multiple_of(base + HD * j, HD), HD)
        inv = inv_ref[0, 0, j : j + 1, :]
        do = dot_s[rows, :].astype(F32) * inv
        dsum = jnp.sum(mixt_ref[0, rows, :].astype(F32) * do, axis=0, keepdims=True)
        dopt[HD * j : HD * (j + 1), :] = do.astype(BF16)
        ds_all.append(dsum)
    dopg = dopt[...]
    dopn = dopg.T
    dv = dk = None
    for j in range(GROUP):
        e = e_ref[0, j]
        dp = mm(vg, head_rows(j, dopg)) - ds_all[j]
        ds = (e.astype(F32) * dp).astype(BF16)
        rows = pl.ds(pl.multiple_of(base + HD * j, HD), HD)
        dqt[HD * j : HD * (j + 1), :] = (mm(kt[rows, :], ds) * HD ** (-0.5)).astype(BF16)
        dv_j = mm(e, head_lanes(j, dopn))
        dk_j = mm(ds, head_lanes(j, qg))
        dv = dv_j if dv is None else dv + dv_j
        dk = dk_j if dk is None else dk + dk_j
    dproj[:, pl.ds(base, 128)] = dqt[...].T
    dproj[:, pl.ds(pl.multiple_of(base + C, 128), 128)] = (dk * HD ** (-0.5)).astype(BF16)
    dproj[:, pl.ds(pl.multiple_of(base + 2 * C, 128), 128)] = dv.astype(BF16)

    @pl.when(g == GROUP - 1)
    def _():
        gout = mm(mixt_ref[0], cot_s[...].astype(BF16)) * scale
        gqkv = mm_tn(normed_s[...], dproj[...]) * scale

        @pl.when(w == 0)
        def _():
            gout_s[...] = gout
            gqkv_s[...] = gqkv

        @pl.when(w == 1)
        def _():
            gout_s[...] += gout
            gqkv_s[...] += gqkv
            write_parts(gqkv_s, gout_s, part_refs)

        dnormed = mm_nt(dproj[...], wqkv_ref[...])
        total = cot_s[...] + norm_backward(dnormed, xhat_s[...], rstd_s[...], gain_ref[...])
        grad_ref[...] = total.reshape(7, 7, 8, C).astype(BF16)


def second_kernel(
    scale,
    y_own, y_ahead, y_behind, y_above, y_corner, c_own, c_ahead, c_behind, c_above, c_corner,
    gain_ref, bias_ref, wqkv_ref, wout_ref,
    own, ahead, behind, above, corner, part0_ref, part1_ref, part2_ref,
    x_s, rstd_s, normed_s, cot_s, q, qt, k, kt, v, vt, dot_s, mixt, dopt, dqt, dproj, pen, e_s, dk_s, dv_s,
    gqkv_s, gout_s,
):
    part_refs = (part0_ref, part1_ref, part2_ref)
    w, g = pl.program_id(0), pl.program_id(1)
    last_frames = lax.axis_index("tm") == jnp.where(w == 0, lax.axis_size("tm") - 1, 0)
    last_rows = (lax.axis_index("rows") == lax.axis_size("rows") - 1) & (w == 1)

    def region_of(token, segment):
        columns = 4 if segment == 0 else 3
        late = jnp.where(last_frames & (token % 8 < 4), 1, 0)
        below = jnp.where(last_rows & (token // 8 // columns >= 4), 2, 0)
        return late + below

    @pl.when(g == 0)
    def _():
        def gather(into, own, ahead, behind, above, corner):
            def put(rho, count, low, high):
                whole = jnp.concatenate([low.astype(F32), high.astype(F32)], axis=2)
                into[32 * rho : 32 * (rho + count)] = whole[:, 3:7].reshape(-1, C)
                into[224 + 24 * rho : 224 + 24 * (rho + count)] = whole[:, 0:3].reshape(-1, C)

            @pl.when(w == 0)
            def _():
                put(0, 7, ahead[...], own[0:7])

            @pl.when(w == 1)
            def _():
                put(0, 4, own[7:11], behind[...])
                put(4, 3, above[...], corner[...])

        gather(x_s, y_own, y_ahead, y_behind, y_above, y_corner)
        gather(cot_s, c_own, c_ahead, c_behind, c_above, c_corner)
        xhat, rstd = standardized(x_s[...])
        x_s[...] = xhat
        rstd_s[...] = rstd
        normed = (xhat * gain_ref[...] + bias_ref[...]).astype(BF16)
        normed_s[...] = normed
        queries = mm(normed, wqkv_ref[:, 0:C])
        q[...] = queries.astype(BF16)
        store_transposed(qt, (queries * QSCALE).astype(BF16), SPLIT)
        keys = mm(normed, wqkv_ref[:, C : 2 * C]).astype(BF16)
        k[...] = keys
        store_transposed(kt, keys, SPLIT)
        values = mm(normed, wqkv_ref[:, 2 * C :]).astype(BF16)
        v[...] = values
        store_values(vt, values, SPLIT)
        for s, (start, stop, lane) in enumerate(SPLIT):
            dot_s[:, lane : lane + stop - start] = mm_nt(
                wout_ref[...], cot_s[start:stop].astype(BF16)
            ).astype(BF16)
            shape = (stop - start, stop - start)
            key = region_of(lax.broadcasted_iota(jnp.int32, shape, 0), s)
            query = region_of(lax.broadcasted_iota(jnp.int32, shape, 1), s)
            pen[start:stop, 0 : stop - start] = jnp.where(key == query, 0.0, MASKED)

    base = pl.multiple_of(g * 128, 128)

    def head(j, s, general):
        start, stop, lane = SPLIT[s]
        count = stop - start
        keys = slice(0, TOK) if general else slice(start, stop)
        lanes = slice(lane, lane + count)
        qtg = qt[pl.ds(base, 128), lanes]
        scores = mm(k[keys, pl.ds(base, 128)], head_rows(j, qtg))
        if general:
            shape = (TOK, count)
            token = lax.broadcasted_iota(jnp.int32, shape, 0)
            key = jnp.where(token < 224, region_of(token, 0), region_of(token - 224, 1) + 4)
            query = region_of(lax.broadcasted_iota(jnp.int32, shape, 1), s) + 4 * s
            same = key == query
            scores = jnp.where(same, scores, MASKED)
            scores = scores - jnp.max(scores, axis=0, keepdims=True)
        else:
            scores = scores + pen[start:stop, 0:count]
        e = jnp.exp2(scores).astype(BF16)
        e_s[0 if general else start : TOK if general else stop, 0:count] = e
        vrows = pl.ds(pl.multiple_of(g * 4 * VROWS + j * VROWS, 16), VROWS)
        if general:
            mixed = mm(vt[vrows, 0:224], e[0:224]) + mm(vt[vrows, 256:424], e[224:392])
        else:
            mixed = mm(vt[vrows, lanes], e)
        sums = mixed[HD : HD + 1]
        inv = 1.0 / sums
        mixed = mixed[:HD] * inv
        rows = pl.ds(pl.multiple_of(base + j * HD, HD), HD)
        mixt[rows, lanes] = mixed.astype(BF16)
        do = dot_s[rows, lanes].astype(F32) * inv
        dsum = jnp.sum(mixed * do, axis=0, keepdims=True)
        do = do.astype(BF16)
        jrow = j * HD if isinstance(j, int) else pl.multiple_of(j * HD, HD)
        dopt[...] = jnp.zeros_like(dopt)
        dopt[pl.ds(jrow, HD), lanes] = do
        dop = dopt[:, lanes]
        dp = mm(v[keys, pl.ds(base, 128)], dop) - dsum
        ds = e.astype(F32) * dp
        if general:
            ds = jnp.where(same, ds, 0.0)
        ds = ds.astype(BF16)
        if general:
            dq = mm(kt[rows, 0:224], ds[0:224]) + mm(kt[rows, 256:424], ds[224:392])
        else:
            dq = mm(kt[rows, lanes], ds)
        dqt[pl.ds(jrow, HD), lanes] = (dq * HD ** (-0.5)).astype(BF16)
        dv_s[keys] += mm(e, dop.T)
        dk_s[keys] += mm(ds, head_lanes(j, q[start:stop, pl.ds(base, 128)]))
        return out_of_range(sums)

    dv_s[...] = jnp.zeros_like(dv_s)
    dk_s[...] = jnp.zeros_like(dk_s)
    bad = jnp.zeros((), F32)
    for s in range(2):
        for j in range(GROUP):
            bad = bad + jnp.max(head(j, s, False))

    @pl.when(bad > 0.0)
    def _():
        dv_s[...] = jnp.zeros_like(dv_s)
        dk_s[...] = jnp.zeros_like(dk_s)

        def step(j, carry):
            head(j, 0, True)
            head(j, 1, True)
            return carry

        lax.fori_loop(0, GROUP, step, 0)

    for start, stop, lane in SPLIT:
        dproj[start:stop, pl.ds(base, 128)] = dqt[:, lane : lane + stop - start].T
    dproj[:, pl.ds(pl.multiple_of(base + C, 128), 128)] = (dk_s[...] * HD ** (-0.5)).astype(BF16)
    dproj[:, pl.ds(pl.multiple_of(base + 2 * C, 128), 128)] = dv_s[...].astype(BF16)

    @pl.when(g == GROUP - 1)
    def _():
        gout = None
        for start, stop, lane in SPLIT:
            part = mm(mixt[:, lane : lane + stop - start], cot_s[start:stop].astype(BF16))
            gout = part if gout is None else gout + part
        gout = gout * scale
        gqkv = mm_tn(normed_s[...], dproj[...]) * scale

        @pl.when(w == 0)
        def _():
            gout_s[...] = gout
            gqkv_s[...] = gqkv

        @pl.when(w == 1)
        def _():
            gout_s[...] += gout
            gqkv_s[...] += gqkv
            write_parts(gqkv_s, gout_s, part_refs)

        dnormed = mm_nt(dproj[...], wqkv_ref[...])
        total = cot_s[...] + norm_backward(dnormed, x_s[...], rstd_s[...], gain_ref[...])
        first = total[0:224].reshape(7, 4, 8, C)
        second = total[224:392].reshape(7, 3, 8, C)
        whole = jnp.concatenate([second, first], axis=1)
        low = whole[:, :, 0:4].astype(BF16)
        high = whole[:, :, 4:8].astype(BF16)

        @pl.when(w == 0)
        def _():
            ahead[...] = low
            own[0:7] = high

        @pl.when(w == 1)
        def _():
            own[7:11] = low[0:4]
            behind[...] = high[0:4]
            above[...] = low[4:7]
            corner[...] = high[4:7]


def whole_block(shape):
    zeros = (0,) * len(shape)
    return pl.BlockSpec(shape, lambda w, g: zeros)


def piece_shapes():
    return [(rows, 7, 4, C) for rows in (11, 7, 4, 3, 3)]


WIDTHS = (640, 640, 768)
PARTS = [(2, 4, 4, 4, 4, width) for width in WIDTHS]
WINDOW = pl.BlockSpec((7, 7, 8, C), lambda w, g: (w, 0, 0, 0))
WEIGHTS = [(1, C), (1, C), (C, 3 * C), (C, C)]
SAVED = [
    pl.BlockSpec((1, GROUP, TOK, TOK), lambda w, g: (w, g, 0, 0)),
    pl.BlockSpec((1, C, TOK), lambda w, g: (w, 0, 0)),
    pl.BlockSpec((1, 1, GROUP, TOK), lambda w, g: (w, g, 0, 0)),
]
SAVED_SHAPES = [
    jax.ShapeDtypeStruct((2, HEADS, TOK, TOK), BF16),
    jax.ShapeDtypeStruct((2, C, TOK), BF16),
    jax.ShapeDtypeStruct((2, HEADS // GROUP, GROUP, TOK), F32),
]


def params():
    return pltpu.CompilerParams(
        dimension_semantics=("arbitrary", "arbitrary"), vmem_limit_bytes=VMEM_LIMIT
    )


def forward_first(x, cot, weights):
    pieces = piece_shapes() * 2
    outs = pl.pallas_call(
        forward_kernel,
        grid=(2, GROUP),
        in_specs=[WINDOW, WINDOW] + [whole_block(s) for s in WEIGHTS],
        out_specs=SAVED + [whole_block(s) for s in pieces],
        out_shape=SAVED_SHAPES + [jax.ShapeDtypeStruct(s, BF16) for s in pieces],
        scratch_shapes=[
            pltpu.VMEM((C, TOK), BF16),
            pltpu.VMEM((TOK, C), BF16),
            pltpu.VMEM((HEADS * VROWS, TOK), BF16),
        ],
        compiler_params=params(),
        name="forward_first",
    )(x, cot, *weights)
    return outs[:3], outs[3:8], outs[8:]


def backward_first(scale, x, weights, saved, pieces):
    return pl.pallas_call(
        functools.partial(backward_first_kernel, scale),
        grid=(2, GROUP),
        in_specs=[WINDOW]
        + [whole_block(s) for s in WEIGHTS]
        + SAVED
        + [whole_block(s) for s in piece_shapes()],
        out_specs=[WINDOW] + [whole_block(s) for s in PARTS],
        out_shape=[jax.ShapeDtypeStruct(s, BF16) for s in [(14, 7, 8, C)] + PARTS],
        scratch_shapes=[
            pltpu.VMEM((TOK, C), F32),
            pltpu.VMEM((TOK, 1), F32),
            pltpu.VMEM((TOK, C), BF16),
            pltpu.VMEM((TOK, C), F32),
            pltpu.VMEM((TOK, C), BF16),
            pltpu.VMEM((C, TOK), BF16),
            pltpu.VMEM((TOK, C), BF16),
            pltpu.VMEM((C, TOK), BF16),
            pltpu.VMEM((128, TOK), BF16),
            pltpu.VMEM((128, TOK), BF16),
            pltpu.VMEM((TOK, 3 * C), BF16),
            pltpu.VMEM((C, 3 * C), F32),
            pltpu.VMEM((C, C), F32),
        ],
        compiler_params=params(),
        name="backward_first",
    )(x, *weights, *saved, *pieces)


def second_block(scale, y_pieces, c_pieces, weights):
    pieces = piece_shapes()
    return pl.pallas_call(
        functools.partial(second_kernel, scale),
        grid=(2, GROUP),
        in_specs=[whole_block(s) for s in pieces + pieces + WEIGHTS],
        out_specs=[whole_block(s) for s in pieces + PARTS],
        out_shape=[jax.ShapeDtypeStruct(s, BF16) for s in pieces + PARTS],
        scratch_shapes=[
            pltpu.VMEM((TOK, C), F32),
            pltpu.VMEM((TOK, 1), F32),
            pltpu.VMEM((TOK, C), BF16),
            pltpu.VMEM((TOK, C), F32),
            pltpu.VMEM((TOK, C), BF16),
            pltpu.VMEM((C, 512), BF16),
            pltpu.VMEM((TOK, C), BF16),
            pltpu.VMEM((C, 512), BF16),
            pltpu.VMEM((TOK, C), BF16),
            pltpu.VMEM((HEADS * VROWS, 512), BF16),
            pltpu.VMEM((C, 512), BF16),
            pltpu.VMEM((C, 512), BF16),
            pltpu.VMEM((128, 512), BF16),
            pltpu.VMEM((128, 512), BF16),
            pltpu.VMEM((TOK, 3 * C), BF16),
            pltpu.VMEM((TOK, 256), F32),
            pltpu.VMEM((TOK, 256), BF16),
            pltpu.VMEM((TOK, 128), F32),
            pltpu.VMEM((TOK, 128), F32),
            pltpu.VMEM((C, 3 * C), F32),
            pltpu.VMEM((C, C), F32),
        ],
        compiler_params=params(),
        name="second_block",
    )(*y_pieces, *c_pieces, *weights)


def coordinates():
    tm, rows = lax.axis_index("tm"), lax.axis_index("rows")
    return {
        "x": tm // 4 % 2 * 2 + rows // 2,
        "y": tm % 4,
        "z": tm // 8,
        "core": rows % 2,
    }


def device_at(place):
    tm = place["z"] * 8 + place["x"] // 2 * 4 + place["y"]
    return (tm, place["x"] % 2 * 2 + place["core"])


def beside(here, axis, steps):
    return device_at({**here, axis: (here[axis] + steps) % (2 if axis == "core" else 4)})


ORDERS = ("xyz", "yzx", "zxy")
MESH = pl.DeviceIdType.MESH


ROUTES = ((-1, 0), (1, 0), (0, -1), (1, -1))


def exchange_kernel(way, *refs):
    count = (len(refs) - 2) // 2
    sent, received, (send_sem, recv_sem) = refs[:count], refs[count : 2 * count], refs[2 * count :]
    tm, rows = lax.axis_index("tm"), lax.axis_index("rows")
    tm_size, rows_size = lax.axis_size("tm"), lax.axis_size("rows")

    def at(steps, sign):
        return (
            (tm + sign * steps[0] + tm_size) % tm_size,
            (rows + sign * steps[1] + rows_size) % rows_size,
        )

    barrier = pltpu.get_barrier_semaphore()
    for steps in ROUTES:
        pl.semaphore_signal(barrier, inc=1, device_id=at(steps, -way), device_id_type=MESH)
    pl.semaphore_wait(barrier, len(ROUTES))
    copies = []
    for i in range(count):
        copy = pltpu.make_async_remote_copy(
            src_ref=sent[i],
            dst_ref=received[i],
            send_sem=send_sem.at[i],
            recv_sem=recv_sem.at[i],
            device_id=at(ROUTES[i % 4], way),
            device_id_type=MESH,
        )
        copy.start()
        copies.append(copy)
    for copy in copies:
        copy.wait()


def exchanged(way, collective_id, *pieces):
    count = len(pieces)
    return pl.pallas_call(
        functools.partial(exchange_kernel, way),
        in_specs=[pl.BlockSpec(memory_space=pl.ANY)] * count,
        out_specs=[pl.BlockSpec(memory_space=pl.ANY)] * count,
        out_shape=[jax.ShapeDtypeStruct(p.shape, p.dtype) for p in pieces],
        scratch_shapes=[pltpu.SemaphoreType.DMA((count,)), pltpu.SemaphoreType.DMA((count,))],
        compiler_params=pltpu.CompilerParams(
            collective_id=collective_id, has_side_effects=True, vmem_limit_bytes=VMEM_LIMIT
        ),
        name="exchange_there" if way == 1 else "exchange_back",
    )(*pieces)


def reduce_kernel(jobs, *refs):
    matrices = 2 * jobs // 3
    parts, outs, refs = refs[:jobs], refs[jobs : jobs + matrices], refs[jobs + matrices :]
    scratch = refs[: 5 * jobs]
    held = [scratch[5 * i : 5 * i + 2] for i in range(jobs)]
    slots = [scratch[5 * i + 2 : 5 * i + 5] for i in range(jobs)]
    send_sem, recv_sem, local_sem = refs[5 * jobs :]
    here = coordinates()
    partners = [beside(here, "core", 1)] + [
        beside(here, axis, steps) for axis in "xyz" for steps in (1, 2, 3)
    ]
    barrier = pltpu.get_barrier_semaphore()
    for partner in partners:
        pl.semaphore_signal(barrier, inc=1, device_id=partner, device_id_type=MESH)

    local = []
    for i in range(jobs):
        copy = pltpu.make_async_copy(parts[i].at[here["core"]], held[i][0], local_sem.at[i])
        copy.start()
        local.append(copy)
    pl.semaphore_wait(barrier, len(partners))

    flying = []
    for i in range(jobs):
        copy = pltpu.make_async_remote_copy(
            src_ref=parts[i].at[1 - here["core"]],
            dst_ref=held[i][1],
            send_sem=send_sem.at[i, 0],
            recv_sem=recv_sem.at[i, 0],
            device_id=partners[0],
            device_id_type=MESH,
        )
        copy.start()
        flying.append([copy])

    sent = list(flying)
    sums = [None] * jobs
    for stage in range(4):
        for i in range(jobs):
            order = ORDERS[i % 3]
            for copy in flying[i]:
                copy.wait_recv()
            if stage == 0:
                local[i].wait()
                for a in range(4):
                    total = held[i][0][a].astype(F32) + held[i][1][a].astype(F32)
                    held[i][0][a] = total.astype(BF16)
                source = held[i][0]
            else:
                total = sums[i]
                for slot in range(3):
                    total = total + slots[i][stage - 1][slot].astype(F32)
                if stage == 3:
                    gqkv, gout = outs[i // 3 * 2 : i // 3 * 2 + 2]
                    if i % 3 == 2:
                        gqkv[:, 1280:1536] = total[:, 0:256]
                        gout[...] = total[:, 256:768]
                    else:
                        gqkv[:, 640 * (i % 3) : 640 * (i % 3 + 1)] = total
                    continue
                source = slots[i][stage - 1].at[3]
                source[...] = total.astype(BF16)
            axis = order[stage]
            copies = []
            for steps in (1, 2, 3):
                copy = pltpu.make_async_remote_copy(
                    src_ref=source.at[(here[axis] + steps) % 4],
                    dst_ref=slots[i][stage].at[steps - 1],
                    send_sem=send_sem.at[i, 3 * stage + steps],
                    recv_sem=recv_sem.at[i, 3 * stage + steps],
                    device_id=beside(here, axis, steps),
                    device_id_type=MESH,
                )
                copy.start()
                copies.append(copy)
            sums[i] = source[here[axis]].astype(F32)
            flying[i] = copies
            sent.append(copies)
    for copies in sent:
        for copy in copies:
            copy.wait_send()


def reduced(parts):
    jobs = len(parts)
    scratch = []
    for part in parts:
        width = part.shape[-1]
        scratch += [
            pltpu.VMEM((4, 4, 4, 4, width), BF16),
            pltpu.VMEM((4, 4, 4, 4, width), BF16),
            pltpu.VMEM((4, 4, 4, 4, width), BF16),
            pltpu.VMEM((4, 4, 4, width), BF16),
            pltpu.VMEM((4, 4, width), BF16),
        ]
    return pl.pallas_call(
        functools.partial(reduce_kernel, jobs),
        in_specs=[pl.BlockSpec(memory_space=pl.ANY)] * jobs,
        out_specs=[pl.BlockSpec(memory_space=pltpu.VMEM)] * (2 * jobs // 3),
        out_shape=[
            jax.ShapeDtypeStruct((4, width), F32) for _ in range(jobs // 3) for width in (3 * C, C)
        ],
        scratch_shapes=scratch
        + [
            pltpu.SemaphoreType.DMA((jobs, 10)),
            pltpu.SemaphoreType.DMA((jobs, 10)),
            pltpu.SemaphoreType.DMA((jobs,)),
        ],
        compiler_params=pltpu.CompilerParams(
            collective_id=0, has_side_effects=True, vmem_limit_bytes=VMEM_LIMIT
        ),
        name="reduce_gradients",
    )(*parts)


def per_device(
    video_clip, cotangent,
    gain_first, bias_first, qkv_first, out_first,
    gain_second, bias_second, qkv_second, out_second,
):
    frames, rows_here, columns, channels = video_clip.shape
    devices = lax.axis_size("tm") * lax.axis_size("rows")
    scale = 1.0 / math.sqrt(frames * rows_here * columns * devices)
    x = video_clip.transpose(1, 2, 0, 3)
    cot = cotangent.transpose(1, 2, 0, 3)
    first = (gain_first.reshape(1, C), bias_first.reshape(1, C), qkv_first, out_first)
    second = (gain_second.reshape(1, C), bias_second.reshape(1, C), qkv_second, out_second)
    saved, y_pieces, c_pieces = forward_first(x, cot, first)
    arrived = exchanged(1, 1, *y_pieces[1:], *c_pieces[1:])
    y_pieces = [y_pieces[0], *arrived[:4]]
    c_pieces = [c_pieces[0], *arrived[4:]]
    *d_pieces, part0, part1, part2 = second_block(scale, y_pieces, c_pieces, second)
    d_pieces = [d_pieces[0], *exchanged(-1, 2, *d_pieces[1:])]
    grad, *parts = backward_first(scale, x, first, saved, d_pieces)
    sums = reduced([*parts, part0, part1, part2])
    return (grad.transpose(2, 0, 1, 3), *sums)


def solution(mesh):
    clip = P("tm", "rows", None, None)
    scattered = P(("tm", "rows"), None)
    return jax.shard_map(
        per_device,
        mesh=mesh,
        in_specs=(clip, clip) + (P(),) * 8,
        out_specs=(clip,) + (scattered,) * 4,
        check_vma=False,
    )
```

```python
import functools
import math

import jax
import jax.numpy as jnp
from jax import lax
from jax.experimental import pallas as pl
from jax.experimental.pallas import tpu as pltpu
from jax.sharding import PartitionSpec as P

F32, BF16 = jnp.float32, jnp.bfloat16
C, HEADS, HD = 512, 16, 32
TOK = 392
GROUP = 4
VROWS = 48
LOG2E = math.log2(math.e)
QSCALE = HD ** (-0.5) * LOG2E
MASKED = -1000000000.0 * LOG2E
LN2 = math.log(2.0)
SPLIT = ((0, 224), (224, 392))
VIRTUAL = 16
ROWS = 400
VMEM_LIMIT = 56 * 1024 * 1024


def mm(a, b):
    return lax.dot_general(a, b, (((1,), (0,)), ((), ())), preferred_element_type=F32)


def mm_nt(a, b):
    return lax.dot_general(a, b, (((1,), (1,)), ((), ())), preferred_element_type=F32)


def mm_tn(a, b):
    return lax.dot_general(a, b, (((0,), (0,)), ((), ())), preferred_element_type=F32)


def standardized(values):
    center = values - jnp.mean(values, axis=-1, keepdims=True)
    rstd = lax.rsqrt(jnp.mean(center * center, axis=-1, keepdims=True) + 1e-05)
    return center * rstd, rstd


def tiles(block):
    return block.astype(F32).reshape(-1, C)


def own_lanes(j, block):
    lane = lax.broadcasted_iota(jnp.int32, block.shape, 1) // HD
    return jnp.where(lane == j, block, jnp.zeros_like(block))


def put_diagonal(ref, turned, pitch, column=0):
    for head in range(HEADS):
        at = pitch * (head % GROUP) + column
        ref[HD * head : HD * (head + 1), at : at + turned.shape[1]] = turned[HD * head : HD * (head + 1)]


def put_values(vt, turned, lane):
    count = turned.shape[1]
    for head in range(HEADS):
        vt[VROWS * head : VROWS * head + HD, lane : lane + count] = turned[HD * head : HD * (head + 1)]
        vt[VROWS * head + HD : VROWS * (head + 1), lane : lane + count] = jnp.ones(
            (VROWS - HD, count), BF16
        )


def channels_of(g, first=0):
    return pl.ds(pl.multiple_of(g * 128 + first, 128), 128)


def head_channels(g, j):
    return pl.ds(pl.multiple_of(g * 128 + j * HD, HD), HD)


def head_values(g, j):
    return pl.ds(pl.multiple_of(g * GROUP * VROWS + j * VROWS, 16), VROWS)


MESH = pl.DeviceIdType.MESH
ROUTES = ((-1, 0), (1, 0), (0, -1), (1, -1))


class Exchange:
    def __init__(self, way, send_sem, recv_sem):
        self.way, self.sems, self.copies = way, (send_sem, recv_sem), []

    def device(self, steps, sign):
        size = lax.axis_size("tm"), lax.axis_size("rows")
        here = lax.axis_index("tm"), lax.axis_index("rows")
        return tuple((i + sign * d + n) % n for i, d, n in zip(here, steps, size))

    def greet(self):
        for steps in ROUTES:
            pl.semaphore_signal(
                pltpu.get_barrier_semaphore(),
                inc=1,
                device_id=self.device(steps, -self.way),
                device_id_type=MESH,
            )

    def wait_for_others(self):
        pl.semaphore_wait(pltpu.get_barrier_semaphore(), len(ROUTES))

    def send(self, route, source, target):
        i = len(self.copies)
        copy = pltpu.make_async_remote_copy(
            src_ref=source,
            dst_ref=target,
            send_sem=self.sems[0].at[i],
            recv_sem=self.sems[1].at[i],
            device_id=self.device(ROUTES[route], self.way),
            device_id_type=MESH,
        )
        copy.start()
        self.copies.append(copy)

    def wait(self):
        for copy in self.copies:
            copy.wait()


def pieces_of(whole, w, pieces):
    own, ahead, behind, above, corner = pieces
    if w == 0:
        above[...] = whole[0:3, :, 0:4].astype(BF16)
        corner[...] = whole[0:3, :, 4:8].astype(BF16)
        ahead[0:4] = whole[3:7, :, 0:4].astype(BF16)
        own[0:4] = whole[3:7, :, 4:8].astype(BF16)
    else:
        ahead[4:7] = whole[0:3, :, 0:4].astype(BF16)
        own[4:7] = whole[0:3, :, 4:8].astype(BF16)
        behind[...] = whole[3:7, :, 4:8].astype(BF16)
        own[7:11] = whole[3:7, :, 0:4].astype(BF16)


def joined(low, high):
    return jnp.concatenate([low.astype(F32), high.astype(F32)], axis=2)


def forward_kernel(
    x_ref, cot_ref, gain_ref, bias_ref, wqkv_ref, wout_ref, mixt_ref, stat_ref, *refs,
):
    y_own, c_own, y_there, c_there, y_here, c_here = (
        refs[0], refs[1], refs[2:6], refs[6:10], refs[10:14], refs[14:18]
    )
    qbd, k, vt, send_sem, recv_sem = refs[18:]
    exchange = Exchange(1, send_sem, recv_sem)
    exchange.greet()
    for w in range(2):
        pieces_of(cot_ref[7 * w : 7 * w + 7].astype(F32), w, (c_own, *c_here))
    exchange.wait_for_others()
    for route in range(4):
        exchange.send(route, c_here[route], c_there[route])
    qbd[...] = jnp.zeros_like(qbd)
    for w in range(2):
        rows = slice(7 * w, 7 * w + 7)
        x = tiles(x_ref[rows])
        xhat, _ = standardized(x)
        normed = (xhat * gain_ref[...] + bias_ref[...]).astype(BF16)
        put_diagonal(qbd, (mm(normed, wqkv_ref[:, 0:C]) * QSCALE).astype(BF16).T, 512)
        k[...] = mm(normed, wqkv_ref[:, C : 2 * C]).astype(BF16)
        put_values(vt, mm(normed, wqkv_ref[:, 2 * C :]).astype(BF16).T, 0)

        def group(g, carry):
            kg = k[:, channels_of(g)]
            for j in range(GROUP):
                lanes = slice(512 * j, 512 * (j + 1))
                scores = mm(kg, qbd[channels_of(g), lanes])
                top = jnp.max(scores, axis=0, keepdims=True)
                e = jnp.exp2(scores - top).astype(BF16)
                mixed = mm(vt[head_values(g, j), :], e)
                sums = mixed[HD : HD + 1]
                stat_ref[w, g, :, lanes] = top + jnp.log2(sums)
                mixt_ref[w, head_channels(g, j), :] = (mixed[:HD] * (1.0 / sums)).astype(BF16)
            return carry

        lax.fori_loop(0, HEADS // GROUP, group, 0)
        y = x + mm_tn(mixt_ref[w, :, 0:TOK], wout_ref[...])
        pieces_of(y.reshape(7, 7, 8, C), w, (y_own, *y_here))
        if w == 0:
            exchange.send(2, y_here[2], y_there[2])
            exchange.send(3, y_here[3], y_there[3])
            exchange.send(0, y_here[0].at[0:4], y_there[0].at[0:4])
        else:
            exchange.send(0, y_here[0].at[4:7], y_there[0].at[4:7])
            exchange.send(1, y_here[1], y_there[1])
    exchange.wait()


def write_parts(gqkv, gout, parts):
    def layer(z, carry):
        for xy in range(16):
            x, y = xy // 4, xy % 4
            rows = pl.ds(pl.multiple_of((z * 16 + x // 2 * 8 + y * 2 + x % 2) * 8, 8), 8)
            blocks = (
                gqkv[rows, 0:640],
                gqkv[rows, 640:1280],
                jnp.concatenate([gqkv[rows, 1280:1536], gout[rows, :]], axis=1),
            )
            for part, block, place in zip(parts, blocks, ((x, y, z), (y, z, x), (z, x, y))):
                part[(0,) + place] = block[0:4].astype(BF16)
                part[(1,) + place] = block[4:8].astype(BF16)
        return carry

    lax.fori_loop(0, 4, layer, 0)


def norm_backward(dnormed, xhat, rstd, gain):
    d = dnormed.astype(BF16).astype(F32) * gain
    return rstd * (
        d
        - jnp.mean(d, axis=-1, keepdims=True)
        - xhat * jnp.mean(d * xhat, axis=-1, keepdims=True)
    )


def finish_gradients(scale, normed, dproj, mixt, cot_b, gqkv_s, gout_s, part_refs):
    gout_s[...] = mm(mixt[...], cot_b[...]) * scale
    gqkv_s[...] = mm_tn(normed[...], dproj[...]) * scale
    write_parts(gqkv_s, gout_s, part_refs)


def backward_first_kernel(
    scale,
    x_ref, gain_ref, bias_ref, wqkv_ref, wout_ref, mixt_ref, stat_ref,
    own, ahead, behind, above, corner,
    grad_ref, part0_ref, part1_ref, part2_ref,
    normed_s, dproj, cot_b, mixt_all, qbd, k, kt, v, qn, don, dobd, p_s, ds_s, dqt, do_rows, q_rows, gqkv_s, gout_s,
):
    for ref in (qbd, dobd, do_rows, q_rows, normed_s, dproj, cot_b):
        ref[...] = jnp.zeros_like(ref)
    for w in range(2):
        base = ROWS * w
        xhat, rstd = standardized(tiles(x_ref[7 * w : 7 * w + 7]))
        normed = (xhat * gain_ref[...] + bias_ref[...]).astype(BF16)
        normed_s[base : base + TOK] = normed
        queries = (mm(normed, wqkv_ref[:, 0:C]) * QSCALE).astype(BF16)
        qn[...] = queries
        put_diagonal(qbd, queries.T, 512)
        keys = mm(normed, wqkv_ref[:, C : 2 * C]).astype(BF16)
        k[...] = keys
        kt[...] = keys.T
        v[...] = mm(normed, wqkv_ref[:, 2 * C :]).astype(BF16)
        if w == 0:
            parts = [joined(above[...], corner[...]), joined(ahead[0:4], own[0:4])]
        else:
            parts = [joined(ahead[4:7], own[4:7]), joined(own[7:11], behind[...])]
        cot = jnp.concatenate([part.reshape(-1, C) for part in parts], axis=0)
        cot_h = cot.astype(BF16)
        cot_b[512 * w : 512 * w + TOK] = cot_h
        dmixed = mm_nt(cot_h, wout_ref[...]).astype(BF16)
        don[...] = dmixed
        put_diagonal(dobd, dmixed.T, 512)
        mixt_all[:, 512 * w : 512 * (w + 1)] = mixt_ref[w]

        def group(g, carry):
            kg = k[:, channels_of(g)]
            vg = v[:, channels_of(g)]
            qg = qn[:, channels_of(g)]
            dog = don[:, channels_of(g)]
            for j in range(GROUP):
                lanes = slice(512 * j, 512 * (j + 1))
                do_rows[512 * j : 512 * j + TOK] = own_lanes(j, dog)
                q_rows[512 * j : 512 * j + TOK] = own_lanes(j, qg)
                scores = mm(kg, qbd[channels_of(g), lanes])
                p = jnp.exp2(scores - stat_ref[w, g, :, lanes]).astype(BF16)
                p_s[:, lanes] = p
                dsum = jnp.sum(
                    mixt_ref[w, head_channels(g, j), :].astype(F32)
                    * dobd[head_channels(g, j), lanes].astype(F32),
                    axis=0, keepdims=True,
                )
                dp = mm(vg, dobd[channels_of(g), lanes]) - dsum
                ds = (p.astype(F32) * dp).astype(BF16)
                ds_s[:, lanes] = ds
                dq = mm(kt[head_channels(g, j), :], ds)
                dqt[HD * j : HD * (j + 1), :] = (dq[:, 0:TOK] * HD ** (-0.5)).astype(BF16)
            dk = mm(ds_s[...], q_rows[...]) * LN2
            dv = mm(p_s[...], do_rows[...])
            rows = slice(base, base + TOK)
            dproj[rows, channels_of(g)] = dqt[...].T
            dproj[rows, channels_of(g, C)] = dk.astype(BF16)
            dproj[rows, channels_of(g, 2 * C)] = dv.astype(BF16)
            return carry

        lax.fori_loop(0, HEADS // GROUP, group, 0)
        dnormed = mm_nt(dproj[base : base + TOK], wqkv_ref[...])
        total = cot + norm_backward(dnormed, xhat, rstd, gain_ref[...])
        grad_ref[7 * w : 7 * w + 7] = total.reshape(7, 7, 8, C).astype(BF16)
    finish_gradients(
        scale, normed_s, dproj, mixt_all, cot_b, gqkv_s, gout_s, (part0_ref, part1_ref, part2_ref)
    )


def second_kernel(
    scale,
    y_own, y_ahead, y_behind, y_above, y_corner, c_own, c_ahead, c_behind, c_above, c_corner,
    gain_ref, bias_ref, wqkv_ref, wout_ref,
    own, ahead_there, behind_there, above_there, corner_there, part0_ref, part1_ref, part2_ref,
    normed_s, dproj, cot_b, mixt, qbd, k, kt, v, vt, qn, dot_s, dobd, dopt, dqt,
    e_a, e_b, ds_a, ds_b, do_rows, q_rows, pen, cot_s, xhat_s, gqkv_s, gout_s,
    ahead, behind, above, corner, send_sem, recv_sem,
):
    exchange = Exchange(-1, send_sem, recv_sem)
    exchange.greet()
    e_s, ds_s = (e_a, e_b), (ds_a, ds_b)
    for ref in (qbd, dobd, do_rows, q_rows, normed_s, dproj, cot_b, mixt):
        ref[...] = jnp.zeros_like(ref)
    for w in range(2):
        base = ROWS * w
        last_frames = lax.axis_index("tm") == (lax.axis_size("tm") - 1 if w == 0 else 0)
        last_rows = (lax.axis_index("rows") == lax.axis_size("rows") - 1) if w == 1 else False

        def region_of(token, segment):
            columns = 4 if segment == 0 else 3
            late = jnp.where(last_frames & (token % 8 < 4), 1, 0)
            below = jnp.where(last_rows & (token // 8 // columns >= 4), 2, 0)
            return late + below

        def gather(into, own, ahead, behind, above, corner):
            def put(rho, count, whole):
                into[32 * rho : 32 * (rho + count)] = whole[:, 3:7].reshape(-1, C)
                into[224 + 24 * rho : 224 + 24 * (rho + count)] = whole[:, 0:3].reshape(-1, C)

            if w == 0:
                put(0, 7, joined(ahead[...], own[0:7]))
            else:
                put(0, 4, joined(own[7:11], behind[...]))
                put(4, 3, joined(above[...], corner[...]))

        gather(xhat_s, y_own, y_ahead, y_behind, y_above, y_corner)
        gather(cot_s, c_own, c_ahead, c_behind, c_above, c_corner)
        xhat, rstd = standardized(xhat_s[...])
        xhat_s[...] = xhat
        normed = (xhat * gain_ref[...] + bias_ref[...]).astype(BF16)
        normed_s[base : base + TOK] = normed
        queries = (mm(normed, wqkv_ref[:, 0:C]) * QSCALE).astype(BF16)
        qn[...] = queries
        keys = mm(normed, wqkv_ref[:, C : 2 * C]).astype(BF16)
        k[...] = keys
        values_f = mm(normed, wqkv_ref[:, 2 * C :])
        values = values_f.astype(BF16)
        v[...] = values
        cot_h = cot_s[...].astype(BF16)
        dmixed = mm_nt(cot_h, wout_ref[...]).astype(BF16)
        for s, (start, stop) in enumerate(SPLIT):
            count = stop - start
            cot_b[512 * w + 256 * s : 512 * w + 256 * s + count] = cot_h[start:stop]
            put_diagonal(qbd, queries[start:stop].T, 256, 1024 * s)
            kt[:, 256 * s : 256 * s + count] = keys[start:stop].T
            dot_s[:, 256 * s : 256 * s + count] = dmixed[start:stop].T
            turned = values[start:stop].T
            put_values(vt, turned, 256 * s)
            total = jnp.sum(turned.astype(F32), axis=1, keepdims=True)
            other = 1 - s
            lane = 256 * other + SPLIT[other][1] - SPLIT[other][0]
            first = lax.broadcasted_iota(jnp.int32, (C, VIRTUAL), 1) == 0
            total = jnp.where(first, total, 0.0).astype(BF16)
            number = jnp.where(first[0 : VROWS - HD], float(count), 0.0).astype(BF16)
            for head in range(HEADS):
                at = VROWS * head
                vt[at : at + HD, lane : lane + VIRTUAL] = total[HD * head : HD * (head + 1)]
                vt[at + HD : at + VROWS, lane : lane + VIRTUAL] = number
            shape = (count, 256)
            key = region_of(lax.broadcasted_iota(jnp.int32, shape, 0), s)
            query = region_of(lax.broadcasted_iota(jnp.int32, shape, 1), s)
            pen[start:stop] = jnp.where(key == query, 0.0, 1.0)

        def group(g, carry):
            virtual_dv = []
            grads = []
            for s, (start, stop) in enumerate(SPLIT):
                count = stop - start
                kg = k[start:stop, channels_of(g)]
                apart = pen[start:stop] > 0.5
                sums_of = []
                for j in range(GROUP):
                    lanes = slice(256 * j, 256 * (j + 1))
                    scores = mm(kg, qbd[channels_of(g), 1024 * s + 256 * j : 1024 * s + 256 * (j + 1)])
                    scores = jnp.where(apart, MASKED, scores)
                    top = jnp.maximum(jnp.max(scores, axis=0, keepdims=True), MASKED)
                    e_s[s][0:count, lanes] = jnp.exp2(scores - top).astype(BF16)
                    first = lax.broadcasted_iota(jnp.int32, (VIRTUAL, 256), 0) == 0
                    e_s[s][count : count + VIRTUAL, lanes] = jnp.where(
                        first, jnp.exp2(MASKED - top), 0.0
                    ).astype(BF16)
                for j in range(GROUP):
                    lanes = slice(256 * j, 256 * (j + 1))
                    tokens = slice(256 * s, 256 * (s + 1))
                    mixed = mm(
                        vt[head_values(g, j), 256 * s : 256 * s + count + VIRTUAL], e_s[s][:, lanes]
                    )
                    inv = 1.0 / mixed[HD : HD + 1]
                    mixed = mixed[:HD] * inv
                    mixt[head_channels(g, j), 512 * w + 256 * s : 512 * w + 256 * s + count] = mixed[
                        :, 0:count
                    ].astype(BF16)
                    do = dot_s[head_channels(g, j), tokens].astype(F32) * inv
                    inside = lax.broadcasted_iota(jnp.int32, do.shape, 1) < count
                    do = jnp.where(inside, do, 0.0).astype(BF16)
                    sums_of.append(jnp.sum(mixed * do.astype(F32), axis=0, keepdims=True))
                    dopt[HD * j : HD * (j + 1), tokens] = do
                    dobd[HD * j : HD * (j + 1), 1024 * s + 256 * j : 1024 * s + 256 * (j + 1)] = do
                turned = dopt[:, 256 * s : 256 * (s + 1)].T
                qg = qn[start:stop, channels_of(g)]
                for j in range(GROUP):
                    lanes = slice(256 * j, 256 * (j + 1))
                    at = 1024 * s + 256 * j
                    do_rows[at : at + 256] = own_lanes(j, turned)
                    q_rows[at : at + count] = own_lanes(j, qg)
                    dp = mm(v[start:stop, channels_of(g)], dobd[:, at : at + 256]) - sums_of[j]
                    ds = e_s[s][0:count, lanes].astype(F32) * jnp.where(apart, 0.0, dp)
                    ds = ds.astype(BF16)
                    ds_s[s][:, lanes] = ds
                    dq = mm(kt[head_channels(g, j), 256 * s : 256 * s + count], ds)
                    dqt[HD * j : HD * (j + 1), 256 * s : 256 * (s + 1)] = (dq * HD ** (-0.5)).astype(BF16)
                block = slice(1024 * s, 1024 * (s + 1))
                dv = mm(e_s[s][...], do_rows[block])
                dk = mm(ds_s[s][...], q_rows[block]) * LN2
                virtual_dv.append(dv[count : count + 1])
                grads.append((dk, dv[0:count]))
            for s, (start, stop) in enumerate(SPLIT):
                rows = slice(base + start, base + stop)
                dk, dv = grads[s]
                dproj[rows, channels_of(g)] = dqt[:, 256 * s : 256 * s + stop - start].T
                dproj[rows, channels_of(g, C)] = dk.astype(BF16)
                dproj[rows, channels_of(g, 2 * C)] = (dv + virtual_dv[1 - s]).astype(BF16)
            return carry

        lax.fori_loop(0, HEADS // GROUP, group, 0)
        dnormed = mm_nt(dproj[base : base + TOK], wqkv_ref[...])
        total = cot_s[...] + norm_backward(dnormed, xhat_s[...], rstd, gain_ref[...])
        whole = jnp.concatenate(
            [total[224:392].reshape(7, 3, 8, C), total[0:224].reshape(7, 4, 8, C)], axis=1
        )
        low, high = whole[:, :, 0:4].astype(BF16), whole[:, :, 4:8].astype(BF16)
        if w == 0:
            ahead[...] = low
            own[0:7] = high
            exchange.wait_for_others()
            exchange.send(0, ahead, ahead_there)
        else:
            own[7:11] = low[0:4]
            behind[...] = high[0:4]
            above[...] = low[4:7]
            corner[...] = high[4:7]
            exchange.send(1, behind, behind_there)
            exchange.send(2, above, above_there)
            exchange.send(3, corner, corner_there)
    finish_gradients(
        scale, normed_s, dproj, mixt, cot_b, gqkv_s, gout_s, (part0_ref, part1_ref, part2_ref)
    )
    exchange.wait()


def piece_shapes():
    return [(rows, 7, 4, C) for rows in (11, 7, 4, 3, 3)]


WIDTHS = (640, 640, 768)
PARTS = [(2, 4, 4, 4, 4, width) for width in WIDTHS]
SAVED = [
    jax.ShapeDtypeStruct((2, C, 512), BF16),
    jax.ShapeDtypeStruct((2, HEADS // GROUP, 1, 2048), F32),
]
TOKENS = (14, 7, 8, C)
IN_VMEM = pl.BlockSpec(memory_space=pltpu.VMEM)


ANYWHERE = pl.BlockSpec(memory_space=pl.ANY)


def call(kernel, name, args, out_shape, scratch, there=(), copies=0, collective_id=None):
    semaphores = [pltpu.SemaphoreType.DMA((copies,))] * 2 if copies else []
    return pl.pallas_call(
        kernel,
        in_specs=[IN_VMEM] * len(args),
        out_specs=[ANYWHERE if i in there else IN_VMEM for i in range(len(out_shape))],
        out_shape=out_shape,
        scratch_shapes=[pltpu.VMEM(shape, dtype) for shape, dtype in scratch] + semaphores,
        compiler_params=pltpu.CompilerParams(
            vmem_limit_bytes=VMEM_LIMIT,
            has_side_effects=bool(copies),
            collective_id=collective_id,
        ),
        name=name,
    )(*args)


def halves(shapes):
    return [jax.ShapeDtypeStruct(shape, BF16) for shape in shapes]


def forward_first(x, cot, weights):
    pieces = piece_shapes()
    outs = call(
        forward_kernel,
        "forward_first",
        (x, cot, *weights),
        SAVED + halves(pieces[:1] * 2 + pieces[1:] * 2),
        [(shape, BF16) for shape in pieces[1:] * 2]
        + [((C, 2048), BF16), ((TOK, C), BF16), ((HEADS * VROWS, TOK), BF16)],
        there=range(4, 12),
        copies=9,
        collective_id=1,
    )
    return outs[:2], [outs[2], *outs[4:8]], [outs[3], *outs[8:12]]


GRADIENT_SCRATCH = [((2 * ROWS, C), BF16), ((2 * ROWS, 3 * C), BF16), ((1024, C), BF16), ((C, 1024), BF16)]
MATRICES = [((C, 3 * C), F32), ((C, C), F32)]


def backward_first(scale, x, weights, saved, pieces):
    return call(
        functools.partial(backward_first_kernel, scale),
        "backward_first",
        (x, *weights, *saved, *pieces),
        halves([TOKENS] + PARTS),
        GRADIENT_SCRATCH
        + [
            ((C, 2048), BF16), ((TOK, C), BF16), ((C, TOK), BF16), ((TOK, C), BF16),
            ((TOK, C), BF16), ((TOK, C), BF16), ((C, 2048), BF16),
            ((TOK, 2048), BF16), ((TOK, 2048), BF16), ((128, TOK), BF16),
            ((2048, 128), BF16), ((2048, 128), BF16),
        ]
        + MATRICES,
    )


def second_block(scale, y_pieces, c_pieces, weights):
    return call(
        functools.partial(second_kernel, scale),
        "second_block",
        (*y_pieces, *c_pieces, *weights),
        halves(piece_shapes() + PARTS),
        GRADIENT_SCRATCH
        + [
            ((C, 2048), BF16), ((TOK, C), BF16), ((C, 512), BF16), ((TOK, C), BF16),
            ((HEADS * VROWS, 512), BF16), ((TOK, C), BF16), ((C, 512), BF16),
            ((128, 2048), BF16), ((128, 512), BF16), ((128, 512), BF16),
            ((224 + VIRTUAL, 1024), BF16), ((168 + VIRTUAL, 1024), BF16),
            ((224, 1024), BF16), ((168, 1024), BF16),
            ((2048, 128), BF16), ((2048, 128), BF16),
            ((TOK, 256), F32), ((TOK, C), F32), ((TOK, C), F32),
        ]
        + MATRICES
        + [(shape, BF16) for shape in piece_shapes()[1:]],
        there=range(1, 5),
        copies=4,
        collective_id=2,
    )


def coordinates():
    tm, rows = lax.axis_index("tm"), lax.axis_index("rows")
    return {
        "x": tm // 4 % 2 * 2 + rows // 2,
        "y": tm % 4,
        "z": tm // 8,
        "core": rows % 2,
    }


def device_at(place):
    tm = place["z"] * 8 + place["x"] // 2 * 4 + place["y"]
    return (tm, place["x"] % 2 * 2 + place["core"])


def beside(here, axis, steps):
    return device_at({**here, axis: (here[axis] + steps) % (2 if axis == "core" else 4)})


ORDERS = ("xyz", "yzx", "zxy")


def reduce_kernel(jobs, *refs):
    matrices = 2 * jobs // 3
    parts, outs, refs = refs[:jobs], refs[jobs : jobs + matrices], refs[jobs + matrices :]
    scratch = refs[: 5 * jobs]
    held = [scratch[5 * i : 5 * i + 2] for i in range(jobs)]
    slots = [scratch[5 * i + 2 : 5 * i + 5] for i in range(jobs)]
    send_sem, recv_sem, local_sem = refs[5 * jobs :]
    here = coordinates()
    partners = [beside(here, "core", 1)] + [
        beside(here, axis, steps) for axis in "xyz" for steps in (1, 2, 3)
    ]
    barrier = pltpu.get_barrier_semaphore()
    for partner in partners:
        pl.semaphore_signal(barrier, inc=1, device_id=partner, device_id_type=MESH)

    local = []
    for i in range(jobs):
        copy = pltpu.make_async_copy(parts[i].at[here["core"]], held[i][0], local_sem.at[i])
        copy.start()
        local.append(copy)
    pl.semaphore_wait(barrier, len(partners))

    flying = []
    for i in range(jobs):
        copy = pltpu.make_async_remote_copy(
            src_ref=parts[i].at[1 - here["core"]],
            dst_ref=held[i][1],
            send_sem=send_sem.at[i, 0],
            recv_sem=recv_sem.at[i, 0],
            device_id=partners[0],
            device_id_type=MESH,
        )
        copy.start()
        flying.append([copy])

    sent = list(flying)
    sums = [None] * jobs
    for stage in range(4):
        for i in range(jobs):
            order = ORDERS[i % 3]
            for copy in flying[i]:
                copy.wait_recv()
            if stage == 0:
                local[i].wait()
                for a in range(4):
                    total = held[i][0][a].astype(F32) + held[i][1][a].astype(F32)
                    held[i][0][a] = total.astype(BF16)
                source = held[i][0]
            else:
                total = sums[i]
                for slot in range(3):
                    total = total + slots[i][stage - 1][slot].astype(F32)
                if stage == 3:
                    gqkv, gout = outs[i // 3 * 2 : i // 3 * 2 + 2]
                    if i % 3 == 2:
                        gqkv[:, 1280:1536] = total[:, 0:256]
                        gout[...] = total[:, 256:768]
                    else:
                        gqkv[:, 640 * (i % 3) : 640 * (i % 3 + 1)] = total
                    continue
                source = slots[i][stage - 1].at[3]
                source[...] = total.astype(BF16)
            axis = order[stage]
            copies = []
            for steps in (1, 2, 3):
                copy = pltpu.make_async_remote_copy(
                    src_ref=source.at[(here[axis] + steps) % 4],
                    dst_ref=slots[i][stage].at[steps - 1],
                    send_sem=send_sem.at[i, 3 * stage + steps],
                    recv_sem=recv_sem.at[i, 3 * stage + steps],
                    device_id=beside(here, axis, steps),
                    device_id_type=MESH,
                )
                copy.start()
                copies.append(copy)
            sums[i] = source[here[axis]].astype(F32)
            flying[i] = copies
            sent.append(copies)
    for copies in sent:
        for copy in copies:
            copy.wait_send()


def reduced(parts):
    jobs = len(parts)
    scratch = []
    for part in parts:
        width = part.shape[-1]
        scratch += [
            pltpu.VMEM((4, 4, 4, 4, width), BF16),
            pltpu.VMEM((4, 4, 4, 4, width), BF16),
            pltpu.VMEM((4, 4, 4, 4, width), BF16),
            pltpu.VMEM((4, 4, 4, width), BF16),
            pltpu.VMEM((4, 4, width), BF16),
        ]
    return pl.pallas_call(
        functools.partial(reduce_kernel, jobs),
        in_specs=[pl.BlockSpec(memory_space=pl.ANY)] * jobs,
        out_specs=[pl.BlockSpec(memory_space=pltpu.VMEM)] * (2 * jobs // 3),
        out_shape=[
            jax.ShapeDtypeStruct((4, width), F32) for _ in range(jobs // 3) for width in (3 * C, C)
        ],
        scratch_shapes=scratch
        + [
            pltpu.SemaphoreType.DMA((jobs, 10)),
            pltpu.SemaphoreType.DMA((jobs, 10)),
            pltpu.SemaphoreType.DMA((jobs,)),
        ],
        compiler_params=pltpu.CompilerParams(
            collective_id=0, has_side_effects=True, vmem_limit_bytes=VMEM_LIMIT
        ),
        name="reduce_gradients",
    )(*parts)


def per_device(
    video_clip, cotangent,
    gain_first, bias_first, qkv_first, out_first,
    gain_second, bias_second, qkv_second, out_second,
):
    frames, rows_here, columns, channels = video_clip.shape
    devices = lax.axis_size("tm") * lax.axis_size("rows")
    scale = 1.0 / math.sqrt(frames * rows_here * columns * devices)
    x = video_clip.transpose(1, 2, 0, 3)
    cot = cotangent.transpose(1, 2, 0, 3)
    first = (gain_first.reshape(1, C), bias_first.reshape(1, C), qkv_first, out_first)
    second = (gain_second.reshape(1, C), bias_second.reshape(1, C), qkv_second, out_second)
    saved, y_pieces, c_pieces = forward_first(x, cot, first)
    *d_pieces, part0, part1, part2 = second_block(scale, y_pieces, c_pieces, second)
    grad, *parts = backward_first(scale, x, first, saved, d_pieces)
    sums = reduced([*parts, part0, part1, part2])
    return (grad.transpose(2, 0, 1, 3), *sums)


def solution(mesh):
    clip = P("tm", "rows", None, None)
    scattered = P(("tm", "rows"), None)
    return jax.shard_map(
        per_device,
        mesh=mesh,
        in_specs=(clip, clip) + (P(),) * 8,
        out_specs=(clip,) + (scattered,) * 4,
        check_vma=False,
    )
```

```python
import functools
import math

import jax
import jax.numpy as jnp
from jax import lax
from jax.experimental import pallas as pl
from jax.experimental.pallas import tpu as pltpu
from jax.sharding import PartitionSpec as P

F32, BF16 = jnp.float32, jnp.bfloat16
C, HEADS, HD = 512, 16, 32
TOK = 392
GROUP = 4
VROWS = 48
LOG2E = math.log2(math.e)
QSCALE = HD ** (-0.5) * LOG2E
MASKED = -1000000000.0 * LOG2E
LN2 = math.log(2.0)
SPLIT = ((0, 224), (224, 392))
VIRTUAL = 16
ROWS = 400
VMEM_LIMIT = 56 * 1024 * 1024


def mm(a, b):
    return lax.dot_general(a, b, (((1,), (0,)), ((), ())), preferred_element_type=F32)


def mm_nt(a, b):
    return lax.dot_general(a, b, (((1,), (1,)), ((), ())), preferred_element_type=F32)


def mm_tn(a, b):
    return lax.dot_general(a, b, (((0,), (0,)), ((), ())), preferred_element_type=F32)


def standardized(values):
    center = values - jnp.mean(values, axis=-1, keepdims=True)
    rstd = lax.rsqrt(jnp.mean(center * center, axis=-1, keepdims=True) + 1e-05)
    return center * rstd, rstd


def tiles(block):
    return block.astype(F32).reshape(-1, C)


def own_lanes(j, block):
    lane = lax.broadcasted_iota(jnp.int32, block.shape, 1) // HD
    return jnp.where(lane == j, block, jnp.zeros_like(block))


def put_diagonal(ref, turned, pitch, column=0):
    for head in range(HEADS):
        at = pitch * (head % GROUP) + column
        ref[HD * head : HD * (head + 1), at : at + turned.shape[1]] = turned[HD * head : HD * (head + 1)]


def put_values(vt, turned, lane):
    count = turned.shape[1]
    for head in range(HEADS):
        vt[VROWS * head : VROWS * head + HD, lane : lane + count] = turned[HD * head : HD * (head + 1)]
        vt[VROWS * head + HD : VROWS * (head + 1), lane : lane + count] = jnp.ones(
            (VROWS - HD, count), BF16
        )


def channels_of(g, first=0):
    return pl.ds(pl.multiple_of(g * 128 + first, 128), 128)


def head_channels(g, j):
    return pl.ds(pl.multiple_of(g * 128 + j * HD, HD), HD)


def head_values(g, j):
    return pl.ds(pl.multiple_of(g * GROUP * VROWS + j * VROWS, 16), VROWS)


MESH = pl.DeviceIdType.MESH
ROUTES = ((-1, 0), (1, 0), (0, -1), (1, -1))


class Exchange:
    def __init__(self, way, send_sem, recv_sem):
        self.way, self.sems, self.copies = way, (send_sem, recv_sem), []

    def device(self, steps, sign):
        size = lax.axis_size("tm"), lax.axis_size("rows")
        here = lax.axis_index("tm"), lax.axis_index("rows")
        return tuple((i + sign * d + n) % n for i, d, n in zip(here, steps, size))

    def greet(self):
        for steps in ROUTES:
            pl.semaphore_signal(
                pltpu.get_barrier_semaphore(),
                inc=1,
                device_id=self.device(steps, -self.way),
                device_id_type=MESH,
            )

    def wait_for_others(self):
        pl.semaphore_wait(pltpu.get_barrier_semaphore(), len(ROUTES))

    def send(self, route, source, target):
        i = len(self.copies)
        copy = pltpu.make_async_remote_copy(
            src_ref=source,
            dst_ref=target,
            send_sem=self.sems[0].at[i],
            recv_sem=self.sems[1].at[i],
            device_id=self.device(ROUTES[route], self.way),
            device_id_type=MESH,
        )
        copy.start()
        self.copies.append(copy)

    def wait(self):
        for copy in self.copies:
            copy.wait()


def pieces_of(whole, w, pieces):
    own, ahead, behind, above, corner = pieces
    if w == 0:
        above[...] = whole[0:3, :, 0:4].astype(BF16)
        corner[...] = whole[0:3, :, 4:8].astype(BF16)
        ahead[0:4] = whole[3:7, :, 0:4].astype(BF16)
        own[0:4] = whole[3:7, :, 4:8].astype(BF16)
    else:
        ahead[4:7] = whole[0:3, :, 0:4].astype(BF16)
        own[4:7] = whole[0:3, :, 4:8].astype(BF16)
        behind[...] = whole[3:7, :, 4:8].astype(BF16)
        own[7:11] = whole[3:7, :, 0:4].astype(BF16)


def joined(low, high):
    return jnp.concatenate([low.astype(F32), high.astype(F32)], axis=2)


def forward_kernel(
    x_ref, cot_ref, gain_ref, bias_ref, wqkv_ref, wout_ref, mixt_ref, stat_ref, *refs,
):
    y_own, c_own, y_there, c_there, y_here, c_here = (
        refs[0], refs[1], refs[2:6], refs[6:10], refs[10:14], refs[14:18]
    )
    qbd, k, vt, send_sem, recv_sem = refs[18:]
    exchange = Exchange(1, send_sem, recv_sem)
    exchange.greet()
    for w in range(2):
        pieces_of(cot_ref[7 * w : 7 * w + 7].astype(F32), w, (c_own, *c_here))
    exchange.wait_for_others()
    for route in range(4):
        exchange.send(route, c_here[route], c_there[route])
    qbd[...] = jnp.zeros_like(qbd)
    for w in range(2):
        rows = slice(7 * w, 7 * w + 7)
        x = tiles(x_ref[rows])
        xhat, _ = standardized(x)
        normed = (xhat * gain_ref[...] + bias_ref[...]).astype(BF16)
        put_diagonal(qbd, (mm(normed, wqkv_ref[:, 0:C]) * QSCALE).astype(BF16).T, 512)
        k[...] = mm(normed, wqkv_ref[:, C : 2 * C]).astype(BF16)
        put_values(vt, mm(normed, wqkv_ref[:, 2 * C :]).astype(BF16).T, 0)

        def group(g, carry):
            kg = k[:, channels_of(g)]
            for j in range(GROUP):
                lanes = slice(512 * j, 512 * (j + 1))
                scores = mm(kg, qbd[channels_of(g), lanes])
                top = jnp.max(scores, axis=0, keepdims=True)
                e = jnp.exp2(scores - top).astype(BF16)
                mixed = mm(vt[head_values(g, j), :], e)
                sums = mixed[HD : HD + 1]
                stat_ref[w, g, :, lanes] = top + jnp.log2(sums)
                mixt_ref[w, head_channels(g, j), :] = (mixed[:HD] * (1.0 / sums)).astype(BF16)
            return carry

        lax.fori_loop(0, HEADS // GROUP, group, 0)
        y = x + mm_tn(mixt_ref[w, :, 0:TOK], wout_ref[...])
        pieces_of(y.reshape(7, 7, 8, C), w, (y_own, *y_here))
        if w == 0:
            exchange.send(2, y_here[2], y_there[2])
            exchange.send(3, y_here[3], y_there[3])
            exchange.send(0, y_here[0].at[0:4], y_there[0].at[0:4])
        else:
            exchange.send(0, y_here[0].at[4:7], y_there[0].at[4:7])
            exchange.send(1, y_here[1], y_there[1])
    exchange.wait()


def write_part(g, block, part):
    turn = g % 3

    def layer(z, carry):
        for xy in range(16):
            x, y = xy // 4, xy % 4
            rows = pl.ds(pl.multiple_of((z * 16 + x // 2 * 8 + y * 2 + x % 2) * 8, 8), 8)
            values = block[rows, :]
            first = jnp.where(turn == 0, x, jnp.where(turn == 1, y, z))
            second = jnp.where(turn == 0, y, jnp.where(turn == 1, z, x))
            third = jnp.where(turn == 0, z, jnp.where(turn == 1, x, y))
            part[0, first, second, third] = values[0:4].astype(BF16)
            part[1, first, second, third] = values[4:8].astype(BF16)
        return carry

    lax.fori_loop(0, 4, layer, 0)


def group_gradients(scale, g, normed_t, dproj, mixt, cot_b, block, part):
    block[:, 0:384] = mm(normed_t[...], dproj[:, columns_of(g)]) * scale
    block[:, 384:512] = mm(mixt[...], cot_b[:, channels_of(g)]) * scale
    write_part(g, block, part)


def columns_of(g):
    return pl.ds(pl.multiple_of(g * 384, 128), 384)


def sort_columns(sorted_ref, wqkv_ref):
    for g in range(HEADS // GROUP):
        for i in range(3):
            sorted_ref[:, 384 * g + 128 * i : 384 * g + 128 * (i + 1)] = wqkv_ref[
                :, C * i + 128 * g : C * i + 128 * (g + 1)
            ]


def norm_backward(dnormed, xhat, rstd, gain):
    d = dnormed.astype(BF16).astype(F32) * gain
    return rstd * (
        d
        - jnp.mean(d, axis=-1, keepdims=True)
        - xhat * jnp.mean(d * xhat, axis=-1, keepdims=True)
    )


def coordinates():
    tm, rows = lax.axis_index("tm"), lax.axis_index("rows")
    return {
        "x": tm // 4 % 2 * 2 + rows // 2,
        "y": tm % 4,
        "z": tm // 8,
        "core": rows % 2,
    }


def device_at(place):
    tm = place["z"] * 8 + place["x"] // 2 * 4 + place["y"]
    return (tm, place["x"] % 2 * 2 + place["core"])


def beside(here, axis, steps):
    return device_at({**here, axis: (here[axis] + steps) % (2 if axis == "core" else 4)})


ORDERS = ("xyz", "yzx", "zxy")


class Reduction:
    def __init__(self, order, here, partners, part, local_sem, buffers, sems):
        self.order, self.here, self.partners, self.part = order, here, partners, part
        self.held, self.other, *self.slots = buffers
        self.local_sem, self.sems = local_sem, sems

    def remote(self, number, source, target, partner):
        return pltpu.make_async_remote_copy(
            src_ref=source,
            dst_ref=target,
            send_sem=self.sems[0].at[number],
            recv_sem=self.sems[1].at[number],
            device_id=partner,
            device_id_type=MESH,
        )

    def local_copy(self):
        return pltpu.make_async_copy(self.part.at[self.here["core"]], self.held, self.local_sem)

    def core_copy(self):
        return self.remote(0, self.part.at[1 - self.here["core"]], self.other, self.partners["core", 1])

    def source(self, step):
        return self.held if step == 0 else self.slots[step - 1].at[3]

    def axis_copies(self, step):
        axis = self.order[step]
        return [
            self.remote(
                3 * step + away,
                self.source(step).at[(self.here[axis] + away) % 4],
                self.slots[step].at[away - 1],
                self.partners[axis, away],
            )
            for away in (1, 2, 3)
        ]

    def start(self):
        self.core_copy().start()

    def advance(self, stage, out=None):
        if stage == 0:
            self.core_copy().wait_recv()
            if self.local_sem is not None:
                self.local_copy().wait()
                own = self.held
            else:
                own = self.part.at[self.here["core"]]
            for i in range(4):
                self.held[i] = (own[i].astype(F32) + self.other[i].astype(F32)).astype(BF16)
        else:
            for copy in self.axis_copies(stage - 1):
                copy.wait_recv()
            total = self.source(stage - 1)[self.here[self.order[stage - 1]]].astype(F32)
            for slot in range(3):
                total = total + self.slots[stage - 1][slot].astype(F32)
            if stage == 3:
                out(total)
                return
            self.slots[stage - 1][3] = total.astype(BF16)
        for copy in self.axis_copies(stage):
            copy.start()

    def finish(self):
        self.core_copy().wait_send()
        for step in range(3):
            for copy in self.axis_copies(step):
                copy.wait_send()


JOBS = HEADS // GROUP


def backward_first_kernel(
    scale,
    x_ref, gain_ref, bias_ref, wqkv_ref, wout_ref, mixt_ref, stat_ref,
    own, ahead, behind, above, corner, parts_second,
    grad_ref, gqkv1, gout1, gqkv2, gout2,
    normed_t, dproj, cot_b, mixt_all, wsorted, block, parts_first,
    qbd, k, kt, v, qn, don, dobd, p_s, ds_s, dqt, do_rows, q_rows, cot_s, xhat_s, rstd_s,
    held, other, slots_a, slots_b, slots_c, local_sem, send_sem, recv_sem,
):
    here = coordinates()
    partners = {("core", 1): beside(here, "core", 1)}
    for axis in "xyz":
        for away in (1, 2, 3):
            partners[axis, away] = beside(here, axis, away)
    barrier = pltpu.get_barrier_semaphore()
    for partner in partners.values():
        pl.semaphore_signal(barrier, inc=1, device_id=partner, device_id_type=MESH)

    def job(i):
        of_first = i < JOBS
        g = i % JOBS
        return Reduction(
            ORDERS[g % 3],
            here,
            partners,
            parts_first.at[g] if of_first else parts_second.at[g],
            None if of_first else local_sem.at[g],
            [ref.at[i] for ref in (held, other, slots_a, slots_b, slots_c)],
            (send_sem.at[i], recv_sem.at[i]),
        )

    def result(i):
        gqkv, gout = (gqkv1, gout1) if i < JOBS else (gqkv2, gout2)
        g = i % JOBS

        def out(total):
            for part in range(3):
                at = C * part + 128 * g
                gqkv[:, at : at + 128] = total[:, 128 * part : 128 * (part + 1)]
            gout[:, 128 * g : 128 * (g + 1)] = total[:, 384:512]

        return out

    first, second = [job(i) for i in range(JOBS)], [job(JOBS + i) for i in range(JOBS)]
    for reduction in second:
        reduction.local_copy().start()
    for ref in (qbd, dobd, do_rows, q_rows, normed_t, dproj, cot_b):
        ref[...] = jnp.zeros_like(ref)
    sort_columns(wsorted, wqkv_ref)
    for w in range(2):
        xhat, rstd = standardized(tiles(x_ref[7 * w : 7 * w + 7]))
        xhat_s[w] = xhat
        rstd_s[w] = rstd
        normed = (xhat * gain_ref[...] + bias_ref[...]).astype(BF16)
        normed_t[:, 512 * w : 512 * w + TOK] = normed.T
        queries = (mm(normed, wqkv_ref[:, 0:C]) * QSCALE).astype(BF16)
        qn[w] = queries
        put_diagonal(qbd.at[w], queries.T, 512)
        keys = mm(normed, wqkv_ref[:, C : 2 * C]).astype(BF16)
        k[w] = keys
        kt[w] = keys.T
        v[w] = mm(normed, wqkv_ref[:, 2 * C :]).astype(BF16)
        if w == 0:
            pieces = [joined(above[...], corner[...]), joined(ahead[0:4], own[0:4])]
        else:
            pieces = [joined(ahead[4:7], own[4:7]), joined(own[7:11], behind[...])]
        cot = jnp.concatenate([piece.reshape(-1, C) for piece in pieces], axis=0)
        cot_s[w] = cot
        cot_h = cot.astype(BF16)
        cot_b[512 * w : 512 * w + TOK] = cot_h
        dmixed = mm_nt(cot_h, wout_ref[...]).astype(BF16)
        don[w] = dmixed
        put_diagonal(dobd.at[w], dmixed.T, 512)
        mixt_all[:, 512 * w : 512 * (w + 1)] = mixt_ref[w]
        if w == 0:
            pl.semaphore_wait(barrier, len(partners))
            for reduction in second:
                reduction.start()

    def group(g, carry):
        for w in range(2):
            kg = k[w, :, channels_of(g)]
            vg = v[w, :, channels_of(g)]
            qg = qn[w, :, channels_of(g)]
            dog = don[w, :, channels_of(g)]
            for j in range(GROUP):
                lanes = slice(512 * j, 512 * (j + 1))
                do_rows[512 * j : 512 * j + TOK] = own_lanes(j, dog)
                q_rows[512 * j : 512 * j + TOK] = own_lanes(j, qg)
                scores = mm(kg, qbd[w, channels_of(g), lanes])
                p = jnp.exp2(scores - stat_ref[w, g, :, lanes]).astype(BF16)
                p_s[:, lanes] = p
                dsum = jnp.sum(
                    mixt_ref[w, head_channels(g, j), :].astype(F32)
                    * dobd[w, head_channels(g, j), lanes].astype(F32),
                    axis=0, keepdims=True,
                )
                dp = mm(vg, dobd[w, channels_of(g), lanes]) - dsum
                ds = (p.astype(F32) * dp).astype(BF16)
                ds_s[:, lanes] = ds
                dq = mm(kt[w, head_channels(g, j), :], ds)
                dqt[HD * j : HD * (j + 1), :] = (dq[:, 0:TOK] * HD ** (-0.5)).astype(BF16)
            dk = mm(ds_s[...], q_rows[...]) * LN2
            dv = mm(p_s[...], do_rows[...])
            dproj[512 * w : 512 * w + TOK, columns_of(g)] = jnp.concatenate(
                [dqt[...].T, dk.astype(BF16), dv.astype(BF16)], axis=1
            )
        group_gradients(scale, g, normed_t, dproj, mixt_all, cot_b, block, parts_first.at[g])
        for now in range(JOBS):

            @pl.when(g == now)
            def _():
                first[now].start()
                for i in range(JOBS):
                    second[i].advance(now, result(JOBS + i))
                for i in range(now):
                    first[i].advance(now - 1 - i)

        return carry

    lax.fori_loop(0, JOBS, group, 0)
    for w in range(2):
        dnormed = mm_nt(dproj[512 * w : 512 * w + TOK], wsorted[...])
        total = cot_s[w] + norm_backward(dnormed, xhat_s[w], rstd_s[w], gain_ref[...])
        grad_ref[7 * w : 7 * w + 7] = total.reshape(7, 7, 8, C).astype(BF16)
    for now in range(JOBS, 2 * JOBS):
        for i in range(JOBS):
            if 0 <= now - 1 - i <= 3:
                first[i].advance(now - 1 - i, result(i))
    for reduction in first + second:
        reduction.finish()


def second_kernel(
    scale,
    y_own, y_ahead, y_behind, y_above, y_corner, c_own, c_ahead, c_behind, c_above, c_corner,
    gain_ref, bias_ref, wqkv_ref, wout_ref,
    own, ahead_there, behind_there, above_there, corner_there, parts,
    normed_t, dproj, cot_b, mixt, wsorted, block, qbd, k, kt, v, vt, qn, dot_s, dobd, dopt, dqt,
    e_a, e_b, ds_a, ds_b, do_rows, q_rows, pen, cot_s, xhat_s,
    ahead, behind, above, corner, send_sem, recv_sem,
):
    exchange = Exchange(-1, send_sem, recv_sem)
    exchange.greet()
    e_s, ds_s = (e_a, e_b), (ds_a, ds_b)
    for ref in (qbd, dobd, do_rows, q_rows, normed_t, dproj, cot_b, mixt):
        ref[...] = jnp.zeros_like(ref)
    sort_columns(wsorted, wqkv_ref)
    for w in range(2):
        base = 512 * w
        last_frames = lax.axis_index("tm") == (lax.axis_size("tm") - 1 if w == 0 else 0)
        last_rows = (lax.axis_index("rows") == lax.axis_size("rows") - 1) if w == 1 else False

        def region_of(token, segment):
            columns = 4 if segment == 0 else 3
            late = jnp.where(last_frames & (token % 8 < 4), 1, 0)
            below = jnp.where(last_rows & (token // 8 // columns >= 4), 2, 0)
            return late + below

        def gather(into, own, ahead, behind, above, corner):
            def put(rho, count, whole):
                into[32 * rho : 32 * (rho + count)] = whole[:, 3:7].reshape(-1, C)
                into[224 + 24 * rho : 224 + 24 * (rho + count)] = whole[:, 0:3].reshape(-1, C)

            if w == 0:
                put(0, 7, joined(ahead[...], own[0:7]))
            else:
                put(0, 4, joined(own[7:11], behind[...]))
                put(4, 3, joined(above[...], corner[...]))

        gather(xhat_s, y_own, y_ahead, y_behind, y_above, y_corner)
        gather(cot_s, c_own, c_ahead, c_behind, c_above, c_corner)
        xhat, rstd = standardized(xhat_s[...])
        xhat_s[...] = xhat
        normed = (xhat * gain_ref[...] + bias_ref[...]).astype(BF16)
        normed_t[:, base : base + TOK] = normed.T
        queries = (mm(normed, wqkv_ref[:, 0:C]) * QSCALE).astype(BF16)
        qn[...] = queries
        keys = mm(normed, wqkv_ref[:, C : 2 * C]).astype(BF16)
        k[...] = keys
        values_f = mm(normed, wqkv_ref[:, 2 * C :])
        values = values_f.astype(BF16)
        v[...] = values
        cot_h = cot_s[...].astype(BF16)
        dmixed = mm_nt(cot_h, wout_ref[...]).astype(BF16)
        for s, (start, stop) in enumerate(SPLIT):
            count = stop - start
            cot_b[512 * w + 256 * s : 512 * w + 256 * s + count] = cot_h[start:stop]
            put_diagonal(qbd, queries[start:stop].T, 256, 1024 * s)
            kt[:, 256 * s : 256 * s + count] = keys[start:stop].T
            dot_s[:, 256 * s : 256 * s + count] = dmixed[start:stop].T
            turned = values[start:stop].T
            put_values(vt, turned, 256 * s)
            total = jnp.sum(turned.astype(F32), axis=1, keepdims=True)
            other = 1 - s
            lane = 256 * other + SPLIT[other][1] - SPLIT[other][0]
            first = lax.broadcasted_iota(jnp.int32, (C, VIRTUAL), 1) == 0
            total = jnp.where(first, total, 0.0).astype(BF16)
            number = jnp.where(first[0 : VROWS - HD], float(count), 0.0).astype(BF16)
            for head in range(HEADS):
                at = VROWS * head
                vt[at : at + HD, lane : lane + VIRTUAL] = total[HD * head : HD * (head + 1)]
                vt[at + HD : at + VROWS, lane : lane + VIRTUAL] = number
            shape = (count, 256)
            key = region_of(lax.broadcasted_iota(jnp.int32, shape, 0), s)
            query = region_of(lax.broadcasted_iota(jnp.int32, shape, 1), s)
            pen[start:stop] = jnp.where(key == query, 0.0, 1.0)

        def group(g, carry):
            virtual_dv = []
            grads = []
            for s, (start, stop) in enumerate(SPLIT):
                count = stop - start
                kg = k[start:stop, channels_of(g)]
                apart = pen[start:stop] > 0.5
                sums_of = []
                for j in range(GROUP):
                    lanes = slice(256 * j, 256 * (j + 1))
                    scores = mm(kg, qbd[channels_of(g), 1024 * s + 256 * j : 1024 * s + 256 * (j + 1)])
                    scores = jnp.where(apart, MASKED, scores)
                    top = jnp.maximum(jnp.max(scores, axis=0, keepdims=True), MASKED)
                    e_s[s][0:count, lanes] = jnp.exp2(scores - top).astype(BF16)
                    first = lax.broadcasted_iota(jnp.int32, (VIRTUAL, 256), 0) == 0
                    e_s[s][count : count + VIRTUAL, lanes] = jnp.where(
                        first, jnp.exp2(MASKED - top), 0.0
                    ).astype(BF16)
                for j in range(GROUP):
                    lanes = slice(256 * j, 256 * (j + 1))
                    tokens = slice(256 * s, 256 * (s + 1))
                    mixed = mm(
                        vt[head_values(g, j), 256 * s : 256 * s + count + VIRTUAL], e_s[s][:, lanes]
                    )
                    inv = 1.0 / mixed[HD : HD + 1]
                    mixed = mixed[:HD] * inv
                    mixt[head_channels(g, j), 512 * w + 256 * s : 512 * w + 256 * s + count] = mixed[
                        :, 0:count
                    ].astype(BF16)
                    do = dot_s[head_channels(g, j), tokens].astype(F32) * inv
                    inside = lax.broadcasted_iota(jnp.int32, do.shape, 1) < count
                    do = jnp.where(inside, do, 0.0).astype(BF16)
                    sums_of.append(jnp.sum(mixed * do.astype(F32), axis=0, keepdims=True))
                    dopt[HD * j : HD * (j + 1), tokens] = do
                    dobd[HD * j : HD * (j + 1), 1024 * s + 256 * j : 1024 * s + 256 * (j + 1)] = do
                turned = dopt[:, 256 * s : 256 * (s + 1)].T
                qg = qn[start:stop, channels_of(g)]
                for j in range(GROUP):
                    lanes = slice(256 * j, 256 * (j + 1))
                    at = 1024 * s + 256 * j
                    do_rows[at : at + 256] = own_lanes(j, turned)
                    q_rows[at : at + count] = own_lanes(j, qg)
                    dp = mm(v[start:stop, channels_of(g)], dobd[:, at : at + 256]) - sums_of[j]
                    ds = e_s[s][0:count, lanes].astype(F32) * jnp.where(apart, 0.0, dp)
                    ds = ds.astype(BF16)
                    ds_s[s][:, lanes] = ds
                    dq = mm(kt[head_channels(g, j), 256 * s : 256 * s + count], ds)
                    dqt[HD * j : HD * (j + 1), 256 * s : 256 * (s + 1)] = (dq * HD ** (-0.5)).astype(BF16)
                block = slice(1024 * s, 1024 * (s + 1))
                dv = mm(e_s[s][...], do_rows[block])
                dk = mm(ds_s[s][...], q_rows[block]) * LN2
                virtual_dv.append(dv[count : count + 1])
                grads.append((dk, dv[0:count]))
            for s, (start, stop) in enumerate(SPLIT):
                rows = slice(base + start, base + stop)
                dk, dv = grads[s]
                dproj[rows, columns_of(g)] = jnp.concatenate(
                    [
                        dqt[:, 256 * s : 256 * s + stop - start].T,
                        dk.astype(BF16),
                        (dv + virtual_dv[1 - s]).astype(BF16),
                    ],
                    axis=1,
                )
            return carry

        lax.fori_loop(0, HEADS // GROUP, group, 0)
        dnormed = mm_nt(dproj[base : base + TOK], wsorted[...])
        total = cot_s[...] + norm_backward(dnormed, xhat_s[...], rstd, gain_ref[...])
        whole = jnp.concatenate(
            [total[224:392].reshape(7, 3, 8, C), total[0:224].reshape(7, 4, 8, C)], axis=1
        )
        low, high = whole[:, :, 0:4].astype(BF16), whole[:, :, 4:8].astype(BF16)
        if w == 0:
            ahead[...] = low
            own[0:7] = high
            exchange.wait_for_others()
            exchange.send(0, ahead, ahead_there)
        else:
            own[7:11] = low[0:4]
            behind[...] = high[0:4]
            above[...] = low[4:7]
            corner[...] = high[4:7]
            exchange.send(1, behind, behind_there)
            exchange.send(2, above, above_there)
            exchange.send(3, corner, corner_there)

    def gradients(g, carry):
        group_gradients(scale, g, normed_t, dproj, mixt, cot_b, block, parts.at[g])
        return carry

    lax.fori_loop(0, JOBS, gradients, 0)
    exchange.wait()


def piece_shapes():
    return [(rows, 7, 4, C) for rows in (11, 7, 4, 3, 3)]


PARTS = [(JOBS, 2, 4, 4, 4, 4, 512)]
SAVED = [
    jax.ShapeDtypeStruct((2, C, 512), BF16),
    jax.ShapeDtypeStruct((2, HEADS // GROUP, 1, 2048), F32),
]
TOKENS = (14, 7, 8, C)
IN_VMEM = pl.BlockSpec(memory_space=pltpu.VMEM)


ANYWHERE = pl.BlockSpec(memory_space=pl.ANY)


def call(
    kernel, name, args, out_shape, scratch, there=(), far=(), semaphores=(), collective_id=None
):
    return pl.pallas_call(
        kernel,
        in_specs=[ANYWHERE if i in far else IN_VMEM for i in range(len(args))],
        out_specs=[ANYWHERE if i in there else IN_VMEM for i in range(len(out_shape))],
        out_shape=out_shape,
        scratch_shapes=[pltpu.VMEM(shape, dtype) for shape, dtype in scratch]
        + [pltpu.SemaphoreType.DMA(shape) for shape in semaphores],
        compiler_params=pltpu.CompilerParams(
            vmem_limit_bytes=VMEM_LIMIT,
            has_side_effects=collective_id is not None,
            collective_id=collective_id,
        ),
        name=name,
    )(*args)


def halves(shapes):
    return [jax.ShapeDtypeStruct(shape, BF16) for shape in shapes]


def forward_first(x, cot, weights):
    pieces = piece_shapes()
    outs = call(
        forward_kernel,
        "forward_first",
        (x, cot, *weights),
        SAVED + halves(pieces[:1] * 2 + pieces[1:] * 2),
        [(shape, BF16) for shape in pieces[1:] * 2]
        + [((C, 2048), BF16), ((TOK, C), BF16), ((HEADS * VROWS, TOK), BF16)],
        there=range(4, 12),
        semaphores=[(9,)] * 2,
        collective_id=1,
    )
    return outs[:2], [outs[2], *outs[4:8]], [outs[3], *outs[8:12]]


GRADIENT_SCRATCH = [
    ((C, 1024), BF16), ((1024, 3 * C), BF16), ((1024, C), BF16), ((C, 1024), BF16), ((C, 3 * C), BF16), ((C, C), F32),
]


def backward_first(scale, x, weights, saved, pieces, parts):
    both = 2 * JOBS
    args = (x, *weights, *saved, *pieces, parts)
    return call(
        functools.partial(backward_first_kernel, scale),
        "backward_first",
        args,
        halves([TOKENS]) + [jax.ShapeDtypeStruct((4, width), F32) for width in (3 * C, C)] * 2,
        GRADIENT_SCRATCH
        + [(PARTS[0], BF16)]
        + [
            ((2, C, 2048), BF16), ((2, TOK, C), BF16), ((2, C, TOK), BF16), ((2, TOK, C), BF16),
            ((2, TOK, C), BF16), ((2, TOK, C), BF16), ((2, C, 2048), BF16),
            ((TOK, 2048), BF16), ((TOK, 2048), BF16), ((128, TOK), BF16),
            ((2048, 128), BF16), ((2048, 128), BF16),
            ((2, TOK, C), F32), ((2, TOK, C), F32), ((2, TOK, 1), F32),
        ]
        + [((both, 4, 4, 4, 4, 512), BF16)] * 3
        + [((both, 4, 4, 4, 512), BF16), ((both, 4, 4, 512), BF16)],
        far=(len(args) - 1,),
        semaphores=[(JOBS,), (both, 10), (both, 10)],
        collective_id=3,
    )


def hand_on_kernel(*refs):
    grad, *sums = refs[:5]
    grad_out, *sums_out = refs[5:10]
    copy = pltpu.make_async_copy(grad, grad_out, refs[10])
    copy.start()
    for source, target in zip(sums, sums_out):
        target[...] = source[...]
    copy.wait()


def handed_on(outs):
    return pl.pallas_call(
        hand_on_kernel,
        in_specs=[ANYWHERE] + [IN_VMEM] * 4,
        out_specs=[ANYWHERE] + [IN_VMEM] * 4,
        out_shape=[jax.ShapeDtypeStruct(out.shape, out.dtype) for out in outs],
        scratch_shapes=[pltpu.SemaphoreType.DMA],
        compiler_params=pltpu.CompilerParams(vmem_limit_bytes=VMEM_LIMIT),
        name="hand_on",
    )(*outs)


def second_block(scale, y_pieces, c_pieces, weights):
    return call(
        functools.partial(second_kernel, scale),
        "second_block",
        (*y_pieces, *c_pieces, *weights),
        halves(piece_shapes() + PARTS),
        GRADIENT_SCRATCH
        + [
            ((C, 2048), BF16), ((TOK, C), BF16), ((C, 512), BF16), ((TOK, C), BF16),
            ((HEADS * VROWS, 512), BF16), ((TOK, C), BF16), ((C, 512), BF16),
            ((128, 2048), BF16), ((128, 512), BF16), ((128, 512), BF16),
            ((224 + VIRTUAL, 1024), BF16), ((168 + VIRTUAL, 1024), BF16),
            ((224, 1024), BF16), ((168, 1024), BF16),
            ((2048, 128), BF16), ((2048, 128), BF16),
            ((TOK, 256), F32), ((TOK, C), F32), ((TOK, C), F32),
        ]
        + [(shape, BF16) for shape in piece_shapes()[1:]],
        there=range(1, 5),
        semaphores=[(4,)] * 2,
        collective_id=2,
    )


def per_device(
    video_clip, cotangent,
    gain_first, bias_first, qkv_first, out_first,
    gain_second, bias_second, qkv_second, out_second,
):
    frames, rows_here, columns, channels = video_clip.shape
    devices = lax.axis_size("tm") * lax.axis_size("rows")
    scale = 1.0 / math.sqrt(frames * rows_here * columns * devices)
    x = video_clip.transpose(1, 2, 0, 3)
    cot = cotangent.transpose(1, 2, 0, 3)
    first = (gain_first.reshape(1, C), bias_first.reshape(1, C), qkv_first, out_first)
    second = (gain_second.reshape(1, C), bias_second.reshape(1, C), qkv_second, out_second)
    saved, y_pieces, c_pieces = forward_first(x, cot, first)
    *d_pieces, parts = second_block(scale, y_pieces, c_pieces, second)
    grad, *sums = handed_on(backward_first(scale, x, first, saved, d_pieces, parts))
    return (grad.transpose(2, 0, 1, 3), *sums)


def solution(mesh):
    clip = P("tm", "rows", None, None)
    scattered = P(("tm", "rows"), None)
    return jax.shard_map(
        per_device,
        mesh=mesh,
        in_specs=(clip, clip) + (P(),) * 8,
        out_specs=(clip,) + (scattered,) * 4,
        check_vma=False,
    )
```

```python
import functools
import math

import jax
import jax.numpy as jnp
from jax import lax
from jax.experimental import pallas as pl
from jax.experimental.pallas import tpu as pltpu
from jax.sharding import PartitionSpec as P

F32, BF16 = jnp.float32, jnp.bfloat16
C, HEADS, HD = 512, 16, 32
TOK = 392
GROUP = 4
VROWS = 48
LOG2E = math.log2(math.e)
QSCALE = HD ** (-0.5) * LOG2E
MASKED = -1000000000.0 * LOG2E
LN2 = math.log(2.0)
SPLIT = ((0, 224), (224, 392))
VIRTUAL = 16
ROWS = 400
VMEM_LIMIT = 56 * 1024 * 1024


def mm(a, b):
    return lax.dot_general(a, b, (((1,), (0,)), ((), ())), preferred_element_type=F32)


def mm_nt(a, b):
    return lax.dot_general(a, b, (((1,), (1,)), ((), ())), preferred_element_type=F32)


def mm_tn(a, b):
    return lax.dot_general(a, b, (((0,), (0,)), ((), ())), preferred_element_type=F32)


def standardized(values):
    center = values - jnp.mean(values, axis=-1, keepdims=True)
    rstd = lax.rsqrt(jnp.mean(center * center, axis=-1, keepdims=True) + 1e-05)
    return center * rstd, rstd


def tiles(block):
    return block.astype(F32).reshape(-1, C)


def own_lanes(j, block):
    lane = lax.broadcasted_iota(jnp.int32, block.shape, 1) // HD
    return jnp.where(lane == j, block, jnp.zeros_like(block))


def put_diagonal(ref, turned, pitch, column=0):
    for head in range(HEADS):
        at = pitch * (head % GROUP) + column
        ref[HD * head : HD * (head + 1), at : at + turned.shape[1]] = turned[HD * head : HD * (head + 1)]


def put_values(vt, turned, lane):
    count = turned.shape[1]
    for head in range(HEADS):
        vt[VROWS * head : VROWS * head + HD, lane : lane + count] = turned[HD * head : HD * (head + 1)]
        vt[VROWS * head + HD : VROWS * (head + 1), lane : lane + count] = jnp.ones(
            (VROWS - HD, count), BF16
        )


def channels_of(g, first=0):
    return pl.ds(pl.multiple_of(g * 128 + first, 128), 128)


def head_channels(g, j):
    return pl.ds(pl.multiple_of(g * 128 + j * HD, HD), HD)


def head_values(g, j):
    return pl.ds(pl.multiple_of(g * GROUP * VROWS + j * VROWS, 16), VROWS)


MESH = pl.DeviceIdType.MESH
ROUTES = ((-1, 0), (1, 0), (0, -1), (1, -1))


class Exchange:
    def __init__(self, way, send_sem, recv_sem):
        self.way, self.sems, self.copies = way, (send_sem, recv_sem), []

    def device(self, steps, sign):
        size = lax.axis_size("tm"), lax.axis_size("rows")
        here = lax.axis_index("tm"), lax.axis_index("rows")
        return tuple((i + sign * d + n) % n for i, d, n in zip(here, steps, size))

    def greet(self, ways):
        self.ways = ways
        for way in ways:
            for steps in ROUTES:
                pl.semaphore_signal(
                    pltpu.get_barrier_semaphore(),
                    inc=1,
                    device_id=self.device(steps, -way),
                    device_id_type=MESH,
                )

    def wait_for_others(self):
        pl.semaphore_wait(pltpu.get_barrier_semaphore(), len(self.ways) * len(ROUTES))

    def send(self, route, source, target, way=None):
        i = len(self.copies)
        copy = pltpu.make_async_remote_copy(
            src_ref=source,
            dst_ref=target,
            send_sem=self.sems[0].at[i],
            recv_sem=self.sems[1].at[i],
            device_id=self.device(ROUTES[route], way or self.way),
            device_id_type=MESH,
        )
        copy.start()
        self.copies.append(copy)

    def wait_for(self, numbers):
        for i in numbers:
            self.copies[i].wait_recv()

    def wait(self, arrived=()):
        for i, copy in enumerate(self.copies):
            copy.wait_send()
            if i not in arrived:
                copy.wait_recv()


def pieces_of(whole, w, pieces):
    own, ahead, behind, above, corner = pieces
    if w == 0:
        above[...] = whole[0:3, :, 0:4].astype(BF16)
        corner[...] = whole[0:3, :, 4:8].astype(BF16)
        ahead[0:4] = whole[3:7, :, 0:4].astype(BF16)
        own[0:4] = whole[3:7, :, 4:8].astype(BF16)
    else:
        ahead[4:7] = whole[0:3, :, 0:4].astype(BF16)
        own[4:7] = whole[0:3, :, 4:8].astype(BF16)
        behind[...] = whole[3:7, :, 4:8].astype(BF16)
        own[7:11] = whole[3:7, :, 0:4].astype(BF16)


def joined(low, high):
    return jnp.concatenate([low.astype(F32), high.astype(F32)], axis=2)


def forward_kernel(
    x_ref, cot_ref, gain_ref, bias_ref, wqkv_ref, wout_ref, mixt_ref, stat_ref, *refs,
):
    y_own, y_there, c_own, c_ahead_there, c_later, y_here = (
        refs[0], refs[1:5], refs[5], refs[6], refs[7:10], refs[10:14]
    )
    c_ahead, qbd, k, vt, send_sem, recv_sem = refs[14:]
    exchange = Exchange(1, send_sem, recv_sem)
    exchange.greet((1,))
    for w in range(2):
        pieces_of(cot_ref[7 * w : 7 * w + 7].astype(F32), w, (c_own, c_ahead, *c_later))
    exchange.wait_for_others()
    exchange.send(0, c_ahead, c_ahead_there)
    qbd[...] = jnp.zeros_like(qbd)
    for w in range(2):
        rows = slice(7 * w, 7 * w + 7)
        x = tiles(x_ref[rows])
        xhat, _ = standardized(x)
        normed = (xhat * gain_ref[...] + bias_ref[...]).astype(BF16)
        put_diagonal(qbd, (mm(normed, wqkv_ref[:, 0:C]) * QSCALE).astype(BF16).T, 512)
        k[...] = mm(normed, wqkv_ref[:, C : 2 * C]).astype(BF16)
        put_values(vt, mm(normed, wqkv_ref[:, 2 * C :]).astype(BF16).T, 0)

        def group(g, carry):
            kg = k[:, channels_of(g)]
            for j in range(GROUP):
                lanes = slice(512 * j, 512 * (j + 1))
                scores = mm(kg, qbd[channels_of(g), lanes])
                top = jnp.max(scores, axis=0, keepdims=True)
                e = jnp.exp2(scores - top).astype(BF16)
                mixed = mm(vt[head_values(g, j), :], e)
                sums = mixed[HD : HD + 1]
                stat_ref[w, g, :, lanes] = top + jnp.log2(sums)
                mixt_ref[w, head_channels(g, j), :] = (mixed[:HD] * (1.0 / sums)).astype(BF16)
            return carry

        lax.fori_loop(0, HEADS // GROUP, group, 0)
        y = x + mm_tn(mixt_ref[w, :, 0:TOK], wout_ref[...])
        pieces_of(y.reshape(7, 7, 8, C), w, (y_own, *y_here))
        if w == 0:
            exchange.send(2, y_here[2], y_there[2])
            exchange.send(3, y_here[3], y_there[3])
            exchange.send(0, y_here[0].at[0:4], y_there[0].at[0:4])
        else:
            exchange.send(0, y_here[0].at[4:7], y_there[0].at[4:7])
            exchange.send(1, y_here[1], y_there[1])
    exchange.wait()


def write_part(g, block, part):
    turn = g % 3

    def layer(z, carry):
        for xy in range(16):
            x, y = xy // 4, xy % 4
            rows = pl.ds(pl.multiple_of((z * 16 + x // 2 * 8 + y * 2 + x % 2) * 8, 8), 8)
            values = block[rows, :]
            first = jnp.where(turn == 0, x, jnp.where(turn == 1, y, z))
            second = jnp.where(turn == 0, y, jnp.where(turn == 1, z, x))
            third = jnp.where(turn == 0, z, jnp.where(turn == 1, x, y))
            part[0, first, second, third] = values[0:4].astype(BF16)
            part[1, first, second, third] = values[4:8].astype(BF16)
        return carry

    lax.fori_loop(0, 4, layer, 0)


def group_gradients(scale, g, normed_t, dproj, mixt, cot_b, block, part):
    block[:, 0:384] = mm(normed_t[...], dproj[:, columns_of(g)]) * scale
    block[:, 384:512] = mm(mixt[...], cot_b[:, channels_of(g)]) * scale
    write_part(g, block, part)


def columns_of(g):
    return pl.ds(pl.multiple_of(g * 384, 128), 384)


def sort_columns(sorted_ref, wqkv_ref):
    for g in range(HEADS // GROUP):
        for i in range(3):
            sorted_ref[:, 384 * g + 128 * i : 384 * g + 128 * (i + 1)] = wqkv_ref[
                :, C * i + 128 * g : C * i + 128 * (g + 1)
            ]


def norm_backward(dnormed, xhat, rstd, gain):
    d = dnormed.astype(BF16).astype(F32) * gain
    return rstd * (
        d
        - jnp.mean(d, axis=-1, keepdims=True)
        - xhat * jnp.mean(d * xhat, axis=-1, keepdims=True)
    )


def coordinates():
    tm, rows = lax.axis_index("tm"), lax.axis_index("rows")
    return {
        "x": tm // 4 % 2 * 2 + rows // 2,
        "y": tm % 4,
        "z": tm // 8,
        "core": rows % 2,
    }


def device_at(place):
    tm = place["z"] * 8 + place["x"] // 2 * 4 + place["y"]
    return (tm, place["x"] % 2 * 2 + place["core"])


def beside(here, axis, steps):
    return device_at({**here, axis: (here[axis] + steps) % (2 if axis == "core" else 4)})


ORDERS = ("xyz", "yzx", "zxy")


class Reduction:
    def __init__(self, order, here, partners, part, local_sem, buffers, sems):
        self.order, self.here, self.partners, self.part = order, here, partners, part
        self.held, self.other, *self.slots = buffers
        self.local_sem, self.sems = local_sem, sems

    def remote(self, number, source, target, partner):
        return pltpu.make_async_remote_copy(
            src_ref=source,
            dst_ref=target,
            send_sem=self.sems[0].at[number],
            recv_sem=self.sems[1].at[number],
            device_id=partner,
            device_id_type=MESH,
        )

    def local_copy(self):
        return pltpu.make_async_copy(self.part.at[self.here["core"]], self.held, self.local_sem)

    def core_copy(self):
        return self.remote(0, self.part.at[1 - self.here["core"]], self.other, self.partners["core", 1])

    def source(self, step):
        return self.held if step == 0 else self.slots[step - 1].at[3]

    def axis_copies(self, step):
        axis = self.order[step]
        return [
            self.remote(
                3 * step + away,
                self.source(step).at[(self.here[axis] + away) % 4],
                self.slots[step].at[away - 1],
                self.partners[axis, away],
            )
            for away in (1, 2, 3)
        ]

    def start(self):
        self.core_copy().start()

    def advance(self, stage, out=None):
        if stage == 0:
            self.core_copy().wait_recv()
            if self.local_sem is not None:
                self.local_copy().wait()
                own = self.held
            else:
                own = self.part.at[self.here["core"]]
            for i in range(4):
                self.held[i] = (own[i].astype(F32) + self.other[i].astype(F32)).astype(BF16)
        else:
            for copy in self.axis_copies(stage - 1):
                copy.wait_recv()
            total = self.source(stage - 1)[self.here[self.order[stage - 1]]].astype(F32)
            for slot in range(3):
                total = total + self.slots[stage - 1][slot].astype(F32)
            if stage == 3:
                out(total)
                return
            self.slots[stage - 1][3] = total.astype(BF16)
        for copy in self.axis_copies(stage):
            copy.start()

    def finish(self):
        self.core_copy().wait_send()
        for step in range(3):
            for copy in self.axis_copies(step):
                copy.wait_send()


JOBS = HEADS // GROUP


def backward_first_kernel(
    scale,
    x_ref, gain_ref, bias_ref, wqkv_ref, wout_ref, mixt_ref, stat_ref,
    own, ahead, behind, above, corner, parts_second,
    grad_ref, gqkv1, gout1, gqkv2, gout2,
    normed_t, dproj, cot_b, mixt_all, wsorted, block, parts_first,
    qbd, k, kt, v, qn, don, dobd, p_s, ds_s, dqt, do_rows, q_rows, cot_s, xhat_s, rstd_s,
    held, other, slots_a, slots_b, slots_c, local_sem, send_sem, recv_sem,
):
    here = coordinates()
    partners = {("core", 1): beside(here, "core", 1)}
    for axis in "xyz":
        for away in (1, 2, 3):
            partners[axis, away] = beside(here, axis, away)
    barrier = pltpu.get_barrier_semaphore()
    for partner in partners.values():
        pl.semaphore_signal(barrier, inc=1, device_id=partner, device_id_type=MESH)

    def job(i):
        of_first = i < JOBS
        g = i % JOBS
        return Reduction(
            ORDERS[g % 3],
            here,
            partners,
            parts_first.at[g] if of_first else parts_second.at[g],
            None if of_first else local_sem.at[g],
            [ref.at[i] for ref in (held, other, slots_a, slots_b, slots_c)],
            (send_sem.at[i], recv_sem.at[i]),
        )

    def result(i):
        gqkv, gout = (gqkv1, gout1) if i < JOBS else (gqkv2, gout2)
        g = i % JOBS

        def out(total):
            for part in range(3):
                at = C * part + 128 * g
                gqkv[:, at : at + 128] = total[:, 128 * part : 128 * (part + 1)]
            gout[:, 128 * g : 128 * (g + 1)] = total[:, 384:512]

        return out

    first, second = [job(i) for i in range(JOBS)], [job(JOBS + i) for i in range(JOBS)]
    for reduction in second:
        reduction.local_copy().start()
    for ref in (qbd, dobd, do_rows, q_rows, normed_t, dproj, cot_b):
        ref[...] = jnp.zeros_like(ref)
    sort_columns(wsorted, wqkv_ref)
    for w in range(2):
        xhat, rstd = standardized(tiles(x_ref[7 * w : 7 * w + 7]))
        xhat_s[w] = xhat
        rstd_s[w] = rstd
        normed = (xhat * gain_ref[...] + bias_ref[...]).astype(BF16)
        normed_t[:, 512 * w : 512 * w + TOK] = normed.T
        queries = (mm(normed, wqkv_ref[:, 0:C]) * QSCALE).astype(BF16)
        qn[w] = queries
        put_diagonal(qbd.at[w], queries.T, 512)
        keys = mm(normed, wqkv_ref[:, C : 2 * C]).astype(BF16)
        k[w] = keys
        kt[w] = keys.T
        v[w] = mm(normed, wqkv_ref[:, 2 * C :]).astype(BF16)
        if w == 0:
            pieces = [joined(above[...], corner[...]), joined(ahead[0:4], own[0:4])]
        else:
            pieces = [joined(ahead[4:7], own[4:7]), joined(own[7:11], behind[...])]
        cot = jnp.concatenate([piece.reshape(-1, C) for piece in pieces], axis=0)
        cot_s[w] = cot
        cot_h = cot.astype(BF16)
        cot_b[512 * w : 512 * w + TOK] = cot_h
        dmixed = mm_nt(cot_h, wout_ref[...]).astype(BF16)
        don[w] = dmixed
        put_diagonal(dobd.at[w], dmixed.T, 512)
        mixt_all[:, 512 * w : 512 * (w + 1)] = mixt_ref[w]
        if w == 0:
            pl.semaphore_wait(barrier, len(partners))
            for reduction in second:
                reduction.start()

    def group(g, carry):
        for w in range(2):
            kg = k[w, :, channels_of(g)]
            vg = v[w, :, channels_of(g)]
            qg = qn[w, :, channels_of(g)]
            dog = don[w, :, channels_of(g)]
            for j in range(GROUP):
                lanes = slice(512 * j, 512 * (j + 1))
                do_rows[512 * j : 512 * j + TOK] = own_lanes(j, dog)
                q_rows[512 * j : 512 * j + TOK] = own_lanes(j, qg)
                scores = mm(kg, qbd[w, channels_of(g), lanes])
                p = jnp.exp2(scores - stat_ref[w, g, :, lanes]).astype(BF16)
                p_s[:, lanes] = p
                dsum = jnp.sum(
                    mixt_ref[w, head_channels(g, j), :].astype(F32)
                    * dobd[w, head_channels(g, j), lanes].astype(F32),
                    axis=0, keepdims=True,
                )
                dp = mm(vg, dobd[w, channels_of(g), lanes]) - dsum
                ds = (p.astype(F32) * dp).astype(BF16)
                ds_s[:, lanes] = ds
                dq = mm(kt[w, head_channels(g, j), :], ds)
                dqt[HD * j : HD * (j + 1), :] = (dq[:, 0:TOK] * HD ** (-0.5)).astype(BF16)
            dk = mm(ds_s[...], q_rows[...]) * LN2
            dv = mm(p_s[...], do_rows[...])
            dproj[512 * w : 512 * w + TOK, columns_of(g)] = jnp.concatenate(
                [dqt[...].T, dk.astype(BF16), dv.astype(BF16)], axis=1
            )
        group_gradients(scale, g, normed_t, dproj, mixt_all, cot_b, block, parts_first.at[g])
        for now in range(JOBS):

            @pl.when(g == now)
            def _():
                first[now].start()
                for i in range(JOBS):
                    second[i].advance(now, result(JOBS + i))
                for i in range(now):
                    first[i].advance(now - 1 - i)

        return carry

    lax.fori_loop(0, JOBS, group, 0)
    for now in range(JOBS, 2 * JOBS):
        w = now - JOBS
        if w < 2:
            dnormed = mm_nt(dproj[512 * w : 512 * w + TOK], wsorted[...])
            total = cot_s[w] + norm_backward(dnormed, xhat_s[w], rstd_s[w], gain_ref[...])
            grad_ref[7 * w : 7 * w + 7] = total.reshape(7, 7, 8, C).astype(BF16)
        for i in range(JOBS):
            if 0 <= now - 1 - i <= 3:
                first[i].advance(now - 1 - i, result(i))
    for reduction in first + second:
        reduction.finish()


def second_kernel(
    scale,
    y_own, y_ahead, y_behind, y_above, y_corner, c_own, c_ahead, c_behind_here, c_above_here, c_corner_here,
    gain_ref, bias_ref, wqkv_ref, wout_ref,
    own, ahead_there, behind_there, above_there, corner_there, parts,
    normed_t, dproj, cot_b, mixt, wsorted, block, qbd, k, kt, v, vt, qn, dot_s, dobd, dopt, dqt,
    e_a, e_b, ds_a, ds_b, do_rows, q_rows, pen, cot_s, xhat_s,
    ahead, behind, above, corner, c_behind, c_above, c_corner, send_sem, recv_sem,
):
    exchange = Exchange(-1, send_sem, recv_sem)
    exchange.greet((1, -1))
    e_s, ds_s = (e_a, e_b), (ds_a, ds_b)
    for ref in (qbd, dobd, do_rows, q_rows, normed_t, dproj, cot_b, mixt):
        ref[...] = jnp.zeros_like(ref)
    sort_columns(wsorted, wqkv_ref)
    for w in range(2):
        base = 512 * w
        last_frames = lax.axis_index("tm") == (lax.axis_size("tm") - 1 if w == 0 else 0)
        last_rows = (lax.axis_index("rows") == lax.axis_size("rows") - 1) if w == 1 else False

        def region_of(token, segment):
            columns = 4 if segment == 0 else 3
            late = jnp.where(last_frames & (token % 8 < 4), 1, 0)
            below = jnp.where(last_rows & (token // 8 // columns >= 4), 2, 0)
            return late + below

        def gather(into, own, ahead, behind, above, corner):
            def put(rho, count, whole):
                into[32 * rho : 32 * (rho + count)] = whole[:, 3:7].reshape(-1, C)
                into[224 + 24 * rho : 224 + 24 * (rho + count)] = whole[:, 0:3].reshape(-1, C)

            if w == 0:
                put(0, 7, joined(ahead[...], own[0:7]))
            else:
                put(0, 4, joined(own[7:11], behind[...]))
                put(4, 3, joined(above[...], corner[...]))

        gather(xhat_s, y_own, y_ahead, y_behind, y_above, y_corner)
        if w == 1:
            exchange.wait_for((0, 1, 2))
        gather(cot_s, c_own, c_ahead, c_behind, c_above, c_corner)
        xhat, rstd = standardized(xhat_s[...])
        xhat_s[...] = xhat
        normed = (xhat * gain_ref[...] + bias_ref[...]).astype(BF16)
        normed_t[:, base : base + TOK] = normed.T
        queries = (mm(normed, wqkv_ref[:, 0:C]) * QSCALE).astype(BF16)
        qn[...] = queries
        keys = mm(normed, wqkv_ref[:, C : 2 * C]).astype(BF16)
        k[...] = keys
        values_f = mm(normed, wqkv_ref[:, 2 * C :])
        values = values_f.astype(BF16)
        v[...] = values
        cot_h = cot_s[...].astype(BF16)
        dmixed = mm_nt(cot_h, wout_ref[...]).astype(BF16)
        for s, (start, stop) in enumerate(SPLIT):
            count = stop - start
            cot_b[512 * w + 256 * s : 512 * w + 256 * s + count] = cot_h[start:stop]
            put_diagonal(qbd, queries[start:stop].T, 256, 1024 * s)
            kt[:, 256 * s : 256 * s + count] = keys[start:stop].T
            dot_s[:, 256 * s : 256 * s + count] = dmixed[start:stop].T
            turned = values[start:stop].T
            put_values(vt, turned, 256 * s)
            total = jnp.sum(turned.astype(F32), axis=1, keepdims=True)
            other = 1 - s
            lane = 256 * other + SPLIT[other][1] - SPLIT[other][0]
            first = lax.broadcasted_iota(jnp.int32, (C, VIRTUAL), 1) == 0
            total = jnp.where(first, total, 0.0).astype(BF16)
            number = jnp.where(first[0 : VROWS - HD], float(count), 0.0).astype(BF16)
            for head in range(HEADS):
                at = VROWS * head
                vt[at : at + HD, lane : lane + VIRTUAL] = total[HD * head : HD * (head + 1)]
                vt[at + HD : at + VROWS, lane : lane + VIRTUAL] = number
            shape = (count, 256)
            key = region_of(lax.broadcasted_iota(jnp.int32, shape, 0), s)
            query = region_of(lax.broadcasted_iota(jnp.int32, shape, 1), s)
            pen[start:stop] = jnp.where(key == query, 0.0, 1.0)

        if w == 0:
            exchange.wait_for_others()
            exchange.send(1, c_behind_here, c_behind, 1)
            exchange.send(2, c_above_here, c_above, 1)
            exchange.send(3, c_corner_here, c_corner, 1)

        def group(g, carry):
            virtual_dv = []
            grads = []
            for s, (start, stop) in enumerate(SPLIT):
                count = stop - start
                kg = k[start:stop, channels_of(g)]
                apart = pen[start:stop] > 0.5
                sums_of = []
                for j in range(GROUP):
                    lanes = slice(256 * j, 256 * (j + 1))
                    scores = mm(kg, qbd[channels_of(g), 1024 * s + 256 * j : 1024 * s + 256 * (j + 1)])
                    scores = jnp.where(apart, MASKED, scores)
                    top = jnp.maximum(jnp.max(scores, axis=0, keepdims=True), MASKED)
                    e_s[s][0:count, lanes] = jnp.exp2(scores - top).astype(BF16)
                    first = lax.broadcasted_iota(jnp.int32, (VIRTUAL, 256), 0) == 0
                    e_s[s][count : count + VIRTUAL, lanes] = jnp.where(
                        first, jnp.exp2(MASKED - top), 0.0
                    ).astype(BF16)
                for j in range(GROUP):
                    lanes = slice(256 * j, 256 * (j + 1))
                    tokens = slice(256 * s, 256 * (s + 1))
                    mixed = mm(
                        vt[head_values(g, j), 256 * s : 256 * s + count + VIRTUAL], e_s[s][:, lanes]
                    )
                    inv = 1.0 / mixed[HD : HD + 1]
                    mixed = mixed[:HD] * inv
                    mixt[head_channels(g, j), 512 * w + 256 * s : 512 * w + 256 * s + count] = mixed[
                        :, 0:count
                    ].astype(BF16)
                    do = dot_s[head_channels(g, j), tokens].astype(F32) * inv
                    inside = lax.broadcasted_iota(jnp.int32, do.shape, 1) < count
                    do = jnp.where(inside, do, 0.0).astype(BF16)
                    sums_of.append(jnp.sum(mixed * do.astype(F32), axis=0, keepdims=True))
                    dopt[HD * j : HD * (j + 1), tokens] = do
                    dobd[HD * j : HD * (j + 1), 1024 * s + 256 * j : 1024 * s + 256 * (j + 1)] = do
                turned = dopt[:, 256 * s : 256 * (s + 1)].T
                qg = qn[start:stop, channels_of(g)]
                for j in range(GROUP):
                    lanes = slice(256 * j, 256 * (j + 1))
                    at = 1024 * s + 256 * j
                    do_rows[at : at + 256] = own_lanes(j, turned)
                    q_rows[at : at + count] = own_lanes(j, qg)
                    dp = mm(v[start:stop, channels_of(g)], dobd[:, at : at + 256]) - sums_of[j]
                    ds = e_s[s][0:count, lanes].astype(F32) * jnp.where(apart, 0.0, dp)
                    ds = ds.astype(BF16)
                    ds_s[s][:, lanes] = ds
                    dq = mm(kt[head_channels(g, j), 256 * s : 256 * s + count], ds)
                    dqt[HD * j : HD * (j + 1), 256 * s : 256 * (s + 1)] = (dq * HD ** (-0.5)).astype(BF16)
                block = slice(1024 * s, 1024 * (s + 1))
                dv = mm(e_s[s][...], do_rows[block])
                dk = mm(ds_s[s][...], q_rows[block]) * LN2
                virtual_dv.append(dv[count : count + 1])
                grads.append((dk, dv[0:count]))
            for s, (start, stop) in enumerate(SPLIT):
                rows = slice(base + start, base + stop)
                dk, dv = grads[s]
                dproj[rows, columns_of(g)] = jnp.concatenate(
                    [
                        dqt[:, 256 * s : 256 * s + stop - start].T,
                        dk.astype(BF16),
                        (dv + virtual_dv[1 - s]).astype(BF16),
                    ],
                    axis=1,
                )
            return carry

        lax.fori_loop(0, HEADS // GROUP, group, 0)
        dnormed = mm_nt(dproj[base : base + TOK], wsorted[...])
        total = cot_s[...] + norm_backward(dnormed, xhat_s[...], rstd, gain_ref[...])
        whole = jnp.concatenate(
            [total[224:392].reshape(7, 3, 8, C), total[0:224].reshape(7, 4, 8, C)], axis=1
        )
        low, high = whole[:, :, 0:4].astype(BF16), whole[:, :, 4:8].astype(BF16)
        if w == 0:
            ahead[...] = low
            own[0:7] = high
            exchange.send(0, ahead, ahead_there)
        else:
            own[7:11] = low[0:4]
            behind[...] = high[0:4]
            above[...] = low[4:7]
            corner[...] = high[4:7]
            exchange.send(1, behind, behind_there)
            exchange.send(2, above, above_there)
            exchange.send(3, corner, corner_there)

    def gradients(g, carry):
        group_gradients(scale, g, normed_t, dproj, mixt, cot_b, block, parts.at[g])
        return carry

    lax.fori_loop(0, JOBS, gradients, 0)
    exchange.wait((0, 1, 2))


def piece_shapes():
    return [(rows, 7, 4, C) for rows in (11, 7, 4, 3, 3)]


PARTS = [(JOBS, 2, 4, 4, 4, 4, 512)]
SAVED = [
    jax.ShapeDtypeStruct((2, C, 512), BF16),
    jax.ShapeDtypeStruct((2, HEADS // GROUP, 1, 2048), F32),
]
TOKENS = (14, 7, 8, C)
IN_VMEM = pl.BlockSpec(memory_space=pltpu.VMEM)


ANYWHERE = pl.BlockSpec(memory_space=pl.ANY)


def call(
    kernel, name, args, out_shape, scratch, there=(), far=(), semaphores=(), collective_id=None
):
    return pl.pallas_call(
        kernel,
        in_specs=[ANYWHERE if i in far else IN_VMEM for i in range(len(args))],
        out_specs=[ANYWHERE if i in there else IN_VMEM for i in range(len(out_shape))],
        out_shape=out_shape,
        scratch_shapes=[pltpu.VMEM(shape, dtype) for shape, dtype in scratch]
        + [pltpu.SemaphoreType.DMA(shape) for shape in semaphores],
        compiler_params=pltpu.CompilerParams(
            vmem_limit_bytes=VMEM_LIMIT,
            has_side_effects=collective_id is not None,
            collective_id=collective_id,
        ),
        name=name,
    )(*args)


def halves(shapes):
    return [jax.ShapeDtypeStruct(shape, BF16) for shape in shapes]


def forward_first(x, cot, weights):
    pieces = piece_shapes()
    outs = call(
        forward_kernel,
        "forward_first",
        (x, cot, *weights),
        SAVED + halves(pieces * 2),
        [(shape, BF16) for shape in pieces[1:] + pieces[1:2]]
        + [((C, 2048), BF16), ((TOK, C), BF16), ((HEADS * VROWS, TOK), BF16)],
        there=(3, 4, 5, 6, 8),
        semaphores=[(6,)] * 2,
        collective_id=1,
    )
    return outs[:2], outs[2:7], outs[7:]


GRADIENT_SCRATCH = [
    ((C, 1024), BF16), ((1024, 3 * C), BF16), ((1024, C), BF16), ((C, 1024), BF16), ((C, 3 * C), BF16), ((C, C), F32),
]


def backward_first(scale, x, weights, saved, pieces, parts):
    both = 2 * JOBS
    args = (x, *weights, *saved, *pieces, parts)
    return call(
        functools.partial(backward_first_kernel, scale),
        "backward_first",
        args,
        halves([TOKENS]) + [jax.ShapeDtypeStruct((4, width), F32) for width in (3 * C, C)] * 2,
        GRADIENT_SCRATCH
        + [(PARTS[0], BF16)]
        + [
            ((2, C, 2048), BF16), ((2, TOK, C), BF16), ((2, C, TOK), BF16), ((2, TOK, C), BF16),
            ((2, TOK, C), BF16), ((2, TOK, C), BF16), ((2, C, 2048), BF16),
            ((TOK, 2048), BF16), ((TOK, 2048), BF16), ((128, TOK), BF16),
            ((2048, 128), BF16), ((2048, 128), BF16),
            ((2, TOK, C), F32), ((2, TOK, C), F32), ((2, TOK, 1), F32),
        ]
        + [((both, 4, 4, 4, 4, 512), BF16)] * 3
        + [((both, 4, 4, 4, 512), BF16), ((both, 4, 4, 512), BF16)],
        far=(len(args) - 1,),
        semaphores=[(JOBS,), (both, 10), (both, 10)],
        collective_id=3,
    )


def hand_on_kernel(*refs):
    for source, target in zip(refs[:5], refs[5:]):
        target[...] = source[...]


def handed_on(outs):
    return call(
        hand_on_kernel,
        "hand_on",
        outs,
        [jax.ShapeDtypeStruct(out.shape, out.dtype) for out in outs],
        [],
    )


def second_block(scale, y_pieces, c_pieces, weights):
    return call(
        functools.partial(second_kernel, scale),
        "second_block",
        (*y_pieces, *c_pieces, *weights),
        halves(piece_shapes() + PARTS),
        GRADIENT_SCRATCH
        + [
            ((C, 2048), BF16), ((TOK, C), BF16), ((C, 512), BF16), ((TOK, C), BF16),
            ((HEADS * VROWS, 512), BF16), ((TOK, C), BF16), ((C, 512), BF16),
            ((128, 2048), BF16), ((128, 512), BF16), ((128, 512), BF16),
            ((224 + VIRTUAL, 1024), BF16), ((168 + VIRTUAL, 1024), BF16),
            ((224, 1024), BF16), ((168, 1024), BF16),
            ((2048, 128), BF16), ((2048, 128), BF16),
            ((TOK, 256), F32), ((TOK, C), F32), ((TOK, C), F32),
        ]
        + [(shape, BF16) for shape in piece_shapes()[1:] + piece_shapes()[2:]],
        there=range(1, 5),
        semaphores=[(7,)] * 2,
        collective_id=2,
    )


def per_device(
    video_clip, cotangent,
    gain_first, bias_first, qkv_first, out_first,
    gain_second, bias_second, qkv_second, out_second,
):
    frames, rows_here, columns, channels = video_clip.shape
    devices = lax.axis_size("tm") * lax.axis_size("rows")
    scale = 1.0 / math.sqrt(frames * rows_here * columns * devices)
    x = video_clip.transpose(1, 2, 0, 3)
    cot = cotangent.transpose(1, 2, 0, 3)
    first = (gain_first.reshape(1, C), bias_first.reshape(1, C), qkv_first, out_first)
    second = (gain_second.reshape(1, C), bias_second.reshape(1, C), qkv_second, out_second)
    saved, y_pieces, c_pieces = forward_first(x, cot, first)
    *d_pieces, parts = second_block(scale, y_pieces, c_pieces, second)
    grad, *sums = handed_on(backward_first(scale, x, first, saved, d_pieces, parts))
    return (grad.transpose(2, 0, 1, 3), *sums)


def solution(mesh):
    clip = P("tm", "rows", None, None)
    scattered = P(("tm", "rows"), None)
    return jax.shard_map(
        per_device,
        mesh=mesh,
        in_specs=(clip, clip) + (P(),) * 8,
        out_specs=(clip,) + (scattered,) * 4,
        check_vma=False,
    )
```

```python
import functools
import math

import jax
import jax.numpy as jnp
from jax import lax
from jax.experimental import pallas as pl
from jax.experimental.pallas import tpu as pltpu
from jax.sharding import PartitionSpec as P

F32, BF16 = jnp.float32, jnp.bfloat16
C, HEADS, HD = 512, 16, 32
TOK = 392
GROUP = 4
LOG2E = math.log2(math.e)
QSCALE = HD ** (-0.5) * LOG2E
MASKED = -1000000000.0 * LOG2E
LN2 = math.log(2.0)
SPLIT = ((0, 224), (224, 392))
VIRTUAL = 16
ROWS = 400
MIB = 1024 * 1024


def mm(a, b):
    return lax.dot_general(a, b, (((1,), (0,)), ((), ())), preferred_element_type=F32)


def mm_nt(a, b):
    return lax.dot_general(a, b, (((1,), (1,)), ((), ())), preferred_element_type=F32)


def mm_tn(a, b):
    return lax.dot_general(a, b, (((0,), (0,)), ((), ())), preferred_element_type=F32)


def standardized(values):
    center = values - jnp.mean(values, axis=-1, keepdims=True)
    rstd = lax.rsqrt(jnp.mean(center * center, axis=-1, keepdims=True) + 1e-05)
    return center * rstd, rstd


def tiles(block):
    return block.astype(F32).reshape(-1, C)


def own_lanes(j, block):
    lane = lax.broadcasted_iota(jnp.int32, block.shape, 1) // HD
    return jnp.where(lane == j, block, jnp.zeros_like(block))


def put_diagonal(ref, turned, pitch, column=0):
    for head in range(HEADS):
        at = pitch * (head % GROUP) + column
        ref[HD * head : HD * (head + 1), at : at + turned.shape[1]] = turned[HD * head : HD * (head + 1)]


def channels_of(g, first=0):
    return pl.ds(pl.multiple_of(g * 128 + first, 128), 128)


def head_channels(g, j):
    return pl.ds(pl.multiple_of(g * 128 + j * HD, HD), HD)


MESH = pl.DeviceIdType.MESH
ROUTES = ((-1, 0), (1, 0), (0, -1), (1, -1))


class Exchange:
    def __init__(self, way, send_sem, recv_sem):
        self.way, self.sems, self.copies = way, (send_sem, recv_sem), []

    def device(self, steps, sign):
        size = lax.axis_size("tm"), lax.axis_size("rows")
        here = lax.axis_index("tm"), lax.axis_index("rows")
        return tuple((i + sign * d + n) % n for i, d, n in zip(here, steps, size))

    def greet(self, ways):
        self.ways = ways
        for way in ways:
            for steps in ROUTES:
                pl.semaphore_signal(
                    pltpu.get_barrier_semaphore(),
                    inc=1,
                    device_id=self.device(steps, -way),
                    device_id_type=MESH,
                )

    def wait_for_others(self):
        pl.semaphore_wait(pltpu.get_barrier_semaphore(), len(self.ways) * len(ROUTES))

    def send(self, route, source, target, way=None):
        i = len(self.copies)
        copy = pltpu.make_async_remote_copy(
            src_ref=source,
            dst_ref=target,
            send_sem=self.sems[0].at[i],
            recv_sem=self.sems[1].at[i],
            device_id=self.device(ROUTES[route], way or self.way),
            device_id_type=MESH,
        )
        copy.start()
        self.copies.append(copy)

    def wait_for(self, numbers):
        for i in numbers:
            self.copies[i].wait_recv()

    def wait(self, arrived=()):
        for i, copy in enumerate(self.copies):
            copy.wait_send()
            if i not in arrived:
                copy.wait_recv()


def pieces_of(whole, w, pieces):
    own, ahead, behind, above, corner = pieces
    if w == 0:
        above[...] = whole[0:3, :, 0:4].astype(BF16)
        corner[...] = whole[0:3, :, 4:8].astype(BF16)
        ahead[0:4] = whole[3:7, :, 0:4].astype(BF16)
        own[0:4] = whole[3:7, :, 4:8].astype(BF16)
    else:
        ahead[4:7] = whole[0:3, :, 0:4].astype(BF16)
        own[4:7] = whole[0:3, :, 4:8].astype(BF16)
        behind[...] = whole[3:7, :, 4:8].astype(BF16)
        own[7:11] = whole[3:7, :, 0:4].astype(BF16)


def joined(low, high):
    return jnp.concatenate([low.astype(F32), high.astype(F32)], axis=2)


def forward_kernel(
    x_ref, cot_ref, gain_ref, bias_ref, wqkv_ref, wout_ref, mixt_ref, stat_ref, *refs,
):
    y_own, y_ahead_there, y_behind, y_above_there, y_corner_there = refs[0:5]
    c_own, c_ahead_there, *c_later = refs[5:10]
    y_ahead, y_above, y_corner, c_ahead, qbd, k, vt, send_sem, recv_sem = refs[10:]
    exchange = Exchange(1, send_sem, recv_sem)
    exchange.greet((1,))
    for w in range(2):
        pieces_of(cot_ref[7 * w : 7 * w + 7].astype(F32), w, (c_own, c_ahead, *c_later))
    exchange.wait_for_others()
    exchange.send(0, c_ahead, c_ahead_there)
    qbd[...] = jnp.zeros_like(qbd)
    for w in range(2):
        rows = slice(7 * w, 7 * w + 7)
        x = tiles(x_ref[rows])
        xhat, _ = standardized(x)
        normed = (xhat * gain_ref[...] + bias_ref[...]).astype(BF16)
        put_diagonal(qbd, (mm(normed, wqkv_ref[:, 0:C]) * QSCALE).astype(BF16).T, 512)
        k[...] = mm(normed, wqkv_ref[:, C : 2 * C]).astype(BF16)
        vt[...] = mm(normed, wqkv_ref[:, 2 * C :]).astype(BF16).T

        def group(g, carry):
            kg = k[:, channels_of(g)]
            for j in range(GROUP):
                lanes = slice(512 * j, 512 * (j + 1))
                scores = mm(kg, qbd[channels_of(g), lanes])
                top = jnp.max(scores, axis=0, keepdims=True)
                e = jnp.exp2(scores - top)
                sums = jnp.sum(e, axis=0, keepdims=True)
                mixed = mm(vt[head_channels(g, j), :], e.astype(BF16))
                stat_ref[w, g, :, lanes] = top + jnp.log2(sums)
                mixt_ref[w, head_channels(g, j), :] = (mixed * (1.0 / sums)).astype(BF16)
            return carry

        lax.fori_loop(0, HEADS // GROUP, group, 0)
        y = x + mm_tn(mixt_ref[w, :, 0:TOK], wout_ref[...])
        pieces_of(y.reshape(7, 7, 8, C), w, (y_own, y_ahead, y_behind, y_above, y_corner))
        if w == 0:
            exchange.send(2, y_above, y_above_there)
            exchange.send(3, y_corner, y_corner_there)
            exchange.send(0, y_ahead.at[0:4], y_ahead_there.at[0:4])
        else:
            exchange.send(0, y_ahead.at[4:7], y_ahead_there.at[4:7])
    exchange.wait()


def write_part(g, block, part):
    turn = g % 3

    def layer(z, carry):
        for xy in range(16):
            x, y = xy // 4, xy % 4
            rows = pl.ds(pl.multiple_of((z * 16 + x // 2 * 8 + y * 2 + x % 2) * 8, 8), 8)
            values = block[rows, :]
            first = jnp.where(turn == 0, x, jnp.where(turn == 1, y, z))
            second = jnp.where(turn == 0, y, jnp.where(turn == 1, z, x))
            third = jnp.where(turn == 0, z, jnp.where(turn == 1, x, y))
            part[0, first, second, third] = values[0:4].astype(BF16)
            part[1, first, second, third] = values[4:8].astype(BF16)
        return carry

    lax.fori_loop(0, 4, layer, 0)


def group_gradients(scale, g, normed_t, dproj, mixt, cot_b, block, part):
    block[:, 0:384] = mm(normed_t[...], dproj[:, columns_of(g)]) * scale
    block[:, 384:512] = mm(mixt[...], cot_b[:, channels_of(g)]) * scale
    write_part(g, block, part)


def columns_of(g):
    return pl.ds(pl.multiple_of(g * 384, 128), 384)


def sort_columns(sorted_ref, wqkv_ref):
    for g in range(HEADS // GROUP):
        for i in range(3):
            sorted_ref[:, 384 * g + 128 * i : 384 * g + 128 * (i + 1)] = wqkv_ref[
                :, C * i + 128 * g : C * i + 128 * (g + 1)
            ]


def norm_backward(dnormed, xhat, rstd, gain):
    d = dnormed.astype(BF16).astype(F32) * gain
    return rstd * (
        d
        - jnp.mean(d, axis=-1, keepdims=True)
        - xhat * jnp.mean(d * xhat, axis=-1, keepdims=True)
    )


def coordinates():
    tm, rows = lax.axis_index("tm"), lax.axis_index("rows")
    return {
        "x": tm // 4 % 2 * 2 + rows // 2,
        "y": tm % 4,
        "z": tm // 8,
        "core": rows % 2,
    }


def device_at(place):
    tm = place["z"] * 8 + place["x"] // 2 * 4 + place["y"]
    return (tm, place["x"] % 2 * 2 + place["core"])


def beside(here, axis, steps):
    return device_at({**here, axis: (here[axis] + steps) % (2 if axis == "core" else 4)})


ORDERS = ("xyz", "yzx", "zxy")


class Reduction:
    def __init__(self, order, here, partners, part, local_sem, buffers, sems):
        self.order, self.here, self.partners, self.part = order, here, partners, part
        self.held, self.other, *self.slots = buffers
        self.local_sem, self.sems = local_sem, sems

    def remote(self, number, source, target, partner):
        return pltpu.make_async_remote_copy(
            src_ref=source,
            dst_ref=target,
            send_sem=self.sems[0].at[number],
            recv_sem=self.sems[1].at[number],
            device_id=partner,
            device_id_type=MESH,
        )

    def local_copy(self):
        return pltpu.make_async_copy(self.part.at[self.here["core"]], self.held, self.local_sem)

    def core_copy(self):
        return self.remote(0, self.part.at[1 - self.here["core"]], self.other, self.partners["core", 1])

    def source(self, step):
        return self.held if step == 0 else self.slots[step - 1].at[3]

    def axis_copies(self, step):
        axis = self.order[step]
        return [
            self.remote(
                3 * step + away,
                self.source(step).at[(self.here[axis] + away) % 4],
                self.slots[step].at[away - 1],
                self.partners[axis, away],
            )
            for away in (1, 2, 3)
        ]

    def start(self):
        self.core_copy().start()

    def advance(self, stage, out=None):
        if stage == 0:
            self.core_copy().wait_recv()
            if self.local_sem is not None:
                self.local_copy().wait()
                own = self.held
            else:
                own = self.part.at[self.here["core"]]
            for i in range(4):
                self.held[i] = (own[i].astype(F32) + self.other[i].astype(F32)).astype(BF16)
        else:
            for copy in self.axis_copies(stage - 1):
                copy.wait_recv()
            total = self.source(stage - 1)[self.here[self.order[stage - 1]]].astype(F32)
            for slot in range(3):
                total = total + self.slots[stage - 1][slot].astype(F32)
            if stage == 3:
                out(total)
                return
            self.slots[stage - 1][3] = total.astype(BF16)
        for copy in self.axis_copies(stage):
            copy.start()

    def finish(self):
        self.core_copy().wait_send()
        for step in range(3):
            for copy in self.axis_copies(step):
                copy.wait_send()


JOBS = HEADS // GROUP


def backward_first_kernel(
    scale,
    x_ref, gain_ref, bias_ref, wqkv_ref, wout_ref, mixt_ref, stat_ref,
    own, ahead, behind, above, corner, parts_second,
    grad_ref, gqkv1, gout1, gqkv2, gout2,
    normed_t, dproj, cot_b, mixt_all, wsorted, block, parts_first,
    qbd, k, kt, v, qn, don, dobd, p_s, ds_s, dqt, do_rows, q_rows, cot_s, xhat_s, rstd_s,
    held, other, slots_a, slots_b, slots_c, local_sem, send_sem, recv_sem,
):
    here = coordinates()
    partners = {("core", 1): beside(here, "core", 1)}
    for axis in "xyz":
        for away in (1, 2, 3):
            partners[axis, away] = beside(here, axis, away)
    barrier = pltpu.get_barrier_semaphore()
    for partner in partners.values():
        pl.semaphore_signal(barrier, inc=1, device_id=partner, device_id_type=MESH)

    def job(i):
        of_first = i < JOBS
        g = i % JOBS
        return Reduction(
            ORDERS[g % 3],
            here,
            partners,
            parts_first.at[g] if of_first else parts_second.at[g],
            None if of_first else local_sem.at[g],
            [ref.at[i] for ref in (held, other, slots_a, slots_b, slots_c)],
            (send_sem.at[i], recv_sem.at[i]),
        )

    def result(i):
        gqkv, gout = (gqkv1, gout1) if i < JOBS else (gqkv2, gout2)
        g = i % JOBS

        def out(total):
            for part in range(3):
                at = C * part + 128 * g
                gqkv[:, at : at + 128] = total[:, 128 * part : 128 * (part + 1)]
            gout[:, 128 * g : 128 * (g + 1)] = total[:, 384:512]

        return out

    first, second = [job(i) for i in range(JOBS)], [job(JOBS + i) for i in range(JOBS)]
    for reduction in second:
        reduction.local_copy().start()
    for ref in (qbd, dobd, do_rows, q_rows, normed_t, dproj, cot_b):
        ref[...] = jnp.zeros_like(ref)
    sort_columns(wsorted, wqkv_ref)
    for w in range(2):
        xhat, rstd = standardized(tiles(x_ref[7 * w : 7 * w + 7]))
        xhat_s[w] = xhat
        rstd_s[w] = rstd
        normed = (xhat * gain_ref[...] + bias_ref[...]).astype(BF16)
        normed_t[:, 512 * w : 512 * w + TOK] = normed.T
        queries = (mm(normed, wqkv_ref[:, 0:C]) * QSCALE).astype(BF16)
        qn[w] = queries
        put_diagonal(qbd.at[w], queries.T, 512)
        keys = mm(normed, wqkv_ref[:, C : 2 * C]).astype(BF16)
        k[w] = keys
        kt[w] = keys.T
        v[w] = mm(normed, wqkv_ref[:, 2 * C :]).astype(BF16)
        if w == 0:
            pieces = [joined(above[...], corner[...]), joined(ahead[0:4], own[0:4])]
        else:
            pieces = [joined(ahead[4:7], own[4:7]), joined(own[7:11], behind[...])]
        cot = jnp.concatenate([piece.reshape(-1, C) for piece in pieces], axis=0)
        cot_s[w] = cot
        cot_h = cot.astype(BF16)
        cot_b[512 * w : 512 * w + TOK] = cot_h
        dmixed = mm_nt(cot_h, wout_ref[...]).astype(BF16)
        don[w] = dmixed
        put_diagonal(dobd.at[w], dmixed.T, 512)
        mixt_all[:, 512 * w : 512 * (w + 1)] = mixt_ref[w]
        if w == 0:
            pl.semaphore_wait(barrier, len(partners))
            for reduction in second:
                reduction.start()

    def group(g, carry):
        for w in range(2):
            kg = k[w, :, channels_of(g)]
            vg = v[w, :, channels_of(g)]
            qg = qn[w, :, channels_of(g)]
            dog = don[w, :, channels_of(g)]
            for j in range(GROUP):
                lanes = slice(512 * j, 512 * (j + 1))
                do_rows[w, 512 * j : 512 * j + TOK] = own_lanes(j, dog)
                q_rows[w, 512 * j : 512 * j + TOK] = own_lanes(j, qg)
                scores = mm(kg, qbd[w, channels_of(g), lanes])
                p = jnp.exp2(scores - stat_ref[w, g, :, lanes]).astype(BF16)
                p_s[w, :, lanes] = p
                dsum = jnp.sum(
                    mixt_ref[w, head_channels(g, j), :].astype(F32)
                    * dobd[w, head_channels(g, j), lanes].astype(F32),
                    axis=0, keepdims=True,
                )
                dp = mm(vg, dobd[w, channels_of(g), lanes]) - dsum
                ds = (p.astype(F32) * dp).astype(BF16)
                ds_s[w, :, lanes] = ds
                dq = mm(kt[w, head_channels(g, j), :], ds)
                dqt[w, HD * j : HD * (j + 1), :] = (dq[:, 0:TOK] * HD ** (-0.5)).astype(BF16)
            dk = mm(ds_s[w], q_rows[w]) * LN2
            dv = mm(p_s[w], do_rows[w])
            dproj[512 * w : 512 * w + TOK, columns_of(g)] = jnp.concatenate(
                [dqt[w].T, dk.astype(BF16), dv.astype(BF16)], axis=1
            )
        group_gradients(scale, g, normed_t, dproj, mixt_all, cot_b, block, parts_first.at[g])
        for now in range(JOBS):

            @pl.when(g == now)
            def _():
                first[now].start()
                for i in range(JOBS):
                    second[i].advance(now, result(JOBS + i))
                for i in range(now):
                    first[i].advance(now - 1 - i)

        return carry

    lax.fori_loop(0, JOBS, group, 0)
    for now in range(JOBS, 2 * JOBS):
        w = now - JOBS
        if w < 2:
            dnormed = mm_nt(dproj[512 * w : 512 * w + TOK], wsorted[...])
            total = cot_s[w] + norm_backward(dnormed, xhat_s[w], rstd_s[w], gain_ref[...])
            grad_ref[7 * w : 7 * w + 7] = total.reshape(7, 7, 8, C).astype(BF16)
        for i in range(JOBS):
            if 0 <= now - 1 - i <= 3:
                first[i].advance(now - 1 - i, result(i))
    for reduction in first + second:
        reduction.finish()


def second_kernel(
    scale,
    y_own, y_ahead, y_behind_here, y_above, y_corner, c_own, c_ahead, c_behind_here, c_above_here, c_corner_here,
    gain_ref, bias_ref, wqkv_ref, wout_ref,
    own, ahead_there, behind_there, above_there, corner_there, parts,
    normed_t, dproj, cot_b, mixt, wsorted, block, qbd, k, kt, v, vt, qn, dot_s, dobd, dopt, dqt,
    e_a, e_b, ds_a, ds_b, do_rows, q_rows, pen, cot_s, xhat_s,
    ahead, behind, above, corner, c_behind, c_above, c_corner, y_behind, send_sem, recv_sem,
):
    exchange = Exchange(-1, send_sem, recv_sem)
    exchange.greet((1, -1))
    e_s, ds_s = (e_a, e_b), (ds_a, ds_b)
    for ref in (qbd, dobd, do_rows, q_rows, normed_t, dproj, cot_b, mixt):
        ref[...] = jnp.zeros_like(ref)
    sort_columns(wsorted, wqkv_ref)
    for w in range(2):
        base = 512 * w
        last_frames = lax.axis_index("tm") == (lax.axis_size("tm") - 1 if w == 0 else 0)
        last_rows = (lax.axis_index("rows") == lax.axis_size("rows") - 1) if w == 1 else False

        def region_of(token, segment):
            columns = 4 if segment == 0 else 3
            late = jnp.where(last_frames & (token % 8 < 4), 1, 0)
            below = jnp.where(last_rows & (token // 8 // columns >= 4), 2, 0)
            return late + below

        def gather(into, own, ahead, behind, above, corner):
            def put(rho, count, whole):
                into[32 * rho : 32 * (rho + count)] = whole[:, 3:7].reshape(-1, C)
                into[224 + 24 * rho : 224 + 24 * (rho + count)] = whole[:, 0:3].reshape(-1, C)

            if w == 0:
                put(0, 7, joined(ahead[...], own[0:7]))
            else:
                put(0, 4, joined(own[7:11], behind[...]))
                put(4, 3, joined(above[...], corner[...]))

        if w == 1:
            exchange.wait_for((0, 1, 2, 3))
        gather(xhat_s, y_own, y_ahead, y_behind, y_above, y_corner)
        gather(cot_s, c_own, c_ahead, c_behind, c_above, c_corner)
        xhat, rstd = standardized(xhat_s[...])
        xhat_s[...] = xhat
        normed = (xhat * gain_ref[...] + bias_ref[...]).astype(BF16)
        normed_t[:, base : base + TOK] = normed.T
        queries = (mm(normed, wqkv_ref[:, 0:C]) * QSCALE).astype(BF16)
        qn[...] = queries
        keys = mm(normed, wqkv_ref[:, C : 2 * C]).astype(BF16)
        k[...] = keys
        values_f = mm(normed, wqkv_ref[:, 2 * C :])
        values = values_f.astype(BF16)
        v[...] = values
        cot_h = cot_s[...].astype(BF16)
        dmixed = mm_nt(cot_h, wout_ref[...]).astype(BF16)
        for s, (start, stop) in enumerate(SPLIT):
            count = stop - start
            cot_b[512 * w + 256 * s : 512 * w + 256 * s + count] = cot_h[start:stop]
            put_diagonal(qbd, queries[start:stop].T, 256, 1024 * s)
            kt[:, 256 * s : 256 * s + count] = keys[start:stop].T
            dot_s[:, 256 * s : 256 * s + count] = dmixed[start:stop].T
            turned = values[start:stop].T
            vt[:, 256 * s : 256 * s + count] = turned
            total = jnp.sum(turned.astype(F32), axis=1, keepdims=True)
            other = 1 - s
            lane = 256 * other + SPLIT[other][1] - SPLIT[other][0]
            first = lax.broadcasted_iota(jnp.int32, (C, VIRTUAL), 1) == 0
            vt[:, lane : lane + VIRTUAL] = jnp.where(first, total, 0.0).astype(BF16)
            shape = (count, 256)
            key = region_of(lax.broadcasted_iota(jnp.int32, shape, 0), s)
            query = region_of(lax.broadcasted_iota(jnp.int32, shape, 1), s)
            pen[start:stop] = jnp.where(key == query, 0.0, 1.0)

        if w == 0:
            exchange.wait_for_others()
            exchange.send(1, y_behind_here, y_behind, 1)
            exchange.send(1, c_behind_here, c_behind, 1)
            exchange.send(2, c_above_here, c_above, 1)
            exchange.send(3, c_corner_here, c_corner, 1)

        def group(g, carry):
            virtual_dv = []
            grads = []
            for s, (start, stop) in enumerate(SPLIT):
                count = stop - start
                kg = k[start:stop, channels_of(g)]
                apart = pen[start:stop] > 0.5
                sums_of, invs = [], []
                for j in range(GROUP):
                    lanes = slice(256 * j, 256 * (j + 1))
                    scores = mm(kg, qbd[channels_of(g), 1024 * s + 256 * j : 1024 * s + 256 * (j + 1)])
                    scores = jnp.where(apart, MASKED, scores)
                    top = jnp.maximum(jnp.max(scores, axis=0, keepdims=True), MASKED)
                    e = jnp.exp2(scores - top)
                    e_s[s][0:count, lanes] = e.astype(BF16)
                    rest = jnp.exp2(MASKED - top)
                    first = lax.broadcasted_iota(jnp.int32, (VIRTUAL, 256), 0) == 0
                    e_s[s][count : count + VIRTUAL, lanes] = jnp.where(first, rest, 0.0).astype(BF16)
                    invs.append(1.0 / (jnp.sum(e, axis=0, keepdims=True) + (TOK - count) * rest))
                for j in range(GROUP):
                    lanes = slice(256 * j, 256 * (j + 1))
                    tokens = slice(256 * s, 256 * (s + 1))
                    inv = invs[j]
                    mixed = inv * mm(
                        vt[head_channels(g, j), 256 * s : 256 * s + count + VIRTUAL], e_s[s][:, lanes]
                    )
                    mixt[head_channels(g, j), 512 * w + 256 * s : 512 * w + 256 * s + count] = mixed[
                        :, 0:count
                    ].astype(BF16)
                    do = dot_s[head_channels(g, j), tokens].astype(F32) * inv
                    inside = lax.broadcasted_iota(jnp.int32, do.shape, 1) < count
                    do = jnp.where(inside, do, 0.0).astype(BF16)
                    sums_of.append(jnp.sum(mixed * do.astype(F32), axis=0, keepdims=True))
                    dopt[HD * j : HD * (j + 1), tokens] = do
                    dobd[HD * j : HD * (j + 1), 1024 * s + 256 * j : 1024 * s + 256 * (j + 1)] = do
                turned = dopt[:, 256 * s : 256 * (s + 1)].T
                qg = qn[start:stop, channels_of(g)]
                for j in range(GROUP):
                    lanes = slice(256 * j, 256 * (j + 1))
                    at = 1024 * s + 256 * j
                    do_rows[at : at + 256] = own_lanes(j, turned)
                    q_rows[at : at + count] = own_lanes(j, qg)
                    dp = mm(v[start:stop, channels_of(g)], dobd[:, at : at + 256]) - sums_of[j]
                    ds = e_s[s][0:count, lanes].astype(F32) * jnp.where(apart, 0.0, dp)
                    ds = ds.astype(BF16)
                    ds_s[s][:, lanes] = ds
                    dq = mm(kt[head_channels(g, j), 256 * s : 256 * s + count], ds)
                    dqt[HD * j : HD * (j + 1), 256 * s : 256 * (s + 1)] = (dq * HD ** (-0.5)).astype(BF16)
                block = slice(1024 * s, 1024 * (s + 1))
                dv = mm(e_s[s][...], do_rows[block])
                dk = mm(ds_s[s][...], q_rows[block]) * LN2
                virtual_dv.append(dv[count : count + 1])
                grads.append((dk, dv[0:count]))
            for s, (start, stop) in enumerate(SPLIT):
                rows = slice(base + start, base + stop)
                dk, dv = grads[s]
                dproj[rows, columns_of(g)] = jnp.concatenate(
                    [
                        dqt[:, 256 * s : 256 * s + stop - start].T,
                        dk.astype(BF16),
                        (dv + virtual_dv[1 - s]).astype(BF16),
                    ],
                    axis=1,
                )
            return carry

        lax.fori_loop(0, HEADS // GROUP, group, 0)
        dnormed = mm_nt(dproj[base : base + TOK], wsorted[...])
        total = cot_s[...] + norm_backward(dnormed, xhat_s[...], rstd, gain_ref[...])
        whole = jnp.concatenate(
            [total[224:392].reshape(7, 3, 8, C), total[0:224].reshape(7, 4, 8, C)], axis=1
        )
        low, high = whole[:, :, 0:4].astype(BF16), whole[:, :, 4:8].astype(BF16)
        if w == 0:
            ahead[...] = low
            own[0:7] = high
            exchange.send(0, ahead, ahead_there)
        else:
            own[7:11] = low[0:4]
            behind[...] = high[0:4]
            above[...] = low[4:7]
            corner[...] = high[4:7]
            exchange.send(1, behind, behind_there)
            exchange.send(2, above, above_there)
            exchange.send(3, corner, corner_there)

    def gradients(g, carry):
        group_gradients(scale, g, normed_t, dproj, mixt, cot_b, block, parts.at[g])
        return carry

    lax.fori_loop(0, JOBS, gradients, 0)
    exchange.wait((0, 1, 2, 3))


def piece_shapes():
    return [(rows, 7, 4, C) for rows in (11, 7, 4, 3, 3)]


PARTS = [(JOBS, 2, 4, 4, 4, 4, 512)]
SAVED = [
    jax.ShapeDtypeStruct((2, C, 512), BF16),
    jax.ShapeDtypeStruct((2, HEADS // GROUP, 1, 2048), F32),
]
TOKENS = (14, 7, 8, C)
IN_VMEM = pl.BlockSpec(memory_space=pltpu.VMEM)


ANYWHERE = pl.BlockSpec(memory_space=pl.ANY)


def call(
    kernel, name, args, out_shape, scratch, vmem, there=(), far=(), semaphores=(), collective_id=None
):
    return pl.pallas_call(
        kernel,
        in_specs=[ANYWHERE if i in far else IN_VMEM for i in range(len(args))],
        out_specs=[ANYWHERE if i in there else IN_VMEM for i in range(len(out_shape))],
        out_shape=out_shape,
        scratch_shapes=[pltpu.VMEM(shape, dtype) for shape, dtype in scratch]
        + [pltpu.SemaphoreType.DMA(shape) for shape in semaphores],
        compiler_params=pltpu.CompilerParams(
            vmem_limit_bytes=vmem * MIB,
            has_side_effects=collective_id is not None,
            collective_id=collective_id,
        ),
        name=name,
    )(*args)


def halves(shapes):
    return [jax.ShapeDtypeStruct(shape, BF16) for shape in shapes]


def forward_first(x, cot, weights):
    pieces = piece_shapes()
    outs = call(
        forward_kernel,
        "forward_first",
        (x, cot, *weights),
        SAVED + halves(pieces * 2),
        [(shape, BF16) for shape in (pieces[1], *pieces[3:], pieces[1])]
        + [((C, 2048), BF16), ((TOK, C), BF16), ((C, TOK), BF16)],
        vmem=20,
        there=(3, 5, 6, 8),
        semaphores=[(5,)] * 2,
        collective_id=1,
    )
    return outs[:2], outs[2:7], outs[7:]


GRADIENT_SCRATCH = [
    ((C, 1024), BF16), ((1024, 3 * C), BF16), ((1024, C), BF16), ((C, 1024), BF16), ((C, 3 * C), BF16), ((C, C), F32),
]


def backward_first(scale, x, weights, saved, pieces, parts):
    both = 2 * JOBS
    args = (x, *weights, *saved, *pieces, parts)
    return call(
        functools.partial(backward_first_kernel, scale),
        "backward_first",
        args,
        halves([TOKENS]) + [jax.ShapeDtypeStruct((4, width), F32) for width in (3 * C, C)] * 2,
        GRADIENT_SCRATCH
        + [(PARTS[0], BF16)]
        + [
            ((2, C, 2048), BF16), ((2, TOK, C), BF16), ((2, C, TOK), BF16), ((2, TOK, C), BF16),
            ((2, TOK, C), BF16), ((2, TOK, C), BF16), ((2, C, 2048), BF16),
            ((2, TOK, 2048), BF16), ((2, TOK, 2048), BF16), ((2, 128, TOK), BF16),
            ((2, 2048, 128), BF16), ((2, 2048, 128), BF16),
            ((2, TOK, C), F32), ((2, TOK, C), F32), ((2, TOK, 1), F32),
        ]
        + [((both, 4, 4, 4, 4, 512), BF16)] * 3
        + [((both, 4, 4, 4, 512), BF16), ((both, 4, 4, 512), BF16)],
        vmem=46,
        far=(len(args) - 1,),
        semaphores=[(JOBS,), (both, 10), (both, 10)],
        collective_id=3,
    )


def hand_on_kernel(*refs):
    for source, target in zip(refs[:5], refs[5:]):
        target[...] = source[...]


def handed_on(outs):
    return call(
        hand_on_kernel,
        "hand_on",
        outs,
        [jax.ShapeDtypeStruct(out.shape, out.dtype) for out in outs],
        [],
        vmem=8,
    )


def second_block(scale, y_pieces, c_pieces, weights):
    return call(
        functools.partial(second_kernel, scale),
        "second_block",
        (*y_pieces, *c_pieces, *weights),
        halves(piece_shapes() + PARTS),
        GRADIENT_SCRATCH
        + [
            ((C, 2048), BF16), ((TOK, C), BF16), ((C, 512), BF16), ((TOK, C), BF16),
            ((C, 512), BF16), ((TOK, C), BF16), ((C, 512), BF16),
            ((128, 2048), BF16), ((128, 512), BF16), ((128, 512), BF16),
            ((224 + VIRTUAL, 1024), BF16), ((168 + VIRTUAL, 1024), BF16),
            ((224, 1024), BF16), ((168, 1024), BF16),
            ((2048, 128), BF16), ((2048, 128), BF16),
            ((TOK, 256), F32), ((TOK, C), F32), ((TOK, C), F32),
        ]
        + [(shape, BF16) for shape in piece_shapes()[1:] + piece_shapes()[2:] + piece_shapes()[2:3]],
        vmem=28,
        there=range(1, 5),
        semaphores=[(8,)] * 2,
        collective_id=2,
    )


def per_device(
    video_clip, cotangent,
    gain_first, bias_first, qkv_first, out_first,
    gain_second, bias_second, qkv_second, out_second,
):
    frames, rows_here, columns, channels = video_clip.shape
    devices = lax.axis_size("tm") * lax.axis_size("rows")
    scale = 1.0 / math.sqrt(frames * rows_here * columns * devices)
    x = video_clip.transpose(1, 2, 0, 3)
    cot = cotangent.transpose(1, 2, 0, 3)
    first = (gain_first.reshape(1, C), bias_first.reshape(1, C), qkv_first, out_first)
    second = (gain_second.reshape(1, C), bias_second.reshape(1, C), qkv_second, out_second)
    saved, y_pieces, c_pieces = forward_first(x, cot, first)
    *d_pieces, parts = second_block(scale, y_pieces, c_pieces, second)
    grad, *sums = handed_on(backward_first(scale, x, first, saved, d_pieces, parts))
    return (grad.transpose(2, 0, 1, 3), *sums)


def solution(mesh):
    clip = P("tm", "rows", None, None)
    scattered = P(("tm", "rows"), None)
    return jax.shard_map(
        per_device,
        mesh=mesh,
        in_specs=(clip, clip) + (P(),) * 8,
        out_specs=(clip,) + (scattered,) * 4,
        check_vma=False,
    )
```

```python
import functools
import math

import jax
import jax.numpy as jnp
from jax import lax
from jax.experimental import pallas as pl
from jax.experimental.pallas import tpu as pltpu
from jax.sharding import PartitionSpec as P

F32, BF16 = jnp.float32, jnp.bfloat16
C, HEADS, HD = 512, 16, 32
TOK = 392
GROUP = 4
LOG2E = math.log2(math.e)
QSCALE = HD ** (-0.5) * LOG2E
MASKED = -1000000000.0 * LOG2E
LN2 = math.log(2.0)
SPLIT = ((0, 224), (224, 392))
MAIN = 384
LEFT = TOK - MAIN
VIRTUAL = 16
ROWS = 400
MIB = 1024 * 1024


def mm(a, b):
    return lax.dot_general(a, b, (((1,), (0,)), ((), ())), preferred_element_type=F32)


def mm_nt(a, b):
    return lax.dot_general(a, b, (((1,), (1,)), ((), ())), preferred_element_type=F32)


def mm_tn(a, b):
    return lax.dot_general(a, b, (((0,), (0,)), ((), ())), preferred_element_type=F32)


def standardized(values):
    center = values - jnp.mean(values, axis=-1, keepdims=True)
    rstd = lax.rsqrt(jnp.mean(center * center, axis=-1, keepdims=True) + 1e-05)
    return center * rstd, rstd


def tiles(block):
    return block.astype(F32).reshape(-1, C)


def own_lanes(j, block):
    lane = lax.broadcasted_iota(jnp.int32, block.shape, 1) // HD
    return jnp.where(lane == j, block, jnp.zeros_like(block))


def put_diagonal(ref, turned, pitch, column=0):
    for head in range(HEADS):
        at = pitch * (head % GROUP) + column
        ref[HD * head : HD * (head + 1), at : at + turned.shape[1]] = turned[HD * head : HD * (head + 1)]


def left_rows(block):
    rows = jnp.concatenate([block.astype(F32)] * HEADS, axis=0)
    row = lax.broadcasted_iota(jnp.int32, rows.shape, 0) // LEFT
    lane = lax.broadcasted_iota(jnp.int32, rows.shape, 1) // HD
    return jnp.where(row == lane, rows, 0.0)


def from_left(product):
    turned = product.T
    row = lax.broadcasted_iota(jnp.int32, turned.shape, 0) // LEFT
    lane = lax.broadcasted_iota(jnp.int32, turned.shape, 1) // HD
    return jnp.sum(jnp.where(row == lane, turned, 0.0).reshape(HEADS, LEFT, C), axis=0)


def pair_channels(g, pair):
    return pl.ds(pl.multiple_of(g * 128 + pair * 64, 64), 64)


def channels_of(g, first=0):
    return pl.ds(pl.multiple_of(g * 128 + first, 128), 128)


def head_channels(g, j):
    return pl.ds(pl.multiple_of(g * 128 + j * HD, HD), HD)


MESH = pl.DeviceIdType.MESH
ROUTES = ((-1, 0), (1, 0), (0, -1), (1, -1))


class Exchange:
    def __init__(self, way, send_sem, recv_sem):
        self.way, self.sems, self.copies = way, (send_sem, recv_sem), []

    def device(self, steps, sign):
        size = lax.axis_size("tm"), lax.axis_size("rows")
        here = lax.axis_index("tm"), lax.axis_index("rows")
        return tuple((i + sign * d + n) % n for i, d, n in zip(here, steps, size))

    def greet(self, ways):
        self.ways = ways
        for way in ways:
            for steps in ROUTES:
                pl.semaphore_signal(
                    pltpu.get_barrier_semaphore(),
                    inc=1,
                    device_id=self.device(steps, -way),
                    device_id_type=MESH,
                )

    def wait_for_others(self):
        pl.semaphore_wait(pltpu.get_barrier_semaphore(), len(self.ways) * len(ROUTES))

    def send(self, route, source, target, way=None):
        i = len(self.copies)
        copy = pltpu.make_async_remote_copy(
            src_ref=source,
            dst_ref=target,
            send_sem=self.sems[0].at[i],
            recv_sem=self.sems[1].at[i],
            device_id=self.device(ROUTES[route], way or self.way),
            device_id_type=MESH,
        )
        copy.start()
        self.copies.append(copy)

    def wait_for(self, numbers):
        for i in numbers:
            self.copies[i].wait_recv()

    def wait(self, arrived=()):
        for i, copy in enumerate(self.copies):
            copy.wait_send()
            if i not in arrived:
                copy.wait_recv()


def pieces_of(whole, w, pieces):
    own, ahead, behind, above, corner = pieces
    if w == 0:
        above[...] = whole[0:3, :, 0:4].astype(BF16)
        corner[...] = whole[0:3, :, 4:8].astype(BF16)
        ahead[0:4] = whole[3:7, :, 0:4].astype(BF16)
        own[0:4] = whole[3:7, :, 4:8].astype(BF16)
    else:
        ahead[4:7] = whole[0:3, :, 0:4].astype(BF16)
        own[4:7] = whole[0:3, :, 4:8].astype(BF16)
        behind[...] = whole[3:7, :, 4:8].astype(BF16)
        own[7:11] = whole[3:7, :, 0:4].astype(BF16)


def joined(low, high):
    return jnp.concatenate([low.astype(F32), high.astype(F32)], axis=2)


def forward_kernel(
    x_ref, cot_ref, gain_ref, bias_ref, wqkv_ref, wout_ref, mixt_ref, stat_ref, stat_left, *refs,
):
    y_own, y_ahead_there, y_behind, y_above_there, y_corner_there = refs[0:5]
    c_own, c_ahead_there, *c_later = refs[5:10]
    y_ahead, y_above, y_corner, c_ahead, qbd, k, vt, send_sem, recv_sem = refs[10:]
    exchange = Exchange(1, send_sem, recv_sem)
    exchange.greet((1,))
    for w in range(2):
        pieces_of(cot_ref[7 * w : 7 * w + 7].astype(F32), w, (c_own, c_ahead, *c_later))
    exchange.wait_for_others()
    exchange.send(0, c_ahead, c_ahead_there)
    qbd[...] = jnp.zeros_like(qbd)
    for w in range(2):
        rows = slice(7 * w, 7 * w + 7)
        x = tiles(x_ref[rows])
        xhat, _ = standardized(x)
        normed = (xhat * gain_ref[...] + bias_ref[...]).astype(BF16)
        queries = mm(normed, wqkv_ref[:, 0:C]) * QSCALE
        put_diagonal(qbd, queries[0:MAIN].astype(BF16).T, MAIN)
        k[...] = mm(normed, wqkv_ref[:, C : 2 * C]).astype(BF16)
        vt[...] = mm(normed, wqkv_ref[:, 2 * C :]).astype(BF16).T

        def group(g, carry):
            kg = k[:, channels_of(g)]
            for pair in range(2):
                lanes = slice(768 * pair, 768 * (pair + 1))
                scores = mm(kg, qbd[channels_of(g), lanes])
                top = jnp.max(scores, axis=0, keepdims=True)
                e = jnp.exp2(scores - top)
                sums = jnp.sum(e, axis=0, keepdims=True)
                mixed = mm(vt[pair_channels(g, pair), :], e.astype(BF16)) * (1.0 / sums)
                stat_ref[w, g, :, lanes] = top + jnp.log2(sums)
                for i in range(2):
                    mixt_ref[w, head_channels(g, 2 * pair + i), 0:MAIN] = mixed[
                        HD * i : HD * (i + 1), MAIN * i : MAIN * (i + 1)
                    ].astype(BF16)
            return carry

        lax.fori_loop(0, HEADS // GROUP, group, 0)
        scores = mm(k[...], left_rows(queries[MAIN:TOK]).astype(BF16).T)
        top = jnp.max(scores, axis=0, keepdims=True)
        e = jnp.exp2(scores - top)
        sums = jnp.sum(e, axis=0, keepdims=True)
        stat_left[w] = top + jnp.log2(sums)
        mixed = from_left(mm(vt[...], e.astype(BF16)) * (1.0 / sums))
        mixt_ref[w, :, MAIN:512] = jnp.concatenate(
            [mixed, jnp.zeros((128 - LEFT, C), F32)], axis=0
        ).T.astype(BF16)
        y = x + mm_tn(mixt_ref[w, :, 0:TOK], wout_ref[...])
        pieces_of(y.reshape(7, 7, 8, C), w, (y_own, y_ahead, y_behind, y_above, y_corner))
        if w == 0:
            exchange.send(2, y_above, y_above_there)
            exchange.send(3, y_corner, y_corner_there)
            exchange.send(0, y_ahead.at[0:4], y_ahead_there.at[0:4])
        else:
            exchange.send(0, y_ahead.at[4:7], y_ahead_there.at[4:7])
    exchange.wait()


def write_part(turn, block, part):
    def layer(z, carry):
        for xy in range(16):
            x, y = xy // 4, xy % 4
            rows = pl.ds(pl.multiple_of((z * 16 + x // 2 * 8 + y * 2 + x % 2) * 8, 8), 8)
            values = block[rows, :]
            first = jnp.where(turn == 0, x, jnp.where(turn == 1, y, z))
            second = jnp.where(turn == 0, y, jnp.where(turn == 1, z, x))
            third = jnp.where(turn == 0, z, jnp.where(turn == 1, x, y))
            part[0, first, second, third] = values[0:4].astype(BF16)
            part[1, first, second, third] = values[4:8].astype(BF16)
        return carry

    lax.fori_loop(0, 4, layer, 0)


def group_gradients(scale, g, turn, normed_t, dproj, mixt, cot_b, block, part):
    block[:, 0:384] = mm(normed_t[...], dproj[:, columns_of(g)]) * scale
    block[:, 384:512] = mm(mixt[...], cot_b[:, channels_of(g)]) * scale
    write_part(turn, block, part)


def columns_of(g):
    return pl.ds(pl.multiple_of(g * 384, 128), 384)


def sort_columns(sorted_ref, wqkv_ref):
    for g in range(HEADS // GROUP):
        for i in range(3):
            sorted_ref[:, 384 * g + 128 * i : 384 * g + 128 * (i + 1)] = wqkv_ref[
                :, C * i + 128 * g : C * i + 128 * (g + 1)
            ]


def norm_backward(dnormed, xhat, rstd, gain):
    d = dnormed.astype(BF16).astype(F32) * gain
    return rstd * (
        d
        - jnp.mean(d, axis=-1, keepdims=True)
        - xhat * jnp.mean(d * xhat, axis=-1, keepdims=True)
    )


def coordinates():
    tm, rows = lax.axis_index("tm"), lax.axis_index("rows")
    return {
        "x": tm // 4 % 2 * 2 + rows // 2,
        "y": tm % 4,
        "z": tm // 8,
        "core": rows % 2,
    }


def device_at(place):
    tm = place["z"] * 8 + place["x"] // 2 * 4 + place["y"]
    return (tm, place["x"] % 2 * 2 + place["core"])


def beside(here, axis, steps):
    return device_at({**here, axis: (here[axis] + steps) % (2 if axis == "core" else 4)})


ORDERS = ("xyz", "yzx", "zxy")


class Reduction:
    def __init__(self, order, plane, here, partners, part, local_sem, buffers, sems):
        self.plane = plane
        self.order, self.here, self.partners, self.part = order, here, partners, part
        self.held, self.other, *self.slots = buffers
        self.local_sem, self.sems = local_sem, sems

    def remote(self, number, source, target, partner):
        return pltpu.make_async_remote_copy(
            src_ref=source,
            dst_ref=target,
            send_sem=self.sems[0].at[number],
            recv_sem=self.sems[1].at[number],
            device_id=partner,
            device_id_type=MESH,
        )

    def local_copy(self):
        return pltpu.make_async_copy(self.part.at[self.here["core"]], self.held, self.local_sem)

    def core_copy(self):
        return self.remote(0, self.part.at[1 - self.here["core"]], self.other, self.partners["core", 1])

    def source(self, step):
        return self.held if step == 0 else self.slots[step - 1].at[3]

    def axis_copies(self, step):
        axis = self.order[step]
        return [
            self.remote(
                3 * step + away,
                self.source(step).at[(self.here[axis] + away) % 4],
                self.slots[step].at[away - 1],
                self.partners[axis, away],
            )
            for away in (1, 2, 3)
        ]

    def plane_copies(self):
        a, b = self.order[1:]
        copies = []
        for i in range(1, 16):
            da, db = i // 4, i % 4
            partner = (b, db) if da == 0 else (a, da) if db == 0 else (a, b, da, db)
            block = self.source(1).at[(self.here[a] + da) % 4, (self.here[b] + db) % 4]
            copies.append(self.remote(3 + i, block, self.slots[1].at[da, db], self.partners[partner]))
        return copies

    def copies(self, step):
        return self.plane_copies() if self.plane and step == 1 else self.axis_copies(step)

    def start(self):
        self.core_copy().start()

    def advance(self, stage, out=None):
        if stage == 0:
            self.core_copy().wait_recv()
            if self.local_sem is not None:
                self.local_copy().wait()
                own = self.held
            else:
                own = self.part.at[self.here["core"]]
            for i in range(4):
                self.held[i] = (own[i].astype(F32) + self.other[i].astype(F32)).astype(BF16)
        else:
            for copy in self.copies(stage - 1):
                copy.wait_recv()
            total = self.source(stage - 1)[self.here[self.order[stage - 1]]].astype(F32)
            if self.plane and stage == 2:
                a, b = self.order[1:]
                total = self.source(1)[self.here[a], self.here[b]].astype(F32)
                for i in range(1, 16):
                    total = total + self.slots[1][i // 4, i % 4].astype(F32)
                out(total)
                return
            for slot in range(3):
                total = total + self.slots[stage - 1][slot].astype(F32)
            if stage == 3:
                out(total)
                return
            self.slots[stage - 1][3] = total.astype(BF16)
        for copy in self.copies(stage):
            copy.start()

    def finish(self):
        self.core_copy().wait_send()
        for step in range(2 if self.plane else 3):
            for copy in self.copies(step):
                copy.wait_send()


JOBS = HEADS // GROUP


def backward_first_kernel(
    scale,
    x_ref, gain_ref, bias_ref, wqkv_ref, wout_ref, mixt_ref, stat_ref, stat_left,
    own, ahead, behind, above, corner, parts_second,
    grad_ref, gqkv1, gout1, gqkv2, gout2,
    normed_t, dproj, cot_b, mixt_all, wsorted, block, parts_first,
    qbd, k, kt, v, qn, don, dobd, p_s, ds_s, dqt, do_rows, q_rows, cot_s, xhat_s, rstd_s,
    dk_left, dv_left, dq_left, held, other, slots_a, slots_b, slots_c, local_sem, send_sem, recv_sem,
):
    here = coordinates()
    partners = {("core", 1): beside(here, "core", 1)}
    for axis in "xyz":
        for away in (1, 2, 3):
            partners[axis, away] = beside(here, axis, away)
    for dy in (1, 2, 3):
        for dz in (1, 2, 3):
            partners["y", "z", dy, dz] = device_at(
                {**here, "y": (here["y"] + dy) % 4, "z": (here["z"] + dz) % 4}
            )
    barrier = pltpu.get_barrier_semaphore()
    for partner in partners.values():
        pl.semaphore_signal(barrier, inc=1, device_id=partner, device_id_type=MESH)

    def job(i):
        of_first = i < JOBS
        g = i % JOBS
        return Reduction(
            ORDERS[0] if of_first else ORDERS[g % 3],
            of_first,
            here,
            partners,
            parts_first.at[g] if of_first else parts_second.at[g],
            None if of_first else local_sem.at[g],
            [ref.at[i] for ref in (held, other, slots_a, slots_b, slots_c)],
            (send_sem.at[i], recv_sem.at[i]),
        )

    def result(i):
        gqkv, gout = (gqkv1, gout1) if i < JOBS else (gqkv2, gout2)
        g = i % JOBS

        def out(total):
            for part in range(3):
                at = C * part + 128 * g
                gqkv[:, at : at + 128] = total[:, 128 * part : 128 * (part + 1)]
            gout[:, 128 * g : 128 * (g + 1)] = total[:, 384:512]

        return out

    first, second = [job(i) for i in range(JOBS)], [job(JOBS + i) for i in range(JOBS)]
    for reduction in second:
        reduction.local_copy().start()
    for ref in (qbd, dobd, do_rows, q_rows, normed_t, dproj, cot_b):
        ref[...] = jnp.zeros_like(ref)
    sort_columns(wsorted, wqkv_ref)
    for w in range(2):
        xhat, rstd = standardized(tiles(x_ref[7 * w : 7 * w + 7]))
        xhat_s[w] = xhat
        rstd_s[w] = rstd
        normed = (xhat * gain_ref[...] + bias_ref[...]).astype(BF16)
        normed_t[:, 512 * w : 512 * w + TOK] = normed.T
        queries = (mm(normed, wqkv_ref[:, 0:C]) * QSCALE).astype(BF16)
        qn[w] = queries
        put_diagonal(qbd.at[w], queries[0:MAIN].T, MAIN)
        keys = mm(normed, wqkv_ref[:, C : 2 * C]).astype(BF16)
        k[w] = keys
        kt[w] = keys.T
        v[w] = mm(normed, wqkv_ref[:, 2 * C :]).astype(BF16)
        if w == 0:
            pieces = [joined(above[...], corner[...]), joined(ahead[0:4], own[0:4])]
        else:
            pieces = [joined(ahead[4:7], own[4:7]), joined(own[7:11], behind[...])]
        cot = jnp.concatenate([piece.reshape(-1, C) for piece in pieces], axis=0)
        cot_s[w] = cot
        cot_h = cot.astype(BF16)
        cot_b[512 * w : 512 * w + TOK] = cot_h
        dmixed = mm_nt(cot_h, wout_ref[...]).astype(BF16)
        don[w] = dmixed
        put_diagonal(dobd.at[w], dmixed[0:MAIN].T, MAIN)
        mixt_all[:, 512 * w : 512 * (w + 1)] = mixt_ref[w]
        q_left = left_rows(queries[MAIN:TOK]).astype(BF16)
        do_left = left_rows(dmixed[MAIN:TOK])
        mixed = mixt_ref[w, :, MAIN:512].astype(F32).T[0:LEFT]
        dsum = jnp.sum((do_left * jnp.concatenate([mixed] * HEADS, axis=0)).T, axis=0, keepdims=True)
        do_left = do_left.astype(BF16)
        p = jnp.exp2(mm(k[w], q_left.T) - stat_left[w])
        ds = (p * (mm(v[w], do_left.T) - dsum)).astype(BF16)
        dv_left[w] = mm(p.astype(BF16), do_left)
        dk_left[w] = mm(ds, q_left)
        dq_left[w] = from_left(mm(kt[w], ds))
        if w == 0:
            pl.semaphore_wait(barrier, len(partners))
            for reduction in second:
                reduction.start()

    def group(g, carry):
        for w in range(2):
            kg = k[w, :, channels_of(g)]
            vg = v[w, :, channels_of(g)]
            qg = qn[w, :, channels_of(g)]
            dog = don[w, :, channels_of(g)]
            for j in range(GROUP):
                do_rows[w, MAIN * j : MAIN * (j + 1)] = own_lanes(j, dog[0:MAIN])
                q_rows[w, MAIN * j : MAIN * (j + 1)] = own_lanes(j, qg[0:MAIN])
            for pair in range(2):
                lanes = slice(768 * pair, 768 * (pair + 1))
                scores = mm(kg, qbd[w, channels_of(g), lanes])
                p = jnp.exp2(scores - stat_ref[w, g, :, lanes]).astype(BF16)
                p_s[w, :, lanes] = p
                dsums = []
                for j in (2 * pair, 2 * pair + 1):
                    dsums.append(
                        jnp.sum(
                            mixt_ref[w, head_channels(g, j), 0:MAIN].astype(F32)
                            * dobd[w, head_channels(g, j), MAIN * j : MAIN * (j + 1)].astype(F32),
                            axis=0, keepdims=True,
                        )
                    )
                dp = mm(vg, dobd[w, channels_of(g), lanes]) - jnp.concatenate(dsums, axis=1)
                ds = (p.astype(F32) * dp).astype(BF16)
                ds_s[w, :, lanes] = ds
                dq = mm(kt[w, pair_channels(g, pair), :], ds)
                for i in range(2):
                    j = 2 * pair + i
                    dqt[w, HD * j : HD * (j + 1), :] = dq[HD * i : HD * (i + 1), MAIN * i : MAIN * (i + 1)]
            dk = (mm(ds_s[w], q_rows[w]) + dk_left[w, :, channels_of(g)]) * LN2
            dv = mm(p_s[w], do_rows[w]) + dv_left[w, :, channels_of(g)]
            dq = jnp.concatenate([dqt[w].T, dq_left[w, :, channels_of(g)]], axis=0) * HD ** (-0.5)
            dproj[512 * w : 512 * w + TOK, columns_of(g)] = jnp.concatenate(
                [dq.astype(BF16), dk.astype(BF16), dv.astype(BF16)], axis=1
            )
        group_gradients(scale, g, 0, normed_t, dproj, mixt_all, cot_b, block, parts_first.at[g])
        for now in range(JOBS):

            @pl.when(g == now)
            def _():
                first[now].start()
                for i in range(JOBS):
                    second[i].advance(now, result(JOBS + i))
                for i in range(now):
                    first[i].advance(now - 1 - i, result(i))

        return carry

    lax.fori_loop(0, JOBS, group, 0)
    for now in range(JOBS, 2 * JOBS - 1):
        w = now - JOBS
        if w < 2:
            dnormed = mm_nt(dproj[512 * w : 512 * w + TOK], wsorted[...])
            total = cot_s[w] + norm_backward(dnormed, xhat_s[w], rstd_s[w], gain_ref[...])
            grad_ref[7 * w : 7 * w + 7] = total.reshape(7, 7, 8, C).astype(BF16)
        for i in range(JOBS):
            if 0 <= now - 1 - i <= 2:
                first[i].advance(now - 1 - i, result(i))
    for reduction in first + second:
        reduction.finish()


def second_kernel(
    scale,
    y_own, y_ahead, y_behind_here, y_above, y_corner, c_own, c_ahead, c_behind_here, c_above_here, c_corner_here,
    gain_ref, bias_ref, wqkv_ref, wout_ref,
    own, ahead_there, behind_there, above_there, corner_there, parts,
    normed_t, dproj, cot_b, mixt, wsorted, block, qbd, k, kt, v, vt, qn, dot_s, dobd, dopt, dqt,
    e_a, e_b, ds_a, ds_b, do_rows, q_rows, pen, cot_s, xhat_s,
    ahead, behind, above, corner, c_behind, c_above, c_corner, y_behind, send_sem, recv_sem,
):
    exchange = Exchange(-1, send_sem, recv_sem)
    exchange.greet((1, -1))
    e_s, ds_s = (e_a, e_b), (ds_a, ds_b)
    for ref in (qbd, dobd, do_rows, q_rows, normed_t, dproj, cot_b, mixt):
        ref[...] = jnp.zeros_like(ref)
    sort_columns(wsorted, wqkv_ref)
    for w in range(2):
        base = 512 * w
        last_frames = lax.axis_index("tm") == (lax.axis_size("tm") - 1 if w == 0 else 0)
        last_rows = (lax.axis_index("rows") == lax.axis_size("rows") - 1) if w == 1 else False

        def region_of(token, segment):
            columns = 4 if segment == 0 else 3
            late = jnp.where(last_frames & (token % 8 < 4), 1, 0)
            below = jnp.where(last_rows & (token // 8 // columns >= 4), 2, 0)
            return late + below

        def gather(into, own, ahead, behind, above, corner):
            def put(rho, count, whole):
                into[32 * rho : 32 * (rho + count)] = whole[:, 3:7].reshape(-1, C)
                into[224 + 24 * rho : 224 + 24 * (rho + count)] = whole[:, 0:3].reshape(-1, C)

            if w == 0:
                put(0, 7, joined(ahead[...], own[0:7]))
            else:
                put(0, 4, joined(own[7:11], behind[...]))
                put(4, 3, joined(above[...], corner[...]))

        if w == 1:
            exchange.wait_for((0, 1, 2, 3))
        gather(xhat_s, y_own, y_ahead, y_behind, y_above, y_corner)
        gather(cot_s, c_own, c_ahead, c_behind, c_above, c_corner)
        xhat, rstd = standardized(xhat_s[...])
        xhat_s[...] = xhat
        normed = (xhat * gain_ref[...] + bias_ref[...]).astype(BF16)
        normed_t[:, base : base + TOK] = normed.T
        queries = (mm(normed, wqkv_ref[:, 0:C]) * QSCALE).astype(BF16)
        qn[...] = queries
        keys = mm(normed, wqkv_ref[:, C : 2 * C]).astype(BF16)
        k[...] = keys
        values_f = mm(normed, wqkv_ref[:, 2 * C :])
        values = values_f.astype(BF16)
        v[...] = values
        cot_h = cot_s[...].astype(BF16)
        dmixed = mm_nt(cot_h, wout_ref[...]).astype(BF16)
        for s, (start, stop) in enumerate(SPLIT):
            count = stop - start
            cot_b[512 * w + 256 * s : 512 * w + 256 * s + count] = cot_h[start:stop]
            put_diagonal(qbd, queries[start:stop].T, 256, 1024 * s)
            kt[:, 256 * s : 256 * s + count] = keys[start:stop].T
            dot_s[:, 256 * s : 256 * s + count] = dmixed[start:stop].T
            turned = values[start:stop].T
            vt[:, 256 * s : 256 * s + count] = turned
            total = jnp.sum(turned.astype(F32), axis=1, keepdims=True)
            other = 1 - s
            lane = 256 * other + SPLIT[other][1] - SPLIT[other][0]
            first = lax.broadcasted_iota(jnp.int32, (C, VIRTUAL), 1) == 0
            vt[:, lane : lane + VIRTUAL] = jnp.where(first, total, 0.0).astype(BF16)
            shape = (count, 256)
            key = region_of(lax.broadcasted_iota(jnp.int32, shape, 0), s)
            query = region_of(lax.broadcasted_iota(jnp.int32, shape, 1), s)
            pen[start:stop] = jnp.where(key == query, 0.0, 1.0)

        if w == 0:
            exchange.wait_for_others()
            exchange.send(1, y_behind_here, y_behind, 1)
            exchange.send(1, c_behind_here, c_behind, 1)
            exchange.send(2, c_above_here, c_above, 1)
            exchange.send(3, c_corner_here, c_corner, 1)

        def group(g, carry):
            virtual_dv = []
            grads = []
            for s, (start, stop) in enumerate(SPLIT):
                count = stop - start
                kg = k[start:stop, channels_of(g)]
                apart = pen[start:stop] > 0.5
                sums_of, invs = [], []
                for j in range(GROUP):
                    lanes = slice(256 * j, 256 * (j + 1))
                    scores = mm(kg, qbd[channels_of(g), 1024 * s + 256 * j : 1024 * s + 256 * (j + 1)])
                    scores = jnp.where(apart, MASKED, scores)
                    top = jnp.maximum(jnp.max(scores, axis=0, keepdims=True), MASKED)
                    e = jnp.exp2(scores - top)
                    e_s[s][0:count, lanes] = e.astype(BF16)
                    rest = jnp.exp2(MASKED - top)
                    first = lax.broadcasted_iota(jnp.int32, (VIRTUAL, 256), 0) == 0
                    e_s[s][count : count + VIRTUAL, lanes] = jnp.where(first, rest, 0.0).astype(BF16)
                    invs.append(1.0 / (jnp.sum(e, axis=0, keepdims=True) + (TOK - count) * rest))
                for j in range(GROUP):
                    lanes = slice(256 * j, 256 * (j + 1))
                    tokens = slice(256 * s, 256 * (s + 1))
                    inv = invs[j]
                    mixed = inv * mm(
                        vt[head_channels(g, j), 256 * s : 256 * s + count + VIRTUAL], e_s[s][:, lanes]
                    )
                    mixt[head_channels(g, j), 512 * w + 256 * s : 512 * w + 256 * s + count] = mixed[
                        :, 0:count
                    ].astype(BF16)
                    do = dot_s[head_channels(g, j), tokens].astype(F32) * inv
                    inside = lax.broadcasted_iota(jnp.int32, do.shape, 1) < count
                    do = jnp.where(inside, do, 0.0).astype(BF16)
                    sums_of.append(jnp.sum(mixed * do.astype(F32), axis=0, keepdims=True))
                    dopt[HD * j : HD * (j + 1), tokens] = do
                    dobd[HD * j : HD * (j + 1), 1024 * s + 256 * j : 1024 * s + 256 * (j + 1)] = do
                turned = dopt[:, 256 * s : 256 * (s + 1)].T
                qg = qn[start:stop, channels_of(g)]
                for j in range(GROUP):
                    lanes = slice(256 * j, 256 * (j + 1))
                    at = 1024 * s + 256 * j
                    do_rows[at : at + 256] = own_lanes(j, turned)
                    q_rows[at : at + count] = own_lanes(j, qg)
                    dp = mm(v[start:stop, channels_of(g)], dobd[:, at : at + 256]) - sums_of[j]
                    ds = e_s[s][0:count, lanes].astype(F32) * jnp.where(apart, 0.0, dp)
                    ds = ds.astype(BF16)
                    ds_s[s][:, lanes] = ds
                    dq = mm(kt[head_channels(g, j), 256 * s : 256 * s + count], ds)
                    dqt[HD * j : HD * (j + 1), 256 * s : 256 * (s + 1)] = (dq * HD ** (-0.5)).astype(BF16)
                block = slice(1024 * s, 1024 * (s + 1))
                dv = mm(e_s[s][...], do_rows[block])
                dk = mm(ds_s[s][...], q_rows[block]) * LN2
                virtual_dv.append(dv[count : count + 1])
                grads.append((dk, dv[0:count]))
            for s, (start, stop) in enumerate(SPLIT):
                rows = slice(base + start, base + stop)
                dk, dv = grads[s]
                dproj[rows, columns_of(g)] = jnp.concatenate(
                    [
                        dqt[:, 256 * s : 256 * s + stop - start].T,
                        dk.astype(BF16),
                        (dv + virtual_dv[1 - s]).astype(BF16),
                    ],
                    axis=1,
                )
            return carry

        lax.fori_loop(0, HEADS // GROUP, group, 0)
        dnormed = mm_nt(dproj[base : base + TOK], wsorted[...])
        total = cot_s[...] + norm_backward(dnormed, xhat_s[...], rstd, gain_ref[...])
        whole = jnp.concatenate(
            [total[224:392].reshape(7, 3, 8, C), total[0:224].reshape(7, 4, 8, C)], axis=1
        )
        low, high = whole[:, :, 0:4].astype(BF16), whole[:, :, 4:8].astype(BF16)
        if w == 0:
            ahead[...] = low
            own[0:7] = high
            exchange.send(0, ahead, ahead_there)
        else:
            own[7:11] = low[0:4]
            behind[...] = high[0:4]
            above[...] = low[4:7]
            corner[...] = high[4:7]
            exchange.send(1, behind, behind_there)
            exchange.send(2, above, above_there)
            exchange.send(3, corner, corner_there)

    def gradients(g, carry):
        group_gradients(scale, g, g % 3, normed_t, dproj, mixt, cot_b, block, parts.at[g])
        return carry

    lax.fori_loop(0, JOBS, gradients, 0)
    exchange.wait((0, 1, 2, 3))


def piece_shapes():
    return [(rows, 7, 4, C) for rows in (11, 7, 4, 3, 3)]


PARTS = [(JOBS, 2, 4, 4, 4, 4, 512)]
SAVED = [
    jax.ShapeDtypeStruct((2, C, 512), BF16),
    jax.ShapeDtypeStruct((2, HEADS // GROUP, 1, 4 * MAIN), F32),
    jax.ShapeDtypeStruct((2, 1, 128), F32),
]
TOKENS = (14, 7, 8, C)
IN_VMEM = pl.BlockSpec(memory_space=pltpu.VMEM)


ANYWHERE = pl.BlockSpec(memory_space=pl.ANY)


def call(
    kernel, name, args, out_shape, scratch, vmem, there=(), far=(), semaphores=(), collective_id=None
):
    return pl.pallas_call(
        kernel,
        in_specs=[ANYWHERE if i in far else IN_VMEM for i in range(len(args))],
        out_specs=[ANYWHERE if i in there else IN_VMEM for i in range(len(out_shape))],
        out_shape=out_shape,
        scratch_shapes=[pltpu.VMEM(shape, dtype) for shape, dtype in scratch]
        + [pltpu.SemaphoreType.DMA(shape) for shape in semaphores],
        compiler_params=pltpu.CompilerParams(
            vmem_limit_bytes=vmem * MIB,
            has_side_effects=collective_id is not None,
            collective_id=collective_id,
        ),
        name=name,
    )(*args)


def halves(shapes):
    return [jax.ShapeDtypeStruct(shape, BF16) for shape in shapes]


def forward_first(x, cot, weights):
    pieces = piece_shapes()
    outs = call(
        forward_kernel,
        "forward_first",
        (x, cot, *weights),
        SAVED + halves(pieces * 2),
        [(shape, BF16) for shape in (pieces[1], *pieces[3:], pieces[1])]
        + [((C, 4 * MAIN), BF16), ((TOK, C), BF16), ((C, TOK), BF16)],
        vmem=20,
        there=(4, 6, 7, 9),
        semaphores=[(5,)] * 2,
        collective_id=1,
    )
    return outs[:3], outs[3:8], outs[8:]


GRADIENT_SCRATCH = [
    ((C, 1024), BF16), ((1024, 3 * C), BF16), ((1024, C), BF16), ((C, 1024), BF16), ((C, 3 * C), BF16), ((C, C), F32),
]


def backward_first(scale, x, weights, saved, pieces, parts):
    both = 2 * JOBS
    args = (x, *weights, *saved, *pieces, parts)
    return call(
        functools.partial(backward_first_kernel, scale),
        "backward_first",
        args,
        halves([TOKENS]) + [jax.ShapeDtypeStruct((4, width), F32) for width in (3 * C, C)] * 2,
        GRADIENT_SCRATCH
        + [(PARTS[0], BF16)]
        + [
            ((2, C, 4 * MAIN), BF16), ((2, TOK, C), BF16), ((2, C, TOK), BF16), ((2, TOK, C), BF16),
            ((2, TOK, C), BF16), ((2, TOK, C), BF16), ((2, C, 4 * MAIN), BF16),
            ((2, TOK, 4 * MAIN), BF16), ((2, TOK, 4 * MAIN), BF16), ((2, 128, MAIN), F32),
            ((2, 4 * MAIN, 128), BF16), ((2, 4 * MAIN, 128), BF16),
            ((2, TOK, C), F32), ((2, TOK, C), F32), ((2, TOK, 1), F32),
            ((2, TOK, C), F32), ((2, TOK, C), F32), ((2, LEFT, C), F32),
        ]
        + [((both, 4, 4, 4, 4, 512), BF16)] * 3
        + [((both, 4, 4, 4, 512), BF16), ((both, 4, 4, 512), BF16)],
        vmem=46,
        far=(len(args) - 1,),
        semaphores=[(JOBS,), (both, 19), (both, 19)],
        collective_id=3,
    )


def hand_on_kernel(*refs):
    for source, target in zip(refs[:5], refs[5:]):
        target[...] = source[...]


def handed_on(outs):
    return call(
        hand_on_kernel,
        "hand_on",
        outs,
        [jax.ShapeDtypeStruct(out.shape, out.dtype) for out in outs],
        [],
        vmem=8,
    )


def second_block(scale, y_pieces, c_pieces, weights):
    return call(
        functools.partial(second_kernel, scale),
        "second_block",
        (*y_pieces, *c_pieces, *weights),
        halves(piece_shapes() + PARTS),
        GRADIENT_SCRATCH
        + [
            ((C, 2048), BF16), ((TOK, C), BF16), ((C, 512), BF16), ((TOK, C), BF16),
            ((C, 512), BF16), ((TOK, C), BF16), ((C, 512), BF16),
            ((128, 2048), BF16), ((128, 512), BF16), ((128, 512), BF16),
            ((224 + VIRTUAL, 1024), BF16), ((168 + VIRTUAL, 1024), BF16),
            ((224, 1024), BF16), ((168, 1024), BF16),
            ((2048, 128), BF16), ((2048, 128), BF16),
            ((TOK, 256), F32), ((TOK, C), F32), ((TOK, C), F32),
        ]
        + [(shape, BF16) for shape in piece_shapes()[1:] + piece_shapes()[2:] + piece_shapes()[2:3]],
        vmem=28,
        there=range(1, 5),
        semaphores=[(8,)] * 2,
        collective_id=2,
    )


def per_device(
    video_clip, cotangent,
    gain_first, bias_first, qkv_first, out_first,
    gain_second, bias_second, qkv_second, out_second,
):
    frames, rows_here, columns, channels = video_clip.shape
    devices = lax.axis_size("tm") * lax.axis_size("rows")
    scale = 1.0 / math.sqrt(frames * rows_here * columns * devices)
    x = video_clip.transpose(1, 2, 0, 3)
    cot = cotangent.transpose(1, 2, 0, 3)
    first = (gain_first.reshape(1, C), bias_first.reshape(1, C), qkv_first, out_first)
    second = (gain_second.reshape(1, C), bias_second.reshape(1, C), qkv_second, out_second)
    saved, y_pieces, c_pieces = forward_first(x, cot, first)
    *d_pieces, parts = second_block(scale, y_pieces, c_pieces, second)
    grad, *sums = handed_on(backward_first(scale, x, first, saved, d_pieces, parts))
    return (grad.transpose(2, 0, 1, 3), *sums)


def solution(mesh):
    clip = P("tm", "rows", None, None)
    scattered = P(("tm", "rows"), None)
    return jax.shard_map(
        per_device,
        mesh=mesh,
        in_specs=(clip, clip) + (P(),) * 8,
        out_specs=(clip,) + (scattered,) * 4,
        check_vma=False,
    )
```

```python
import functools
import math

import jax
import jax.numpy as jnp
from jax import lax
from jax.experimental import pallas as pl
from jax.experimental.pallas import tpu as pltpu
from jax.sharding import PartitionSpec as P

F32, BF16 = jnp.float32, jnp.bfloat16
C, HEADS, HD = 512, 16, 32
TOK = 392
GROUP = 4
LOG2E = math.log2(math.e)
QSCALE = HD ** (-0.5) * LOG2E
MASKED = -1000000000.0 * LOG2E
LN2 = math.log(2.0)
SPLIT = ((0, 224), (224, 392))
MAIN = 384
LEFT = TOK - MAIN
VIRTUAL = 16
ROWS = 400
MIB = 1024 * 1024


def mm(a, b):
    return lax.dot_general(a, b, (((1,), (0,)), ((), ())), preferred_element_type=F32)


def mm_nt(a, b):
    return lax.dot_general(a, b, (((1,), (1,)), ((), ())), preferred_element_type=F32)


def mm_tn(a, b):
    return lax.dot_general(a, b, (((0,), (0,)), ((), ())), preferred_element_type=F32)


def standardized(values):
    center = values - jnp.mean(values, axis=-1, keepdims=True)
    rstd = lax.rsqrt(jnp.mean(center * center, axis=-1, keepdims=True) + 1e-05)
    return center * rstd, rstd


def tiles(block):
    return block.astype(F32).reshape(-1, C)


def own_lanes(j, block):
    lane = lax.broadcasted_iota(jnp.int32, block.shape, 1) // HD
    return jnp.where(lane == j, block, jnp.zeros_like(block))


def put_diagonal(ref, turned, pitch, column=0):
    for head in range(HEADS):
        at = pitch * (head % GROUP) + column
        ref[HD * head : HD * (head + 1), at : at + turned.shape[1]] = turned[HD * head : HD * (head + 1)]


def left_rows(block):
    rows = jnp.concatenate([block.astype(F32)] * HEADS, axis=0)
    row = lax.broadcasted_iota(jnp.int32, rows.shape, 0) // LEFT
    lane = lax.broadcasted_iota(jnp.int32, rows.shape, 1) // HD
    return jnp.where(row == lane, rows, 0.0)


def from_left(product):
    turned = product.T
    row = lax.broadcasted_iota(jnp.int32, turned.shape, 0) // LEFT
    lane = lax.broadcasted_iota(jnp.int32, turned.shape, 1) // HD
    return jnp.sum(jnp.where(row == lane, turned, 0.0).reshape(HEADS, LEFT, C), axis=0)


def pair_channels(g, pair):
    return pl.ds(pl.multiple_of(g * 128 + pair * 64, 64), 64)


def channels_of(g, first=0):
    return pl.ds(pl.multiple_of(g * 128 + first, 128), 128)


def head_channels(g, j):
    return pl.ds(pl.multiple_of(g * 128 + j * HD, HD), HD)


MESH = pl.DeviceIdType.MESH
ROUTES = ((-1, 0), (1, 0), (0, -1), (1, -1))


class Exchange:
    def __init__(self, way, send_sem, recv_sem):
        self.way, self.sems, self.copies = way, (send_sem, recv_sem), []

    def device(self, steps, sign):
        size = lax.axis_size("tm"), lax.axis_size("rows")
        here = lax.axis_index("tm"), lax.axis_index("rows")
        return tuple((i + sign * d + n) % n for i, d, n in zip(here, steps, size))

    def greet(self, ways):
        self.ways = ways
        for way in ways:
            for steps in ROUTES:
                pl.semaphore_signal(
                    pltpu.get_barrier_semaphore(),
                    inc=1,
                    device_id=self.device(steps, -way),
                    device_id_type=MESH,
                )

    def wait_for_others(self):
        pl.semaphore_wait(pltpu.get_barrier_semaphore(), len(self.ways) * len(ROUTES))

    def send(self, route, source, target, way=None):
        i = len(self.copies)
        copy = pltpu.make_async_remote_copy(
            src_ref=source,
            dst_ref=target,
            send_sem=self.sems[0].at[i],
            recv_sem=self.sems[1].at[i],
            device_id=self.device(ROUTES[route], way or self.way),
            device_id_type=MESH,
        )
        copy.start()
        self.copies.append(copy)

    def wait_for(self, numbers):
        for i in numbers:
            self.copies[i].wait_recv()

    def wait(self, arrived=()):
        for i, copy in enumerate(self.copies):
            copy.wait_send()
            if i not in arrived:
                copy.wait_recv()


def pieces_of(whole, w, pieces):
    own, ahead, behind, above, corner = pieces
    if w == 0:
        above[...] = whole[0:3, :, 0:4].astype(BF16)
        corner[...] = whole[0:3, :, 4:8].astype(BF16)
        ahead[0:4] = whole[3:7, :, 0:4].astype(BF16)
        own[0:4] = whole[3:7, :, 4:8].astype(BF16)
    else:
        ahead[4:7] = whole[0:3, :, 0:4].astype(BF16)
        own[4:7] = whole[0:3, :, 4:8].astype(BF16)
        behind[...] = whole[3:7, :, 4:8].astype(BF16)
        own[7:11] = whole[3:7, :, 0:4].astype(BF16)


def joined(low, high):
    return jnp.concatenate([low.astype(F32), high.astype(F32)], axis=2)


def forward_kernel(
    x_far, cot_far, gain_far, bias_far, wqkv_far, wout_far, mixt_ref, stat_ref, stat_left, *refs,
):
    y_own, y_ahead_there, y_behind, y_above_there, y_corner_there = refs[0:5]
    c_own, c_ahead_there, *c_later = refs[5:10]
    y_ahead, y_above, y_corner, c_ahead, qbd, k, vt = refs[10:17]
    x_ref, cot_ref, gain_ref, bias_ref, wqkv_ref, wout_ref, send_sem, recv_sem, load_sem = refs[17:]
    loads = []
    for far, near in (
        (cot_far, cot_ref), (x_far, x_ref), (gain_far, gain_ref), (bias_far, bias_ref),
        (wqkv_far, wqkv_ref), (wout_far, wout_ref),
    ):
        loads.append(pltpu.make_async_copy(far, near, load_sem.at[len(loads)]))
        loads[-1].start()
    exchange = Exchange(1, send_sem, recv_sem)
    exchange.greet((1,))
    qbd[...] = jnp.zeros_like(qbd)
    loads[0].wait()
    for w in range(2):
        pieces_of(cot_ref[7 * w : 7 * w + 7].astype(F32), w, (c_own, c_ahead, *c_later))
    exchange.wait_for_others()
    exchange.send(0, c_ahead, c_ahead_there)
    for load in loads[1:4]:
        load.wait()
    for w in range(2):
        rows = slice(7 * w, 7 * w + 7)
        x = tiles(x_ref[rows])
        xhat, _ = standardized(x)
        normed = (xhat * gain_ref[...] + bias_ref[...]).astype(BF16)
        if w == 0:
            for load in loads[4:]:
                load.wait()
        queries = mm(normed, wqkv_ref[:, 0:C]) * QSCALE
        put_diagonal(qbd, queries[0:MAIN].astype(BF16).T, MAIN)
        k[...] = mm(normed, wqkv_ref[:, C : 2 * C]).astype(BF16)
        vt[...] = mm(normed, wqkv_ref[:, 2 * C :]).astype(BF16).T

        def group(g, carry):
            kg = k[:, channels_of(g)]
            for pair in range(2):
                lanes = slice(768 * pair, 768 * (pair + 1))
                scores = mm(kg, qbd[channels_of(g), lanes])
                top = jnp.max(scores, axis=0, keepdims=True)
                e = jnp.exp2(scores - top)
                sums = jnp.sum(e, axis=0, keepdims=True)
                mixed = mm(vt[pair_channels(g, pair), :], e.astype(BF16)) * (1.0 / sums)
                stat_ref[w, g, :, lanes] = top + jnp.log2(sums)
                for i in range(2):
                    mixt_ref[w, head_channels(g, 2 * pair + i), 0:MAIN] = mixed[
                        HD * i : HD * (i + 1), MAIN * i : MAIN * (i + 1)
                    ].astype(BF16)
            return carry

        lax.fori_loop(0, HEADS // GROUP, group, 0)
        scores = mm(k[...], left_rows(queries[MAIN:TOK]).astype(BF16).T)
        top = jnp.max(scores, axis=0, keepdims=True)
        e = jnp.exp2(scores - top)
        sums = jnp.sum(e, axis=0, keepdims=True)
        stat_left[w] = top + jnp.log2(sums)
        mixed = from_left(mm(vt[...], e.astype(BF16)) * (1.0 / sums))
        mixt_ref[w, :, MAIN:512] = jnp.concatenate(
            [mixed, jnp.zeros((128 - LEFT, C), F32)], axis=0
        ).T.astype(BF16)
        y = x + mm_tn(mixt_ref[w, :, 0:TOK], wout_ref[...])
        pieces_of(y.reshape(7, 7, 8, C), w, (y_own, y_ahead, y_behind, y_above, y_corner))
        if w == 0:
            exchange.send(2, y_above, y_above_there)
            exchange.send(3, y_corner, y_corner_there)
            exchange.send(0, y_ahead.at[0:4], y_ahead_there.at[0:4])
        else:
            exchange.send(0, y_ahead.at[4:7], y_ahead_there.at[4:7])
    exchange.wait()


def write_part(turn, block, part):
    def layer(z, carry):
        for xy in range(16):
            x, y = xy // 4, xy % 4
            rows = pl.ds(pl.multiple_of((z * 16 + x // 2 * 8 + y * 2 + x % 2) * 8, 8), 8)
            values = block[rows, :]
            first = jnp.where(turn == 0, x, jnp.where(turn == 1, y, z))
            second = jnp.where(turn == 0, y, jnp.where(turn == 1, z, x))
            third = jnp.where(turn == 0, z, jnp.where(turn == 1, x, y))
            part[0, first, second, third] = values[0:4].astype(BF16)
            part[1, first, second, third] = values[4:8].astype(BF16)
        return carry

    lax.fori_loop(0, 4, layer, 0)


def group_gradients(scale, g, turn, normed_t, dproj, mixt, cot_b, block, part):
    block[:, 0:384] = mm(normed_t[...], dproj[:, columns_of(g)]) * scale
    block[:, 384:512] = mm(mixt[...], cot_b[:, channels_of(g)]) * scale
    write_part(turn, block, part)


def columns_of(g):
    return pl.ds(pl.multiple_of(g * 384, 128), 384)


def sort_columns(sorted_ref, wqkv_ref):
    for g in range(HEADS // GROUP):
        for i in range(3):
            sorted_ref[:, 384 * g + 128 * i : 384 * g + 128 * (i + 1)] = wqkv_ref[
                :, C * i + 128 * g : C * i + 128 * (g + 1)
            ]


def norm_backward(dnormed, xhat, rstd, gain):
    d = dnormed.astype(BF16).astype(F32) * gain
    return rstd * (
        d
        - jnp.mean(d, axis=-1, keepdims=True)
        - xhat * jnp.mean(d * xhat, axis=-1, keepdims=True)
    )


def coordinates():
    tm, rows = lax.axis_index("tm"), lax.axis_index("rows")
    return {
        "x": tm // 4 % 2 * 2 + rows // 2,
        "y": tm % 4,
        "z": tm // 8,
        "core": rows % 2,
    }


def device_at(place):
    tm = place["z"] * 8 + place["x"] // 2 * 4 + place["y"]
    return (tm, place["x"] % 2 * 2 + place["core"])


def beside(here, axis, steps):
    return device_at({**here, axis: (here[axis] + steps) % (2 if axis == "core" else 4)})


ORDERS = ("xyz", "yzx", "zxy")


class Reduction:
    def __init__(self, order, plane, here, partners, part, local_sem, buffers, sems):
        self.plane = plane
        self.order, self.here, self.partners, self.part = order, here, partners, part
        self.held, self.other, *self.slots = buffers
        self.local_sem, self.sems = local_sem, sems

    def remote(self, number, source, target, partner):
        return pltpu.make_async_remote_copy(
            src_ref=source,
            dst_ref=target,
            send_sem=self.sems[0].at[number],
            recv_sem=self.sems[1].at[number],
            device_id=partner,
            device_id_type=MESH,
        )

    def local_copy(self):
        return pltpu.make_async_copy(self.part.at[self.here["core"]], self.held, self.local_sem)

    def core_copy(self):
        return self.remote(0, self.part.at[1 - self.here["core"]], self.other, self.partners["core", 1])

    def source(self, step):
        return self.held if step == 0 else self.slots[step - 1].at[3]

    def axis_copies(self, step):
        axis = self.order[step]
        return [
            self.remote(
                3 * step + away,
                self.source(step).at[(self.here[axis] + away) % 4],
                self.slots[step].at[away - 1],
                self.partners[axis, away],
            )
            for away in (1, 2, 3)
        ]

    def plane_copies(self):
        a, b = self.order[1:]
        copies = []
        for i in range(1, 16):
            da, db = i // 4, i % 4
            partner = (b, db) if da == 0 else (a, da) if db == 0 else (a, b, da, db)
            block = self.source(1).at[(self.here[a] + da) % 4, (self.here[b] + db) % 4]
            copies.append(self.remote(3 + i, block, self.slots[1].at[da, db], self.partners[partner]))
        return copies

    def copies(self, step):
        return self.plane_copies() if self.plane and step == 1 else self.axis_copies(step)

    def start(self):
        self.core_copy().start()

    def advance(self, stage, out=None):
        if stage == 0:
            self.core_copy().wait_recv()
            if self.local_sem is not None:
                self.local_copy().wait()
                own = self.held
            else:
                own = self.part.at[self.here["core"]]
            for i in range(4):
                self.held[i] = (own[i].astype(F32) + self.other[i].astype(F32)).astype(BF16)
        else:
            for copy in self.copies(stage - 1):
                copy.wait_recv()
            total = self.source(stage - 1)[self.here[self.order[stage - 1]]].astype(F32)
            if self.plane and stage == 2:
                a, b = self.order[1:]
                total = self.source(1)[self.here[a], self.here[b]].astype(F32)
                for i in range(1, 16):
                    total = total + self.slots[1][i // 4, i % 4].astype(F32)
                out(total)
                return
            for slot in range(3):
                total = total + self.slots[stage - 1][slot].astype(F32)
            if stage == 3:
                out(total)
                return
            self.slots[stage - 1][3] = total.astype(BF16)
        for copy in self.copies(stage):
            copy.start()

    def finish(self):
        self.core_copy().wait_send()
        for step in range(2 if self.plane else 3):
            for copy in self.copies(step):
                copy.wait_send()


JOBS = HEADS // GROUP
SECOND_STAGES = {0: 0, 2: 1, 3: 2}


def backward_first_kernel(
    scale,
    x_ref, gain_ref, bias_ref, wqkv_ref, wout_ref, mixt_ref, stat_ref, stat_left,
    own, ahead, behind, above, corner, parts_second,
    grad_ref, gqkv1, gout1, gqkv2, gout2,
    normed_t, dproj, cot_b, mixt_all, wsorted, block, parts_first,
    qbd, k, kt, v, qn, don, dobd, p_s, ds_s, dqt, do_rows, q_rows, cot_s, xhat_s, rstd_s,
    dk_left, dv_left, dq_left, held, other, slots_a, slots_b, slots_c, local_sem, send_sem, recv_sem,
):
    here = coordinates()
    partners = {("core", 1): beside(here, "core", 1)}
    for axis in "xyz":
        for away in (1, 2, 3):
            partners[axis, away] = beside(here, axis, away)
    for dy in (1, 2, 3):
        for dz in (1, 2, 3):
            partners["y", "z", dy, dz] = device_at(
                {**here, "y": (here["y"] + dy) % 4, "z": (here["z"] + dz) % 4}
            )
    barrier = pltpu.get_barrier_semaphore()
    for partner in partners.values():
        pl.semaphore_signal(barrier, inc=1, device_id=partner, device_id_type=MESH)

    def job(i):
        of_first = i < JOBS
        g = i % JOBS
        return Reduction(
            ORDERS[0] if of_first else ORDERS[g % 3],
            of_first,
            here,
            partners,
            parts_first.at[g] if of_first else parts_second.at[g],
            None if of_first else local_sem.at[g],
            [ref.at[i] for ref in (held, other, slots_a, slots_b, slots_c)],
            (send_sem.at[i], recv_sem.at[i]),
        )

    def result(i):
        gqkv, gout = (gqkv1, gout1) if i < JOBS else (gqkv2, gout2)
        g = i % JOBS

        def out(total):
            for part in range(3):
                at = C * part + 128 * g
                gqkv[:, at : at + 128] = total[:, 128 * part : 128 * (part + 1)]
            gout[:, 128 * g : 128 * (g + 1)] = total[:, 384:512]

        return out

    first, second = [job(i) for i in range(JOBS)], [job(JOBS + i) for i in range(JOBS)]
    for reduction in second:
        reduction.local_copy().start()
    for ref in (qbd, dobd, do_rows, q_rows, normed_t, dproj, cot_b):
        ref[...] = jnp.zeros_like(ref)
    sort_columns(wsorted, wqkv_ref)
    for w in range(2):
        xhat, rstd = standardized(tiles(x_ref[7 * w : 7 * w + 7]))
        xhat_s[w] = xhat
        rstd_s[w] = rstd
        normed = (xhat * gain_ref[...] + bias_ref[...]).astype(BF16)
        normed_t[:, 512 * w : 512 * w + TOK] = normed.T
        queries = (mm(normed, wqkv_ref[:, 0:C]) * QSCALE).astype(BF16)
        qn[w] = queries
        put_diagonal(qbd.at[w], queries[0:MAIN].T, MAIN)
        keys = mm(normed, wqkv_ref[:, C : 2 * C]).astype(BF16)
        k[w] = keys
        kt[w] = keys.T
        v[w] = mm(normed, wqkv_ref[:, 2 * C :]).astype(BF16)
        if w == 0:
            pieces = [joined(above[...], corner[...]), joined(ahead[0:4], own[0:4])]
        else:
            pieces = [joined(ahead[4:7], own[4:7]), joined(own[7:11], behind[...])]
        cot = jnp.concatenate([piece.reshape(-1, C) for piece in pieces], axis=0)
        cot_s[w] = cot
        cot_h = cot.astype(BF16)
        cot_b[512 * w : 512 * w + TOK] = cot_h
        dmixed = mm_nt(cot_h, wout_ref[...]).astype(BF16)
        don[w] = dmixed
        put_diagonal(dobd.at[w], dmixed[0:MAIN].T, MAIN)
        mixt_all[:, 512 * w : 512 * (w + 1)] = mixt_ref[w]
        q_left = left_rows(queries[MAIN:TOK]).astype(BF16)
        do_left = left_rows(dmixed[MAIN:TOK])
        mixed = mixt_ref[w, :, MAIN:512].astype(F32).T[0:LEFT]
        dsum = jnp.sum((do_left * jnp.concatenate([mixed] * HEADS, axis=0)).T, axis=0, keepdims=True)
        do_left = do_left.astype(BF16)
        p = jnp.exp2(mm(k[w], q_left.T) - stat_left[w])
        ds = (p * (mm(v[w], do_left.T) - dsum)).astype(BF16)
        dv_left[w] = mm(p.astype(BF16), do_left)
        dk_left[w] = mm(ds, q_left)
        dq_left[w] = from_left(mm(kt[w], ds))
        if w == 0:
            pl.semaphore_wait(barrier, len(partners))
            for reduction in second:
                reduction.start()

    def group(g, carry):
        for w in range(2):
            kg = k[w, :, channels_of(g)]
            vg = v[w, :, channels_of(g)]
            qg = qn[w, :, channels_of(g)]
            dog = don[w, :, channels_of(g)]
            for j in range(GROUP):
                do_rows[w, MAIN * j : MAIN * (j + 1)] = own_lanes(j, dog[0:MAIN])
                q_rows[w, MAIN * j : MAIN * (j + 1)] = own_lanes(j, qg[0:MAIN])
            for pair in range(2):
                lanes = slice(768 * pair, 768 * (pair + 1))
                scores = mm(kg, qbd[w, channels_of(g), lanes])
                p = jnp.exp2(scores - stat_ref[w, g, :, lanes]).astype(BF16)
                p_s[w, :, lanes] = p
                dsums = []
                for j in (2 * pair, 2 * pair + 1):
                    dsums.append(
                        jnp.sum(
                            mixt_ref[w, head_channels(g, j), 0:MAIN].astype(F32)
                            * dobd[w, head_channels(g, j), MAIN * j : MAIN * (j + 1)].astype(F32),
                            axis=0, keepdims=True,
                        )
                    )
                dp = mm(vg, dobd[w, channels_of(g), lanes]) - jnp.concatenate(dsums, axis=1)
                ds = (p.astype(F32) * dp).astype(BF16)
                ds_s[w, :, lanes] = ds
                dq = mm(kt[w, pair_channels(g, pair), :], ds)
                for i in range(2):
                    j = 2 * pair + i
                    dqt[w, HD * j : HD * (j + 1), :] = dq[HD * i : HD * (i + 1), MAIN * i : MAIN * (i + 1)]
            dk = (mm(ds_s[w], q_rows[w]) + dk_left[w, :, channels_of(g)]) * LN2
            dv = mm(p_s[w], do_rows[w]) + dv_left[w, :, channels_of(g)]
            dq = jnp.concatenate([dqt[w].T, dq_left[w, :, channels_of(g)]], axis=0) * HD ** (-0.5)
            dproj[512 * w : 512 * w + TOK, columns_of(g)] = jnp.concatenate(
                [dq.astype(BF16), dk.astype(BF16), dv.astype(BF16)], axis=1
            )
        group_gradients(scale, g, 0, normed_t, dproj, mixt_all, cot_b, block, parts_first.at[g])
        for now in range(JOBS):

            @pl.when(g == now)
            def _():
                first[now].start()
                for i in range(JOBS):
                    if now in SECOND_STAGES:
                        second[i].advance(SECOND_STAGES[now])
                for i in range(now):
                    first[i].advance(now - 1 - i, result(i))

        return carry

    lax.fori_loop(0, JOBS, group, 0)
    for now in range(JOBS, 2 * JOBS - 1):
        w = now - JOBS
        if w < 2:
            dnormed = mm_nt(dproj[512 * w : 512 * w + TOK], wsorted[...])
            total = cot_s[w] + norm_backward(dnormed, xhat_s[w], rstd_s[w], gain_ref[...])
            grad_ref[7 * w : 7 * w + 7] = total.reshape(7, 7, 8, C).astype(BF16)
        for i in reversed(range(JOBS)):
            if 0 <= now - 1 - i <= 2:
                first[i].advance(now - 1 - i, result(i))
        if now == JOBS:
            for i in range(JOBS):
                second[i].advance(3, result(JOBS + i))
    for reduction in first + second:
        reduction.finish()


def second_kernel(
    scale,
    y_own, y_ahead, y_behind_here, y_above, y_corner, c_own, c_ahead, c_behind_here, c_above_here, c_corner_here,
    gain_ref, bias_ref, wqkv_ref, wout_ref,
    own, ahead_there, behind_there, above_there, corner_there, parts,
    normed_t, dproj, cot_b, mixt, wsorted, block, qbd, k, kt, v, vt, qn, dot_s, dobd, dopt, dqt,
    e_a, e_b, ds_a, ds_b, do_rows, q_rows, pen, cot_s, xhat_s,
    ahead, behind, above, corner, c_behind, c_above, c_corner, y_behind, send_sem, recv_sem,
):
    exchange = Exchange(-1, send_sem, recv_sem)
    exchange.greet((1, -1))
    e_s, ds_s = (e_a, e_b), (ds_a, ds_b)
    for ref in (qbd, dobd, do_rows, q_rows, normed_t, dproj, cot_b, mixt):
        ref[...] = jnp.zeros_like(ref)
    sort_columns(wsorted, wqkv_ref)
    for w in range(2):
        base = 512 * w
        last_frames = lax.axis_index("tm") == (lax.axis_size("tm") - 1 if w == 0 else 0)
        last_rows = (lax.axis_index("rows") == lax.axis_size("rows") - 1) if w == 1 else False

        def region_of(token, segment):
            columns = 4 if segment == 0 else 3
            late = jnp.where(last_frames & (token % 8 < 4), 1, 0)
            below = jnp.where(last_rows & (token // 8 // columns >= 4), 2, 0)
            return late + below

        def gather(into, own, ahead, behind, above, corner):
            def put(rho, count, whole):
                into[32 * rho : 32 * (rho + count)] = whole[:, 3:7].reshape(-1, C)
                into[224 + 24 * rho : 224 + 24 * (rho + count)] = whole[:, 0:3].reshape(-1, C)

            if w == 0:
                put(0, 7, joined(ahead[...], own[0:7]))
            else:
                put(0, 4, joined(own[7:11], behind[...]))
                put(4, 3, joined(above[...], corner[...]))

        if w == 1:
            exchange.wait_for((0, 1, 2, 3))
        gather(xhat_s, y_own, y_ahead, y_behind, y_above, y_corner)
        gather(cot_s, c_own, c_ahead, c_behind, c_above, c_corner)
        xhat, rstd = standardized(xhat_s[...])
        xhat_s[...] = xhat
        normed = (xhat * gain_ref[...] + bias_ref[...]).astype(BF16)
        normed_t[:, base : base + TOK] = normed.T
        queries = (mm(normed, wqkv_ref[:, 0:C]) * QSCALE).astype(BF16)
        qn[...] = queries
        keys = mm(normed, wqkv_ref[:, C : 2 * C]).astype(BF16)
        k[...] = keys
        values_f = mm(normed, wqkv_ref[:, 2 * C :])
        values = values_f.astype(BF16)
        v[...] = values
        cot_h = cot_s[...].astype(BF16)
        dmixed = mm_nt(cot_h, wout_ref[...]).astype(BF16)
        for s, (start, stop) in enumerate(SPLIT):
            count = stop - start
            cot_b[512 * w + 256 * s : 512 * w + 256 * s + count] = cot_h[start:stop]
            put_diagonal(qbd, queries[start:stop].T, 256, 1024 * s)
            kt[:, 256 * s : 256 * s + count] = keys[start:stop].T
            dot_s[:, 256 * s : 256 * s + count] = dmixed[start:stop].T
            turned = values[start:stop].T
            vt[:, 256 * s : 256 * s + count] = turned
            total = jnp.sum(turned.astype(F32), axis=1, keepdims=True)
            other = 1 - s
            lane = 256 * other + SPLIT[other][1] - SPLIT[other][0]
            first = lax.broadcasted_iota(jnp.int32, (C, VIRTUAL), 1) == 0
            vt[:, lane : lane + VIRTUAL] = jnp.where(first, total, 0.0).astype(BF16)
            shape = (count, 256)
            key = region_of(lax.broadcasted_iota(jnp.int32, shape, 0), s)
            query = region_of(lax.broadcasted_iota(jnp.int32, shape, 1), s)
            pen[start:stop] = jnp.where(key == query, 0.0, 1.0)

        if w == 0:
            exchange.wait_for_others()
            exchange.send(1, y_behind_here, y_behind, 1)
            exchange.send(1, c_behind_here, c_behind, 1)
            exchange.send(2, c_above_here, c_above, 1)
            exchange.send(3, c_corner_here, c_corner, 1)

        def group(g, carry):
            virtual_dv = []
            grads = []
            for s, (start, stop) in enumerate(SPLIT):
                count = stop - start
                kg = k[start:stop, channels_of(g)]
                apart = pen[start:stop] > 0.5
                sums_of, invs = [], []
                for j in range(GROUP):
                    lanes = slice(256 * j, 256 * (j + 1))
                    scores = mm(kg, qbd[channels_of(g), 1024 * s + 256 * j : 1024 * s + 256 * (j + 1)])
                    scores = jnp.where(apart, MASKED, scores)
                    top = jnp.maximum(jnp.max(scores, axis=0, keepdims=True), MASKED)
                    e = jnp.exp2(scores - top)
                    e_s[s][0:count, lanes] = e.astype(BF16)
                    rest = jnp.exp2(MASKED - top)
                    first = lax.broadcasted_iota(jnp.int32, (VIRTUAL, 256), 0) == 0
                    e_s[s][count : count + VIRTUAL, lanes] = jnp.where(first, rest, 0.0).astype(BF16)
                    invs.append(1.0 / (jnp.sum(e, axis=0, keepdims=True) + (TOK - count) * rest))
                for j in range(GROUP):
                    lanes = slice(256 * j, 256 * (j + 1))
                    tokens = slice(256 * s, 256 * (s + 1))
                    inv = invs[j]
                    mixed = inv * mm(
                        vt[head_channels(g, j), 256 * s : 256 * s + count + VIRTUAL], e_s[s][:, lanes]
                    )
                    mixt[head_channels(g, j), 512 * w + 256 * s : 512 * w + 256 * s + count] = mixed[
                        :, 0:count
                    ].astype(BF16)
                    do = dot_s[head_channels(g, j), tokens].astype(F32) * inv
                    inside = lax.broadcasted_iota(jnp.int32, do.shape, 1) < count
                    do = jnp.where(inside, do, 0.0).astype(BF16)
                    sums_of.append(jnp.sum(mixed * do.astype(F32), axis=0, keepdims=True))
                    dopt[HD * j : HD * (j + 1), tokens] = do
                    dobd[HD * j : HD * (j + 1), 1024 * s + 256 * j : 1024 * s + 256 * (j + 1)] = do
                turned = dopt[:, 256 * s : 256 * (s + 1)].T
                qg = qn[start:stop, channels_of(g)]
                for j in range(GROUP):
                    lanes = slice(256 * j, 256 * (j + 1))
                    at = 1024 * s + 256 * j
                    do_rows[at : at + 256] = own_lanes(j, turned)
                    q_rows[at : at + count] = own_lanes(j, qg)
                    dp = mm(v[start:stop, channels_of(g)], dobd[:, at : at + 256]) - sums_of[j]
                    ds = e_s[s][0:count, lanes].astype(F32) * jnp.where(apart, 0.0, dp)
                    ds = ds.astype(BF16)
                    ds_s[s][:, lanes] = ds
                    dq = mm(kt[head_channels(g, j), 256 * s : 256 * s + count], ds)
                    dqt[HD * j : HD * (j + 1), 256 * s : 256 * (s + 1)] = (dq * HD ** (-0.5)).astype(BF16)
                block = slice(1024 * s, 1024 * (s + 1))
                dv = mm(e_s[s][...], do_rows[block])
                dk = mm(ds_s[s][...], q_rows[block]) * LN2
                virtual_dv.append(dv[count : count + 1])
                grads.append((dk, dv[0:count]))
            for s, (start, stop) in enumerate(SPLIT):
                rows = slice(base + start, base + stop)
                dk, dv = grads[s]
                dproj[rows, columns_of(g)] = jnp.concatenate(
                    [
                        dqt[:, 256 * s : 256 * s + stop - start].T,
                        dk.astype(BF16),
                        (dv + virtual_dv[1 - s]).astype(BF16),
                    ],
                    axis=1,
                )
            return carry

        lax.fori_loop(0, HEADS // GROUP, group, 0)
        dnormed = mm_nt(dproj[base : base + TOK], wsorted[...])
        total = cot_s[...] + norm_backward(dnormed, xhat_s[...], rstd, gain_ref[...])
        whole = jnp.concatenate(
            [total[224:392].reshape(7, 3, 8, C), total[0:224].reshape(7, 4, 8, C)], axis=1
        )
        low, high = whole[:, :, 0:4].astype(BF16), whole[:, :, 4:8].astype(BF16)
        if w == 0:
            ahead[...] = low
            own[0:7] = high
            exchange.send(0, ahead, ahead_there)
        else:
            own[7:11] = low[0:4]
            behind[...] = high[0:4]
            above[...] = low[4:7]
            corner[...] = high[4:7]
            exchange.send(1, behind, behind_there)
            exchange.send(2, above, above_there)
            exchange.send(3, corner, corner_there)

    def gradients(g, carry):
        group_gradients(scale, g, g % 3, normed_t, dproj, mixt, cot_b, block, parts.at[g])
        return carry

    lax.fori_loop(0, JOBS, gradients, 0)
    exchange.wait((0, 1, 2, 3))


def piece_shapes():
    return [(rows, 7, 4, C) for rows in (11, 7, 4, 3, 3)]


PARTS = [(JOBS, 2, 4, 4, 4, 4, 512)]
SAVED = [
    jax.ShapeDtypeStruct((2, C, 512), BF16),
    jax.ShapeDtypeStruct((2, HEADS // GROUP, 1, 4 * MAIN), F32),
    jax.ShapeDtypeStruct((2, 1, 128), F32),
]
TOKENS = (14, 7, 8, C)
IN_VMEM = pl.BlockSpec(memory_space=pltpu.VMEM)


ANYWHERE = pl.BlockSpec(memory_space=pl.ANY)
IN_HBM = pl.BlockSpec(memory_space=pltpu.HBM)


def call(
    kernel, name, args, out_shape, scratch, vmem, there=(), far=(), semaphores=(), collective_id=None
):
    return pl.pallas_call(
        kernel,
        in_specs=[IN_HBM if i in far else IN_VMEM for i in range(len(args))],
        out_specs=[ANYWHERE if i in there else IN_VMEM for i in range(len(out_shape))],
        out_shape=out_shape,
        scratch_shapes=[pltpu.VMEM(shape, dtype) for shape, dtype in scratch]
        + [pltpu.SemaphoreType.DMA(shape) for shape in semaphores],
        compiler_params=pltpu.CompilerParams(
            vmem_limit_bytes=vmem * MIB,
            has_side_effects=collective_id is not None,
            collective_id=collective_id,
        ),
        name=name,
    )(*args)


def halves(shapes):
    return [jax.ShapeDtypeStruct(shape, BF16) for shape in shapes]


def forward_first(x, cot, weights):
    pieces = piece_shapes()
    outs = call(
        forward_kernel,
        "forward_first",
        (x, cot, *weights),
        SAVED + halves(pieces * 2),
        [(shape, BF16) for shape in (pieces[1], *pieces[3:], pieces[1])]
        + [((C, 4 * MAIN), BF16), ((TOK, C), BF16), ((C, TOK), BF16)]
        + [(x.shape, BF16), (cot.shape, BF16)]
        + [(weight.shape, weight.dtype) for weight in weights],
        vmem=52,
        far=range(6),
        there=(4, 6, 7, 9),
        semaphores=[(5,), (5,), (6,)],
        collective_id=1,
    )
    return outs[:3], outs[3:8], outs[8:]


GRADIENT_SCRATCH = [
    ((C, 1024), BF16), ((1024, 3 * C), BF16), ((1024, C), BF16), ((C, 1024), BF16), ((C, 3 * C), BF16), ((C, C), F32),
]


def backward_first(scale, x, weights, saved, pieces, parts):
    both = 2 * JOBS
    args = (x, *weights, *saved, *pieces, parts)
    return call(
        functools.partial(backward_first_kernel, scale),
        "backward_first",
        args,
        halves([TOKENS]) + [jax.ShapeDtypeStruct((4, width), F32) for width in (3 * C, C)] * 2,
        GRADIENT_SCRATCH
        + [(PARTS[0], BF16)]
        + [
            ((2, C, 4 * MAIN), BF16), ((2, TOK, C), BF16), ((2, C, TOK), BF16), ((2, TOK, C), BF16),
            ((2, TOK, C), BF16), ((2, TOK, C), BF16), ((2, C, 4 * MAIN), BF16),
            ((2, TOK, 4 * MAIN), BF16), ((2, TOK, 4 * MAIN), BF16), ((2, 128, MAIN), F32),
            ((2, 4 * MAIN, 128), BF16), ((2, 4 * MAIN, 128), BF16),
            ((2, TOK, C), F32), ((2, TOK, C), F32), ((2, TOK, 1), F32),
            ((2, TOK, C), F32), ((2, TOK, C), F32), ((2, LEFT, C), F32),
        ]
        + [((both, 4, 4, 4, 4, 512), BF16)] * 3
        + [((both, 4, 4, 4, 512), BF16), ((both, 4, 4, 512), BF16)],
        vmem=46,
        far=(len(args) - 1,),
        semaphores=[(JOBS,), (both, 19), (both, 19)],
        collective_id=3,
    )


def hand_on_kernel(*refs):
    for source, target in zip(refs[:5], refs[5:]):
        target[...] = source[...]


def handed_on(outs):
    return call(
        hand_on_kernel,
        "hand_on",
        outs,
        [jax.ShapeDtypeStruct(out.shape, out.dtype) for out in outs],
        [],
        vmem=8,
    )


def second_block(scale, y_pieces, c_pieces, weights):
    return call(
        functools.partial(second_kernel, scale),
        "second_block",
        (*y_pieces, *c_pieces, *weights),
        halves(piece_shapes() + PARTS),
        GRADIENT_SCRATCH
        + [
            ((C, 2048), BF16), ((TOK, C), BF16), ((C, 512), BF16), ((TOK, C), BF16),
            ((C, 512), BF16), ((TOK, C), BF16), ((C, 512), BF16),
            ((128, 2048), BF16), ((128, 512), BF16), ((128, 512), BF16),
            ((224 + VIRTUAL, 1024), BF16), ((168 + VIRTUAL, 1024), BF16),
            ((224, 1024), BF16), ((168, 1024), BF16),
            ((2048, 128), BF16), ((2048, 128), BF16),
            ((TOK, 256), F32), ((TOK, C), F32), ((TOK, C), F32),
        ]
        + [(shape, BF16) for shape in piece_shapes()[1:] + piece_shapes()[2:] + piece_shapes()[2:3]],
        vmem=28,
        there=range(1, 5),
        semaphores=[(8,)] * 2,
        collective_id=2,
    )


def per_device(
    video_clip, cotangent,
    gain_first, bias_first, qkv_first, out_first,
    gain_second, bias_second, qkv_second, out_second,
):
    frames, rows_here, columns, channels = video_clip.shape
    devices = lax.axis_size("tm") * lax.axis_size("rows")
    scale = 1.0 / math.sqrt(frames * rows_here * columns * devices)
    x = video_clip.transpose(1, 2, 0, 3)
    cot = cotangent.transpose(1, 2, 0, 3)
    first = (gain_first.reshape(1, C), bias_first.reshape(1, C), qkv_first, out_first)
    second = (gain_second.reshape(1, C), bias_second.reshape(1, C), qkv_second, out_second)
    saved, y_pieces, c_pieces = forward_first(x, cot, first)
    *d_pieces, parts = second_block(scale, y_pieces, c_pieces, second)
    grad, *sums = handed_on(backward_first(scale, x, first, saved, d_pieces, parts))
    return (grad.transpose(2, 0, 1, 3), *sums)


def solution(mesh):
    clip = P("tm", "rows", None, None)
    scattered = P(("tm", "rows"), None)
    return jax.shard_map(
        per_device,
        mesh=mesh,
        in_specs=(clip, clip) + (P(),) * 8,
        out_specs=(clip,) + (scattered,) * 4,
        check_vma=False,
    )
```

```python
import functools
import math

import jax
import jax.numpy as jnp
from jax import lax
from jax.experimental import pallas as pl
from jax.experimental.pallas import tpu as pltpu
from jax.sharding import PartitionSpec as P

F32, BF16 = jnp.float32, jnp.bfloat16
C, HEADS, HD = 512, 16, 32
TOK = 392
GROUP = 4
LOG2E = math.log2(math.e)
QSCALE = HD ** (-0.5) * LOG2E
MASKED = -1000000000.0 * LOG2E
LN2 = math.log(2.0)
SPLIT = ((0, 224), (224, 392))
MAIN = 384
LEFT = TOK - MAIN
VIRTUAL = 16
ROWS = 400
MIB = 1024 * 1024


def mm(a, b):
    return lax.dot_general(a, b, (((1,), (0,)), ((), ())), preferred_element_type=F32)


def mm_nt(a, b):
    return lax.dot_general(a, b, (((1,), (1,)), ((), ())), preferred_element_type=F32)


def mm_tn(a, b):
    return lax.dot_general(a, b, (((0,), (0,)), ((), ())), preferred_element_type=F32)


def standardized(values):
    center = values - jnp.mean(values, axis=-1, keepdims=True)
    rstd = lax.rsqrt(jnp.mean(center * center, axis=-1, keepdims=True) + 1e-05)
    return center * rstd, rstd


def tiles(block):
    return block.astype(F32).reshape(-1, C)


def own_lanes(j, block):
    lane = lax.broadcasted_iota(jnp.int32, block.shape, 1) // HD
    return jnp.where(lane == j, block, jnp.zeros_like(block))


def put_diagonal(ref, turned, pitch, column=0):
    for head in range(HEADS):
        at = pitch * (head % GROUP) + column
        ref[HD * head : HD * (head + 1), at : at + turned.shape[1]] = turned[HD * head : HD * (head + 1)]


def left_rows(block):
    rows = jnp.concatenate([block.astype(F32)] * HEADS, axis=0)
    row = lax.broadcasted_iota(jnp.int32, rows.shape, 0) // LEFT
    lane = lax.broadcasted_iota(jnp.int32, rows.shape, 1) // HD
    return jnp.where(row == lane, rows, 0.0)


def from_left(product):
    turned = product.T
    row = lax.broadcasted_iota(jnp.int32, turned.shape, 0) // LEFT
    lane = lax.broadcasted_iota(jnp.int32, turned.shape, 1) // HD
    return jnp.sum(jnp.where(row == lane, turned, 0.0).reshape(HEADS, LEFT, C), axis=0)


def pair_channels(g, pair):
    return pl.ds(pl.multiple_of(g * 128 + pair * 64, 64), 64)


def channels_of(g, first=0):
    return pl.ds(pl.multiple_of(g * 128 + first, 128), 128)


def head_channels(g, j):
    return pl.ds(pl.multiple_of(g * 128 + j * HD, HD), HD)


MESH = pl.DeviceIdType.MESH
ROUTES = ((-1, 0), (1, 0), (0, -1), (1, -1))


class Exchange:
    def __init__(self, way, send_sem, recv_sem):
        self.way, self.sems, self.copies = way, (send_sem, recv_sem), []

    def device(self, steps, sign):
        size = lax.axis_size("tm"), lax.axis_size("rows")
        here = lax.axis_index("tm"), lax.axis_index("rows")
        return tuple((i + sign * d + n) % n for i, d, n in zip(here, steps, size))

    def greet(self, ways):
        self.ways = ways
        for way in ways:
            for steps in ROUTES:
                pl.semaphore_signal(
                    pltpu.get_barrier_semaphore(),
                    inc=1,
                    device_id=self.device(steps, -way),
                    device_id_type=MESH,
                )

    def wait_for_others(self):
        pl.semaphore_wait(pltpu.get_barrier_semaphore(), len(self.ways) * len(ROUTES))

    def send(self, route, source, target, way=None):
        i = len(self.copies)
        copy = pltpu.make_async_remote_copy(
            src_ref=source,
            dst_ref=target,
            send_sem=self.sems[0].at[i],
            recv_sem=self.sems[1].at[i],
            device_id=self.device(ROUTES[route], way or self.way),
            device_id_type=MESH,
        )
        copy.start()
        self.copies.append(copy)

    def wait_for(self, numbers):
        for i in numbers:
            self.copies[i].wait_recv()

    def wait(self, arrived=()):
        for i, copy in enumerate(self.copies):
            copy.wait_send()
            if i not in arrived:
                copy.wait_recv()


def pieces_of(whole, w, pieces):
    own, ahead, behind, above, corner = pieces
    if w == 0:
        above[...] = whole[0:3, :, 0:4].astype(BF16)
        corner[...] = whole[0:3, :, 4:8].astype(BF16)
        ahead[0:4] = whole[3:7, :, 0:4].astype(BF16)
        own[0:4] = whole[3:7, :, 4:8].astype(BF16)
    else:
        ahead[4:7] = whole[0:3, :, 0:4].astype(BF16)
        own[4:7] = whole[0:3, :, 4:8].astype(BF16)
        behind[...] = whole[3:7, :, 4:8].astype(BF16)
        own[7:11] = whole[3:7, :, 0:4].astype(BF16)


def joined(low, high):
    return jnp.concatenate([low.astype(F32), high.astype(F32)], axis=2)


def forward_kernel(
    x_far, cot_far, gain_far, bias_far, wqkv_far, wout_far, mixt_ref, stat_ref, stat_left, *refs,
):
    y_own, y_ahead_there, y_behind, y_above_there, y_corner_there = refs[0:5]
    c_own, c_ahead_there, *c_later = refs[5:10]
    y_ahead, y_above, y_corner, c_ahead, qbd, k, vt = refs[10:17]
    x_ref, cot_ref, gain_ref, bias_ref, wqkv_ref, wout_ref, send_sem, recv_sem, load_sem = refs[17:]
    loads = []
    for far, near in (
        (cot_far, cot_ref), (x_far, x_ref), (gain_far, gain_ref), (bias_far, bias_ref),
        (wqkv_far, wqkv_ref), (wout_far, wout_ref),
    ):
        loads.append(pltpu.make_async_copy(far, near, load_sem.at[len(loads)]))
        loads[-1].start()
    exchange = Exchange(1, send_sem, recv_sem)
    exchange.greet((1,))
    qbd[...] = jnp.zeros_like(qbd)
    loads[0].wait()
    for w in range(2):
        pieces_of(cot_ref[7 * w : 7 * w + 7].astype(F32), w, (c_own, c_ahead, *c_later))
    exchange.wait_for_others()
    exchange.send(0, c_ahead, c_ahead_there)
    for load in loads[1:4]:
        load.wait()
    for w in range(2):
        rows = slice(7 * w, 7 * w + 7)
        x = tiles(x_ref[rows])
        xhat, _ = standardized(x)
        normed = (xhat * gain_ref[...] + bias_ref[...]).astype(BF16)
        if w == 0:
            for load in loads[4:]:
                load.wait()
        queries = mm(normed, wqkv_ref[:, 0:C]) * QSCALE
        put_diagonal(qbd, queries[0:MAIN].astype(BF16).T, MAIN)
        k[...] = mm(normed, wqkv_ref[:, C : 2 * C]).astype(BF16)
        vt[...] = mm(normed, wqkv_ref[:, 2 * C :]).astype(BF16).T

        def group(g, carry):
            kg = k[:, channels_of(g)]
            for pair in range(2):
                lanes = slice(768 * pair, 768 * (pair + 1))
                scores = mm(kg, qbd[channels_of(g), lanes])
                top = jnp.max(scores, axis=0, keepdims=True)
                e = jnp.exp2(scores - top)
                sums = jnp.sum(e, axis=0, keepdims=True)
                mixed = mm(vt[pair_channels(g, pair), :], e.astype(BF16)) * (1.0 / sums)
                stat_ref[w, g, :, lanes] = top + jnp.log2(sums)
                for i in range(2):
                    mixt_ref[w, head_channels(g, 2 * pair + i), 0:MAIN] = mixed[
                        HD * i : HD * (i + 1), MAIN * i : MAIN * (i + 1)
                    ].astype(BF16)
            return carry

        lax.fori_loop(0, HEADS // GROUP, group, 0)
        scores = mm(k[...], left_rows(queries[MAIN:TOK]).astype(BF16).T)
        top = jnp.max(scores, axis=0, keepdims=True)
        e = jnp.exp2(scores - top)
        sums = jnp.sum(e, axis=0, keepdims=True)
        stat_left[w] = top + jnp.log2(sums)
        mixed = from_left(mm(vt[...], e.astype(BF16)) * (1.0 / sums))
        mixt_ref[w, :, MAIN:512] = jnp.concatenate(
            [mixed, jnp.zeros((128 - LEFT, C), F32)], axis=0
        ).T.astype(BF16)
        y = x + mm_tn(mixt_ref[w, :, 0:TOK], wout_ref[...])
        pieces_of(y.reshape(7, 7, 8, C), w, (y_own, y_ahead, y_behind, y_above, y_corner))
        if w == 0:
            exchange.send(2, y_above, y_above_there)
            exchange.send(3, y_corner, y_corner_there)
            exchange.send(0, y_ahead.at[0:4], y_ahead_there.at[0:4])
        else:
            exchange.send(0, y_ahead.at[4:7], y_ahead_there.at[4:7])
    exchange.wait()


def write_part(turn, block, part):
    def layer(z, carry):
        for xy in range(16):
            x, y = xy // 4, xy % 4
            rows = pl.ds(pl.multiple_of((z * 16 + x // 2 * 8 + y * 2 + x % 2) * 8, 8), 8)
            values = block[rows, :]
            first = jnp.where(turn == 0, x, jnp.where(turn == 1, y, z))
            second = jnp.where(turn == 0, y, jnp.where(turn == 1, z, x))
            third = jnp.where(turn == 0, z, jnp.where(turn == 1, x, y))
            part[0, first, second, third] = values[0:4].astype(BF16)
            part[1, first, second, third] = values[4:8].astype(BF16)
        return carry

    lax.fori_loop(0, 4, layer, 0)


def group_gradients(scale, g, turn, normed_t, dproj, mixt, cot_b, block, part):
    block[:, 0:384] = mm(normed_t[...], dproj[:, columns_of(g)]) * scale
    block[:, 384:512] = mm(mixt[...], cot_b[:, channels_of(g)]) * scale
    write_part(turn, block, part)


def columns_of(g):
    return pl.ds(pl.multiple_of(g * 384, 128), 384)


def clear_padding(by_rows, by_lanes):
    for w in range(2):
        padding = slice(512 * w + MAIN, 512 * (w + 1))
        for ref in by_rows:
            ref[padding] = jnp.zeros((128, ref.shape[1]), BF16)
        by_lanes[:, padding] = jnp.zeros((C, 128), BF16)


def sort_columns(sorted_ref, wqkv_ref):
    for g in range(HEADS // GROUP):
        for i in range(3):
            sorted_ref[:, 384 * g + 128 * i : 384 * g + 128 * (i + 1)] = wqkv_ref[
                :, C * i + 128 * g : C * i + 128 * (g + 1)
            ]


def norm_backward(dnormed, xhat, rstd, gain):
    d = dnormed.astype(BF16).astype(F32) * gain
    return rstd * (
        d
        - jnp.mean(d, axis=-1, keepdims=True)
        - xhat * jnp.mean(d * xhat, axis=-1, keepdims=True)
    )


def coordinates():
    tm, rows = lax.axis_index("tm"), lax.axis_index("rows")
    return {
        "x": tm // 4 % 2 * 2 + rows // 2,
        "y": tm % 4,
        "z": tm // 8,
        "core": rows % 2,
    }


def device_at(place):
    tm = place["z"] * 8 + place["x"] // 2 * 4 + place["y"]
    return (tm, place["x"] % 2 * 2 + place["core"])


def beside(here, axis, steps):
    return device_at({**here, axis: (here[axis] + steps) % (2 if axis == "core" else 4)})


ORDERS = ("xyz", "yzx", "zxy")


class Reduction:
    def __init__(self, order, plane, here, partners, part, local_sem, buffers, sems):
        self.plane = plane
        self.order, self.here, self.partners, self.part = order, here, partners, part
        self.held, self.other, *self.slots = buffers
        self.local_sem, self.sems = local_sem, sems

    def remote(self, number, source, target, partner):
        return pltpu.make_async_remote_copy(
            src_ref=source,
            dst_ref=target,
            send_sem=self.sems[0].at[number],
            recv_sem=self.sems[1].at[number],
            device_id=partner,
            device_id_type=MESH,
        )

    def local_copy(self):
        return pltpu.make_async_copy(self.part.at[self.here["core"]], self.held, self.local_sem)

    def core_copy(self):
        return self.remote(0, self.part.at[1 - self.here["core"]], self.other, self.partners["core", 1])

    def source(self, step):
        return self.held if step == 0 else self.slots[step - 1].at[3]

    def axis_copies(self, step):
        axis = self.order[step]
        return [
            self.remote(
                3 * step + away,
                self.source(step).at[(self.here[axis] + away) % 4],
                self.slots[step].at[away - 1],
                self.partners[axis, away],
            )
            for away in (1, 2, 3)
        ]

    def plane_copies(self):
        a, b = self.order[1:]
        copies = []
        for i in range(1, 16):
            da, db = i // 4, i % 4
            partner = (b, db) if da == 0 else (a, da) if db == 0 else (a, b, da, db)
            block = self.source(1).at[(self.here[a] + da) % 4, (self.here[b] + db) % 4]
            copies.append(self.remote(3 + i, block, self.slots[1].at[da, db], self.partners[partner]))
        return copies

    def copies(self, step):
        return self.plane_copies() if self.plane and step == 1 else self.axis_copies(step)

    def start(self):
        self.core_copy().start()

    def advance(self, stage, out=None):
        if stage == 0:
            self.core_copy().wait_recv()
            if self.local_sem is not None:
                self.local_copy().wait()
                own = self.held
            else:
                own = self.part.at[self.here["core"]]
            for i in range(4):
                self.held[i] = (own[i].astype(F32) + self.other[i].astype(F32)).astype(BF16)
        else:
            for copy in self.copies(stage - 1):
                copy.wait_recv()
            total = self.source(stage - 1)[self.here[self.order[stage - 1]]].astype(F32)
            if self.plane and stage == 2:
                a, b = self.order[1:]
                total = self.source(1)[self.here[a], self.here[b]].astype(F32)
                for i in range(1, 16):
                    total = total + self.slots[1][i // 4, i % 4].astype(F32)
                out(total)
                return
            for slot in range(3):
                total = total + self.slots[stage - 1][slot].astype(F32)
            if stage == 3:
                out(total)
                return
            self.slots[stage - 1][3] = total.astype(BF16)
        for copy in self.copies(stage):
            copy.start()

    def finish(self):
        self.core_copy().wait_send()
        for step in range(2 if self.plane else 3):
            for copy in self.copies(step):
                copy.wait_send()


JOBS = HEADS // GROUP
SECOND_STAGES = {0: 0, 2: 1, 3: 2}


def backward_first_kernel(
    scale,
    x_ref, gain_ref, bias_ref, wqkv_ref, wout_ref, mixt_ref, stat_ref, stat_left,
    own, ahead, behind, above, corner, parts_second,
    grad_ref, gqkv1, gout1, gqkv2, gout2,
    normed_t, dproj, cot_b, mixt_all, wsorted, block, parts_first,
    qbd, k, kt, v, qn, don, dobd, p_s, ds_s, dqt, do_rows, q_rows, cot_s, xhat_s, rstd_s,
    dk_left, dv_left, dq_left, held, other, slots_a, slots_b, slots_c, local_sem, send_sem, recv_sem,
):
    here = coordinates()
    partners = {("core", 1): beside(here, "core", 1)}
    for axis in "xyz":
        for away in (1, 2, 3):
            partners[axis, away] = beside(here, axis, away)
    for a, b in ("yz", "xy"):
        for da in (1, 2, 3):
            for db in (1, 2, 3):
                partners[a, b, da, db] = device_at(
                    {**here, a: (here[a] + da) % 4, b: (here[b] + db) % 4}
                )
    barrier = pltpu.get_barrier_semaphore()
    for partner in partners.values():
        pl.semaphore_signal(barrier, inc=1, device_id=partner, device_id_type=MESH)

    def job(i):
        of_first = i < JOBS
        g = i % JOBS
        return Reduction(
            ORDERS[g % 2 * 2] if of_first else ORDERS[g % 3],
            of_first,
            here,
            partners,
            parts_first.at[g] if of_first else parts_second.at[g],
            None if of_first else local_sem.at[g],
            [ref.at[i] for ref in (held, other, slots_a, slots_b, slots_c)],
            (send_sem.at[i], recv_sem.at[i]),
        )

    def result(i):
        gqkv, gout = (gqkv1, gout1) if i < JOBS else (gqkv2, gout2)
        g = i % JOBS

        def out(total):
            for part in range(3):
                at = C * part + 128 * g
                gqkv[:, at : at + 128] = total[:, 128 * part : 128 * (part + 1)]
            gout[:, 128 * g : 128 * (g + 1)] = total[:, 384:512]

        return out

    first, second = [job(i) for i in range(JOBS)], [job(JOBS + i) for i in range(JOBS)]
    for reduction in second:
        reduction.local_copy().start()
    for ref in (qbd, dobd):
        ref[...] = jnp.zeros_like(ref)
    clear_padding((dproj, cot_b), normed_t)
    sort_columns(wsorted, wqkv_ref)
    for w in range(2):
        xhat, rstd = standardized(tiles(x_ref[7 * w : 7 * w + 7]))
        xhat_s[w] = xhat
        rstd_s[w] = rstd
        normed = (xhat * gain_ref[...] + bias_ref[...]).astype(BF16)
        normed_t[:, 512 * w : 512 * w + TOK] = normed.T
        queries = (mm(normed, wqkv_ref[:, 0:C]) * QSCALE).astype(BF16)
        qn[w] = queries
        put_diagonal(qbd.at[w], queries[0:MAIN].T, MAIN)
        keys = mm(normed, wqkv_ref[:, C : 2 * C]).astype(BF16)
        k[w] = keys
        kt[w] = keys.T
        v[w] = mm(normed, wqkv_ref[:, 2 * C :]).astype(BF16)
        if w == 0:
            pieces = [joined(above[...], corner[...]), joined(ahead[0:4], own[0:4])]
        else:
            pieces = [joined(ahead[4:7], own[4:7]), joined(own[7:11], behind[...])]
        cot = jnp.concatenate([piece.reshape(-1, C) for piece in pieces], axis=0)
        cot_s[w] = cot
        cot_h = cot.astype(BF16)
        cot_b[512 * w : 512 * w + TOK] = cot_h
        dmixed = mm_nt(cot_h, wout_ref[...]).astype(BF16)
        don[w] = dmixed
        put_diagonal(dobd.at[w], dmixed[0:MAIN].T, MAIN)
        mixt_all[:, 512 * w : 512 * (w + 1)] = mixt_ref[w]
        q_left = left_rows(queries[MAIN:TOK]).astype(BF16)
        do_left = left_rows(dmixed[MAIN:TOK])
        mixed = mixt_ref[w, :, MAIN:512].astype(F32).T[0:LEFT]
        dsum = jnp.sum((do_left * jnp.concatenate([mixed] * HEADS, axis=0)).T, axis=0, keepdims=True)
        do_left = do_left.astype(BF16)
        p = jnp.exp2(mm(k[w], q_left.T) - stat_left[w])
        ds = (p * (mm(v[w], do_left.T) - dsum)).astype(BF16)
        dv_left[w] = mm(p.astype(BF16), do_left)
        dk_left[w] = mm(ds, q_left)
        dq_left[w] = from_left(mm(kt[w], ds))
        if w == 0:
            pl.semaphore_wait(barrier, len(partners))
            for reduction in second:
                reduction.start()

    def group(g, carry):
        for w in range(2):
            kg = k[w, :, channels_of(g)]
            vg = v[w, :, channels_of(g)]
            qg = qn[w, :, channels_of(g)]
            dog = don[w, :, channels_of(g)]
            for j in range(GROUP):
                do_rows[w, MAIN * j : MAIN * (j + 1)] = own_lanes(j, dog[0:MAIN])
                q_rows[w, MAIN * j : MAIN * (j + 1)] = own_lanes(j, qg[0:MAIN])
            for pair in range(2):
                lanes = slice(768 * pair, 768 * (pair + 1))
                scores = mm(kg, qbd[w, channels_of(g), lanes])
                p = jnp.exp2(scores - stat_ref[w, g, :, lanes]).astype(BF16)
                p_s[w, :, lanes] = p
                dsums = []
                for j in (2 * pair, 2 * pair + 1):
                    dsums.append(
                        jnp.sum(
                            mixt_ref[w, head_channels(g, j), 0:MAIN].astype(F32)
                            * dobd[w, head_channels(g, j), MAIN * j : MAIN * (j + 1)].astype(F32),
                            axis=0, keepdims=True,
                        )
                    )
                dp = mm(vg, dobd[w, channels_of(g), lanes]) - jnp.concatenate(dsums, axis=1)
                ds = (p.astype(F32) * dp).astype(BF16)
                ds_s[w, :, lanes] = ds
                dq = mm(kt[w, pair_channels(g, pair), :], ds)
                for i in range(2):
                    j = 2 * pair + i
                    dqt[w, HD * j : HD * (j + 1), :] = dq[HD * i : HD * (i + 1), MAIN * i : MAIN * (i + 1)]
            dk = (mm(ds_s[w], q_rows[w]) + dk_left[w, :, channels_of(g)]) * LN2
            dv = mm(p_s[w], do_rows[w]) + dv_left[w, :, channels_of(g)]
            dq = jnp.concatenate([dqt[w].T, dq_left[w, :, channels_of(g)]], axis=0) * HD ** (-0.5)
            dproj[512 * w : 512 * w + TOK, columns_of(g)] = jnp.concatenate(
                [dq.astype(BF16), dk.astype(BF16), dv.astype(BF16)], axis=1
            )
        group_gradients(scale, g, g % 2 * 2, normed_t, dproj, mixt_all, cot_b, block, parts_first.at[g])
        for now in range(JOBS):

            @pl.when(g == now)
            def _():
                first[now].start()
                for i in range(JOBS):
                    if now in SECOND_STAGES:
                        second[i].advance(SECOND_STAGES[now])
                for i in range(now):
                    first[i].advance(now - 1 - i, result(i))

        return carry

    lax.fori_loop(0, JOBS, group, 0)
    for now in range(JOBS, 2 * JOBS - 1):
        w = now - JOBS
        if w < 2:
            dnormed = mm_nt(dproj[512 * w : 512 * w + TOK], wsorted[...])
            total = cot_s[w] + norm_backward(dnormed, xhat_s[w], rstd_s[w], gain_ref[...])
            grad_ref[7 * w : 7 * w + 7] = total.reshape(7, 7, 8, C).astype(BF16)
        for i in reversed(range(JOBS)):
            if 0 <= now - 1 - i <= 2:
                first[i].advance(now - 1 - i, result(i))
        if now == JOBS:
            for i in range(JOBS):
                second[i].advance(3, result(JOBS + i))
    for reduction in first + second:
        reduction.finish()


def second_kernel(
    scale,
    y_own, y_ahead, y_behind_here, y_above, y_corner, c_own, c_ahead, c_behind_here, c_above_here, c_corner_here,
    gain_ref, bias_ref, wqkv_ref, wout_ref,
    own, ahead_there, behind_there, above_there, corner_there, parts,
    normed_t, dproj, cot_b, mixt, wsorted, block, qbd, k, kt, v, vt, qn, dot_s, dobd, dopt, dqt,
    e_a, e_b, ds_a, ds_b, do_rows, q_rows, pen, cot_s, xhat_s,
    ahead, behind, above, corner, c_behind, c_above, c_corner, y_behind, send_sem, recv_sem,
):
    exchange = Exchange(-1, send_sem, recv_sem)
    exchange.greet((1, -1))
    e_s, ds_s = (e_a, e_b), (ds_a, ds_b)
    for ref in (qbd, dobd, q_rows, cot_b, mixt):
        ref[...] = jnp.zeros_like(ref)
    clear_padding((dproj,), normed_t)
    sort_columns(wsorted, wqkv_ref)
    for w in range(2):
        base = 512 * w
        last_frames = lax.axis_index("tm") == (lax.axis_size("tm") - 1 if w == 0 else 0)
        last_rows = (lax.axis_index("rows") == lax.axis_size("rows") - 1) if w == 1 else False

        def region_of(token, segment):
            columns = 4 if segment == 0 else 3
            late = jnp.where(last_frames & (token % 8 < 4), 1, 0)
            below = jnp.where(last_rows & (token // 8 // columns >= 4), 2, 0)
            return late + below

        def gather(into, own, ahead, behind, above, corner):
            def put(rho, count, whole):
                into[32 * rho : 32 * (rho + count)] = whole[:, 3:7].reshape(-1, C)
                into[224 + 24 * rho : 224 + 24 * (rho + count)] = whole[:, 0:3].reshape(-1, C)

            if w == 0:
                put(0, 7, joined(ahead[...], own[0:7]))
            else:
                put(0, 4, joined(own[7:11], behind[...]))
                put(4, 3, joined(above[...], corner[...]))

        if w == 1:
            exchange.wait_for((0, 1, 2, 3))
        gather(xhat_s, y_own, y_ahead, y_behind, y_above, y_corner)
        gather(cot_s, c_own, c_ahead, c_behind, c_above, c_corner)
        xhat, rstd = standardized(xhat_s[...])
        xhat_s[...] = xhat
        normed = (xhat * gain_ref[...] + bias_ref[...]).astype(BF16)
        normed_t[:, base : base + TOK] = normed.T
        queries = (mm(normed, wqkv_ref[:, 0:C]) * QSCALE).astype(BF16)
        qn[...] = queries
        keys = mm(normed, wqkv_ref[:, C : 2 * C]).astype(BF16)
        k[...] = keys
        values_f = mm(normed, wqkv_ref[:, 2 * C :])
        values = values_f.astype(BF16)
        v[...] = values
        cot_h = cot_s[...].astype(BF16)
        dmixed = mm_nt(cot_h, wout_ref[...]).astype(BF16)
        for s, (start, stop) in enumerate(SPLIT):
            count = stop - start
            cot_b[512 * w + 256 * s : 512 * w + 256 * s + count] = cot_h[start:stop]
            put_diagonal(qbd, queries[start:stop].T, 256, 1024 * s)
            kt[:, 256 * s : 256 * s + count] = keys[start:stop].T
            dot_s[:, 256 * s : 256 * s + count] = dmixed[start:stop].T
            turned = values[start:stop].T
            vt[:, 256 * s : 256 * s + count] = turned
            total = jnp.sum(turned.astype(F32), axis=1, keepdims=True)
            other = 1 - s
            lane = 256 * other + SPLIT[other][1] - SPLIT[other][0]
            first = lax.broadcasted_iota(jnp.int32, (C, VIRTUAL), 1) == 0
            vt[:, lane : lane + VIRTUAL] = jnp.where(first, total, 0.0).astype(BF16)
            shape = (count, 256)
            key = region_of(lax.broadcasted_iota(jnp.int32, shape, 0), s)
            query = region_of(lax.broadcasted_iota(jnp.int32, shape, 1), s)
            pen[start:stop] = jnp.where(key == query, 0.0, 1.0)

        if w == 0:
            exchange.wait_for_others()
            exchange.send(1, y_behind_here, y_behind, 1)
            exchange.send(1, c_behind_here, c_behind, 1)
            exchange.send(2, c_above_here, c_above, 1)
            exchange.send(3, c_corner_here, c_corner, 1)

        def group(g, carry):
            virtual_dv = []
            grads = []
            for s, (start, stop) in enumerate(SPLIT):
                count = stop - start
                kg = k[start:stop, channels_of(g)]
                apart = pen[start:stop] > 0.5
                sums_of, invs = [], []
                for j in range(GROUP):
                    lanes = slice(256 * j, 256 * (j + 1))
                    scores = mm(kg, qbd[channels_of(g), 1024 * s + 256 * j : 1024 * s + 256 * (j + 1)])
                    scores = jnp.where(apart, MASKED, scores)
                    top = jnp.maximum(jnp.max(scores, axis=0, keepdims=True), MASKED)
                    e = jnp.exp2(scores - top)
                    e_s[s][0:count, lanes] = e.astype(BF16)
                    rest = jnp.exp2(MASKED - top)
                    first = lax.broadcasted_iota(jnp.int32, (VIRTUAL, 256), 0) == 0
                    e_s[s][count : count + VIRTUAL, lanes] = jnp.where(first, rest, 0.0).astype(BF16)
                    invs.append(1.0 / (jnp.sum(e, axis=0, keepdims=True) + (TOK - count) * rest))
                for j in range(GROUP):
                    lanes = slice(256 * j, 256 * (j + 1))
                    tokens = slice(256 * s, 256 * (s + 1))
                    inv = invs[j]
                    mixed = inv * mm(
                        vt[head_channels(g, j), 256 * s : 256 * s + count + VIRTUAL], e_s[s][:, lanes]
                    )
                    mixt[head_channels(g, j), 512 * w + 256 * s : 512 * w + 256 * s + count] = mixed[
                        :, 0:count
                    ].astype(BF16)
                    do = dot_s[head_channels(g, j), tokens].astype(F32) * inv
                    inside = lax.broadcasted_iota(jnp.int32, do.shape, 1) < count
                    do = jnp.where(inside, do, 0.0).astype(BF16)
                    sums_of.append(jnp.sum(mixed * do.astype(F32), axis=0, keepdims=True))
                    dopt[HD * j : HD * (j + 1), tokens] = do
                    dobd[HD * j : HD * (j + 1), 1024 * s + 256 * j : 1024 * s + 256 * (j + 1)] = do
                turned = dopt[:, 256 * s : 256 * (s + 1)].T
                qg = qn[start:stop, channels_of(g)]
                for j in range(GROUP):
                    lanes = slice(256 * j, 256 * (j + 1))
                    at = 1024 * s + 256 * j
                    do_rows[at : at + 256] = own_lanes(j, turned)
                    q_rows[at : at + count] = own_lanes(j, qg)
                    dp = mm(v[start:stop, channels_of(g)], dobd[:, at : at + 256]) - sums_of[j]
                    ds = e_s[s][0:count, lanes].astype(F32) * jnp.where(apart, 0.0, dp)
                    ds = ds.astype(BF16)
                    ds_s[s][:, lanes] = ds
                    dq = mm(kt[head_channels(g, j), 256 * s : 256 * s + count], ds)
                    dqt[HD * j : HD * (j + 1), 256 * s : 256 * (s + 1)] = (dq * HD ** (-0.5)).astype(BF16)
                block = slice(1024 * s, 1024 * (s + 1))
                dv = mm(e_s[s][...], do_rows[block])
                dk = mm(ds_s[s][...], q_rows[block]) * LN2
                virtual_dv.append(dv[count : count + 1])
                grads.append((dk, dv[0:count]))
            for s, (start, stop) in enumerate(SPLIT):
                rows = slice(base + start, base + stop)
                dk, dv = grads[s]
                dproj[rows, columns_of(g)] = jnp.concatenate(
                    [
                        dqt[:, 256 * s : 256 * s + stop - start].T,
                        dk.astype(BF16),
                        (dv + virtual_dv[1 - s]).astype(BF16),
                    ],
                    axis=1,
                )
            return carry

        lax.fori_loop(0, HEADS // GROUP, group, 0)
        dnormed = mm_nt(dproj[base : base + TOK], wsorted[...])
        total = cot_s[...] + norm_backward(dnormed, xhat_s[...], rstd, gain_ref[...])
        whole = jnp.concatenate(
            [total[224:392].reshape(7, 3, 8, C), total[0:224].reshape(7, 4, 8, C)], axis=1
        )
        low, high = whole[:, :, 0:4].astype(BF16), whole[:, :, 4:8].astype(BF16)
        if w == 0:
            ahead[...] = low
            own[0:7] = high
            exchange.send(0, ahead, ahead_there)
        else:
            own[7:11] = low[0:4]
            behind[...] = high[0:4]
            above[...] = low[4:7]
            corner[...] = high[4:7]
            exchange.send(1, behind, behind_there)
            exchange.send(2, above, above_there)
            exchange.send(3, corner, corner_there)

    def gradients(g, carry):
        group_gradients(scale, g, g % 3, normed_t, dproj, mixt, cot_b, block, parts.at[g])
        return carry

    lax.fori_loop(0, JOBS, gradients, 0)
    exchange.wait((0, 1, 2, 3))


def piece_shapes():
    return [(rows, 7, 4, C) for rows in (11, 7, 4, 3, 3)]


PARTS = [(JOBS, 2, 4, 4, 4, 4, 512)]
SAVED = [
    jax.ShapeDtypeStruct((2, C, 512), BF16),
    jax.ShapeDtypeStruct((2, HEADS // GROUP, 1, 4 * MAIN), F32),
    jax.ShapeDtypeStruct((2, 1, 128), F32),
]
TOKENS = (14, 7, 8, C)
IN_VMEM = pl.BlockSpec(memory_space=pltpu.VMEM)


ANYWHERE = pl.BlockSpec(memory_space=pl.ANY)
IN_HBM = pl.BlockSpec(memory_space=pltpu.HBM)


def call(
    kernel, name, args, out_shape, scratch, vmem, there=(), far=(), semaphores=(), collective_id=None
):
    return pl.pallas_call(
        kernel,
        in_specs=[IN_HBM if i in far else IN_VMEM for i in range(len(args))],
        out_specs=[ANYWHERE if i in there else IN_VMEM for i in range(len(out_shape))],
        out_shape=out_shape,
        scratch_shapes=[pltpu.VMEM(shape, dtype) for shape, dtype in scratch]
        + [pltpu.SemaphoreType.DMA(shape) for shape in semaphores],
        compiler_params=pltpu.CompilerParams(
            vmem_limit_bytes=vmem * MIB,
            has_side_effects=collective_id is not None,
            collective_id=collective_id,
        ),
        name=name,
    )(*args)


def halves(shapes):
    return [jax.ShapeDtypeStruct(shape, BF16) for shape in shapes]


def forward_first(x, cot, weights):
    pieces = piece_shapes()
    outs = call(
        forward_kernel,
        "forward_first",
        (x, cot, *weights),
        SAVED + halves(pieces * 2),
        [(shape, BF16) for shape in (pieces[1], *pieces[3:], pieces[1])]
        + [((C, 4 * MAIN), BF16), ((TOK, C), BF16), ((C, TOK), BF16)]
        + [(x.shape, BF16), (cot.shape, BF16)]
        + [(weight.shape, weight.dtype) for weight in weights],
        vmem=52,
        far=range(6),
        there=(4, 6, 7, 9),
        semaphores=[(5,), (5,), (6,)],
        collective_id=1,
    )
    return outs[:3], outs[3:8], outs[8:]


GRADIENT_SCRATCH = [
    ((C, 1024), BF16), ((1024, 3 * C), BF16), ((1024, C), BF16), ((C, 1024), BF16), ((C, 3 * C), BF16), ((C, C), F32),
]


def backward_first(scale, x, weights, saved, pieces, parts):
    both = 2 * JOBS
    args = (x, *weights, *saved, *pieces, parts)
    return call(
        functools.partial(backward_first_kernel, scale),
        "backward_first",
        args,
        halves([TOKENS]) + [jax.ShapeDtypeStruct((4, width), F32) for width in (3 * C, C)] * 2,
        GRADIENT_SCRATCH
        + [(PARTS[0], BF16)]
        + [
            ((2, C, 4 * MAIN), BF16), ((2, TOK, C), BF16), ((2, C, TOK), BF16), ((2, TOK, C), BF16),
            ((2, TOK, C), BF16), ((2, TOK, C), BF16), ((2, C, 4 * MAIN), BF16),
            ((2, TOK, 4 * MAIN), BF16), ((2, TOK, 4 * MAIN), BF16), ((2, 128, MAIN), F32),
            ((2, 4 * MAIN, 128), BF16), ((2, 4 * MAIN, 128), BF16),
            ((2, TOK, C), F32), ((2, TOK, C), F32), ((2, TOK, 1), F32),
            ((2, TOK, C), F32), ((2, TOK, C), F32), ((2, LEFT, C), F32),
        ]
        + [((both, 4, 4, 4, 4, 512), BF16)] * 3
        + [((both, 4, 4, 4, 512), BF16), ((both, 4, 4, 512), BF16)],
        vmem=46,
        far=(len(args) - 1,),
        semaphores=[(JOBS,), (both, 19), (both, 19)],
        collective_id=3,
    )


def hand_on_kernel(*refs):
    for source, target in zip(refs[:5], refs[5:]):
        target[...] = source[...]


def handed_on(outs):
    return call(
        hand_on_kernel,
        "hand_on",
        outs,
        [jax.ShapeDtypeStruct(out.shape, out.dtype) for out in outs],
        [],
        vmem=8,
    )


def second_block(scale, y_pieces, c_pieces, weights):
    return call(
        functools.partial(second_kernel, scale),
        "second_block",
        (*y_pieces, *c_pieces, *weights),
        halves(piece_shapes() + PARTS),
        GRADIENT_SCRATCH
        + [
            ((C, 2048), BF16), ((TOK, C), BF16), ((C, 512), BF16), ((TOK, C), BF16),
            ((C, 512), BF16), ((TOK, C), BF16), ((C, 512), BF16),
            ((128, 2048), BF16), ((128, 512), BF16), ((128, 512), BF16),
            ((224 + VIRTUAL, 1024), BF16), ((168 + VIRTUAL, 1024), BF16),
            ((224, 1024), BF16), ((168, 1024), BF16),
            ((2048, 128), BF16), ((2048, 128), BF16),
            ((TOK, 256), F32), ((TOK, C), F32), ((TOK, C), F32),
        ]
        + [(shape, BF16) for shape in piece_shapes()[1:] + piece_shapes()[2:] + piece_shapes()[2:3]],
        vmem=28,
        there=range(1, 5),
        semaphores=[(8,)] * 2,
        collective_id=2,
    )


def per_device(
    video_clip, cotangent,
    gain_first, bias_first, qkv_first, out_first,
    gain_second, bias_second, qkv_second, out_second,
):
    frames, rows_here, columns, channels = video_clip.shape
    devices = lax.axis_size("tm") * lax.axis_size("rows")
    scale = 1.0 / math.sqrt(frames * rows_here * columns * devices)
    x = video_clip.transpose(1, 2, 0, 3)
    cot = cotangent.transpose(1, 2, 0, 3)
    first = (gain_first.reshape(1, C), bias_first.reshape(1, C), qkv_first, out_first)
    second = (gain_second.reshape(1, C), bias_second.reshape(1, C), qkv_second, out_second)
    saved, y_pieces, c_pieces = forward_first(x, cot, first)
    *d_pieces, parts = second_block(scale, y_pieces, c_pieces, second)
    grad, *sums = handed_on(backward_first(scale, x, first, saved, d_pieces, parts))
    return (grad.transpose(2, 0, 1, 3), *sums)


def solution(mesh):
    clip = P("tm", "rows", None, None)
    scattered = P(("tm", "rows"), None)
    return jax.shard_map(
        per_device,
        mesh=mesh,
        in_specs=(clip, clip) + (P(),) * 8,
        out_specs=(clip,) + (scattered,) * 4,
        check_vma=False,
    )
```

```python
import functools
import math

import jax
import jax.numpy as jnp
from jax import lax
from jax.experimental import pallas as pl
from jax.experimental.pallas import tpu as pltpu
from jax.sharding import PartitionSpec as P

F32, BF16 = jnp.float32, jnp.bfloat16
C, HEADS, HD = 512, 16, 32
TOK = 392
GROUP = 4
LOG2E = math.log2(math.e)
QSCALE = HD ** (-0.5) * LOG2E
MASKED = -1000000000.0 * LOG2E
LN2 = math.log(2.0)
SPLIT = ((0, 224), (224, 392))
MAIN = 384
LEFT = TOK - MAIN
VIRTUAL = 16
ROWS = 400
MIB = 1024 * 1024


def mm(a, b):
    return lax.dot_general(a, b, (((1,), (0,)), ((), ())), preferred_element_type=F32)


def mm_nt(a, b):
    return lax.dot_general(a, b, (((1,), (1,)), ((), ())), preferred_element_type=F32)


def mm_tn(a, b):
    return lax.dot_general(a, b, (((0,), (0,)), ((), ())), preferred_element_type=F32)


def standardized(values):
    center = values - jnp.mean(values, axis=-1, keepdims=True)
    rstd = lax.rsqrt(jnp.mean(center * center, axis=-1, keepdims=True) + 1e-05)
    return center * rstd, rstd


def tiles(block):
    return block.astype(F32).reshape(-1, C)


def own_lanes(j, block):
    lane = lax.broadcasted_iota(jnp.int32, block.shape, 1) // HD
    return jnp.where(lane == j, block, jnp.zeros_like(block))


def put_diagonal(ref, turned, pitch, column=0):
    for head in range(HEADS):
        at = pitch * (head % GROUP) + column
        ref[HD * head : HD * (head + 1), at : at + turned.shape[1]] = turned[HD * head : HD * (head + 1)]


def left_rows(block):
    rows = jnp.concatenate([block.astype(F32)] * HEADS, axis=0)
    row = lax.broadcasted_iota(jnp.int32, rows.shape, 0) // LEFT
    lane = lax.broadcasted_iota(jnp.int32, rows.shape, 1) // HD
    return jnp.where(row == lane, rows, 0.0)


def from_left(product):
    turned = product.T
    row = lax.broadcasted_iota(jnp.int32, turned.shape, 0) // LEFT
    lane = lax.broadcasted_iota(jnp.int32, turned.shape, 1) // HD
    return jnp.sum(jnp.where(row == lane, turned, 0.0).reshape(HEADS, LEFT, C), axis=0)


def pair_channels(g, pair):
    return pl.ds(pl.multiple_of(g * 128 + pair * 64, 64), 64)


def channels_of(g, first=0):
    return pl.ds(pl.multiple_of(g * 128 + first, 128), 128)


def head_channels(g, j):
    return pl.ds(pl.multiple_of(g * 128 + j * HD, HD), HD)


MESH = pl.DeviceIdType.MESH
ROUTES = ((-1, 0), (1, 0), (0, -1), (1, -1))


class Exchange:
    def __init__(self, way, send_sem, recv_sem):
        self.way, self.sems, self.copies = way, (send_sem, recv_sem), []

    def device(self, steps, sign):
        size = lax.axis_size("tm"), lax.axis_size("rows")
        here = lax.axis_index("tm"), lax.axis_index("rows")
        return tuple((i + sign * d + n) % n for i, d, n in zip(here, steps, size))

    def greet(self, ways):
        self.ways = ways
        for way in ways:
            for steps in ROUTES:
                pl.semaphore_signal(
                    pltpu.get_barrier_semaphore(),
                    inc=1,
                    device_id=self.device(steps, -way),
                    device_id_type=MESH,
                )

    def wait_for_others(self):
        pl.semaphore_wait(pltpu.get_barrier_semaphore(), len(self.ways) * len(ROUTES))

    def send(self, route, source, target, way=None):
        i = len(self.copies)
        copy = pltpu.make_async_remote_copy(
            src_ref=source,
            dst_ref=target,
            send_sem=self.sems[0].at[i],
            recv_sem=self.sems[1].at[i],
            device_id=self.device(ROUTES[route], way or self.way),
            device_id_type=MESH,
        )
        copy.start()
        self.copies.append(copy)

    def wait_for(self, numbers):
        for i in numbers:
            self.copies[i].wait_recv()

    def wait(self, arrived=()):
        for i, copy in enumerate(self.copies):
            copy.wait_send()
            if i not in arrived:
                copy.wait_recv()


def pieces_of(whole, w, pieces):
    own, ahead, behind, above, corner = pieces
    if w == 0:
        above[...] = whole[0:3, :, 0:4].astype(BF16)
        corner[...] = whole[0:3, :, 4:8].astype(BF16)
        ahead[0:4] = whole[3:7, :, 0:4].astype(BF16)
        own[0:4] = whole[3:7, :, 4:8].astype(BF16)
    else:
        ahead[4:7] = whole[0:3, :, 0:4].astype(BF16)
        own[4:7] = whole[0:3, :, 4:8].astype(BF16)
        behind[...] = whole[3:7, :, 4:8].astype(BF16)
        own[7:11] = whole[3:7, :, 0:4].astype(BF16)


def joined(low, high):
    return jnp.concatenate([low.astype(F32), high.astype(F32)], axis=2)


def forward_kernel(
    x_far, cot_far, gain_far, bias_far, wqkv_far, wout_far, mixt_ref, stat_ref, stat_left, *refs,
):
    y_own, y_ahead_there, y_behind, y_above_there, y_corner_there = refs[0:5]
    c_own, c_ahead_there, *c_later = refs[5:10]
    y_ahead, y_above, y_corner, c_ahead, qbd, k, vt = refs[10:17]
    x_ref, cot_ref, gain_ref, bias_ref, wqkv_ref, wout_ref, send_sem, recv_sem, load_sem = refs[17:]
    loads = []
    for far, near in (
        (cot_far, cot_ref), (x_far, x_ref), (gain_far, gain_ref), (bias_far, bias_ref),
        (wqkv_far, wqkv_ref), (wout_far, wout_ref),
    ):
        loads.append(pltpu.make_async_copy(far, near, load_sem.at[len(loads)]))
        loads[-1].start()
    exchange = Exchange(1, send_sem, recv_sem)
    exchange.greet((1,))
    qbd[...] = jnp.zeros_like(qbd)
    loads[0].wait()
    for w in range(2):
        pieces_of(cot_ref[7 * w : 7 * w + 7].astype(F32), w, (c_own, c_ahead, *c_later))
    exchange.wait_for_others()
    exchange.send(0, c_ahead, c_ahead_there)
    for load in loads[1:4]:
        load.wait()
    for w in range(2):
        rows = slice(7 * w, 7 * w + 7)
        x = tiles(x_ref[rows])
        xhat, _ = standardized(x)
        normed = (xhat * gain_ref[...] + bias_ref[...]).astype(BF16)
        if w == 0:
            for load in loads[4:]:
                load.wait()
        queries = mm(normed, wqkv_ref[:, 0:C]) * QSCALE
        put_diagonal(qbd, queries[0:MAIN].astype(BF16).T, MAIN)
        k[...] = mm(normed, wqkv_ref[:, C : 2 * C]).astype(BF16)
        vt[...] = mm(normed, wqkv_ref[:, 2 * C :]).astype(BF16).T

        def group(g, carry):
            kg = k[:, channels_of(g)]
            for pair in range(2):
                lanes = slice(768 * pair, 768 * (pair + 1))
                scores = mm(kg, qbd[channels_of(g), lanes])
                top = jnp.max(scores, axis=0, keepdims=True)
                e = jnp.exp2(scores - top)
                sums = jnp.sum(e, axis=0, keepdims=True)
                mixed = mm(vt[pair_channels(g, pair), :], e.astype(BF16)) * (1.0 / sums)
                stat_ref[w, g, :, lanes] = top + jnp.log2(sums)
                for i in range(2):
                    mixt_ref[w, head_channels(g, 2 * pair + i), 0:MAIN] = mixed[
                        HD * i : HD * (i + 1), MAIN * i : MAIN * (i + 1)
                    ].astype(BF16)
            return carry

        lax.fori_loop(0, HEADS // GROUP, group, 0)
        scores = mm(k[...], left_rows(queries[MAIN:TOK]).astype(BF16).T)
        top = jnp.max(scores, axis=0, keepdims=True)
        e = jnp.exp2(scores - top)
        sums = jnp.sum(e, axis=0, keepdims=True)
        stat_left[w] = top + jnp.log2(sums)
        mixed = from_left(mm(vt[...], e.astype(BF16)) * (1.0 / sums))
        mixt_ref[w, :, MAIN:512] = jnp.concatenate(
            [mixed, jnp.zeros((128 - LEFT, C), F32)], axis=0
        ).T.astype(BF16)
        y = x + mm_tn(mixt_ref[w, :, 0:TOK], wout_ref[...])
        pieces_of(y.reshape(7, 7, 8, C), w, (y_own, y_ahead, y_behind, y_above, y_corner))
        if w == 0:
            exchange.send(2, y_above, y_above_there)
            exchange.send(3, y_corner, y_corner_there)
            exchange.send(0, y_ahead.at[0:4], y_ahead_there.at[0:4])
        else:
            exchange.send(0, y_ahead.at[4:7], y_ahead_there.at[4:7])
    exchange.wait()


def write_part(turn, block, part):
    def layer(z, carry):
        for xy in range(16):
            x, y = xy // 4, xy % 4
            rows = pl.ds(pl.multiple_of((z * 16 + x // 2 * 8 + y * 2 + x % 2) * 8, 8), 8)
            values = block[rows, :]
            first = jnp.where(turn == 0, x, jnp.where(turn == 1, y, z))
            second = jnp.where(turn == 0, y, jnp.where(turn == 1, z, x))
            third = jnp.where(turn == 0, z, jnp.where(turn == 1, x, y))
            part[0, first, second, third] = values[0:4].astype(BF16)
            part[1, first, second, third] = values[4:8].astype(BF16)
        return carry

    lax.fori_loop(0, 4, layer, 0)


def group_gradients(scale, g, turn, normed_t, dproj, mixt, cot_b, block, part):
    block[:, 0:384] = mm(normed_t[...], dproj[:, columns_of(g)]) * scale
    block[:, 384:512] = mm(mixt[...], cot_b[:, channels_of(g)]) * scale
    write_part(turn, block, part)


def columns_of(g):
    return pl.ds(pl.multiple_of(g * 384, 128), 384)


def clear_padding(by_rows, by_lanes):
    for w in range(2):
        padding = slice(512 * w + MAIN, 512 * (w + 1))
        for ref in by_rows:
            ref[padding] = jnp.zeros((128, ref.shape[1]), BF16)
        by_lanes[:, padding] = jnp.zeros((C, 128), BF16)


def sort_columns(sorted_ref, wqkv_ref):
    for g in range(HEADS // GROUP):
        for i in range(3):
            sorted_ref[:, 384 * g + 128 * i : 384 * g + 128 * (i + 1)] = wqkv_ref[
                :, C * i + 128 * g : C * i + 128 * (g + 1)
            ]


def norm_backward(dnormed, xhat, rstd, gain):
    d = dnormed.astype(BF16).astype(F32) * gain
    return rstd * (
        d
        - jnp.mean(d, axis=-1, keepdims=True)
        - xhat * jnp.mean(d * xhat, axis=-1, keepdims=True)
    )


def coordinates():
    tm, rows = lax.axis_index("tm"), lax.axis_index("rows")
    return {
        "x": tm // 4 % 2 * 2 + rows // 2,
        "y": tm % 4,
        "z": tm // 8,
        "core": rows % 2,
    }


def device_at(place):
    tm = place["z"] * 8 + place["x"] // 2 * 4 + place["y"]
    return (tm, place["x"] % 2 * 2 + place["core"])


def beside(here, axis, steps):
    return device_at({**here, axis: (here[axis] + steps) % (2 if axis == "core" else 4)})


ORDERS = ("xyz", "yzx", "zxy")


class Reduction:
    def __init__(self, order, plane, here, partners, part, local_sem, buffers, sems):
        self.plane = plane
        self.order, self.here, self.partners, self.part = order, here, partners, part
        self.held, self.other, *self.slots = buffers
        self.local_sem, self.sems = local_sem, sems

    def remote(self, number, source, target, partner):
        return pltpu.make_async_remote_copy(
            src_ref=source,
            dst_ref=target,
            send_sem=self.sems[0].at[number],
            recv_sem=self.sems[1].at[number],
            device_id=partner,
            device_id_type=MESH,
        )

    def local_copy(self):
        return pltpu.make_async_copy(self.part.at[self.here["core"]], self.held, self.local_sem)

    def core_copy(self):
        return self.remote(0, self.part.at[1 - self.here["core"]], self.other, self.partners["core", 1])

    def source(self, step):
        return self.held if step == 0 else self.slots[step - 1].at[3]

    def axis_copies(self, step):
        axis = self.order[step]
        return [
            self.remote(
                3 * step + away,
                self.source(step).at[(self.here[axis] + away) % 4],
                self.slots[step].at[away - 1],
                self.partners[axis, away],
            )
            for away in (1, 2, 3)
        ]

    def plane_copies(self):
        a, b = self.order[1:]
        copies = []
        for i in range(1, 16):
            da, db = i // 4, i % 4
            partner = (b, db) if da == 0 else (a, da) if db == 0 else (a, b, da, db)
            block = self.source(1).at[(self.here[a] + da) % 4, (self.here[b] + db) % 4]
            copies.append(self.remote(3 + i, block, self.slots[1].at[da, db], self.partners[partner]))
        return copies

    def copies(self, step):
        return self.plane_copies() if self.plane and step == 1 else self.axis_copies(step)

    def start(self):
        self.core_copy().start()

    def advance(self, stage, out=None):
        if stage == 0:
            self.core_copy().wait_recv()
            if self.local_sem is not None:
                self.local_copy().wait()
                own = self.held
            else:
                own = self.part.at[self.here["core"]]
            for i in range(4):
                self.held[i] = (own[i].astype(F32) + self.other[i].astype(F32)).astype(BF16)
        else:
            for copy in self.copies(stage - 1):
                copy.wait_recv()
            total = self.source(stage - 1)[self.here[self.order[stage - 1]]].astype(F32)
            if self.plane and stage == 2:
                a, b = self.order[1:]
                total = self.source(1)[self.here[a], self.here[b]].astype(F32)
                for i in range(1, 16):
                    total = total + self.slots[1][i // 4, i % 4].astype(F32)
                out(total)
                return
            for slot in range(3):
                total = total + self.slots[stage - 1][slot].astype(F32)
            if stage == 3:
                out(total)
                return
            self.slots[stage - 1][3] = total.astype(BF16)
        for copy in self.copies(stage):
            copy.start()

    def finish(self):
        self.core_copy().wait_send()
        for step in range(2 if self.plane else 3):
            for copy in self.copies(step):
                copy.wait_send()


JOBS = HEADS // GROUP
SECOND_STAGES = {0: 0, 2: 1, 3: 2}


def backward_first_kernel(
    scale,
    x_ref, gain_ref, bias_ref, wqkv_ref, wout_ref, mixt_far, stat_ref, stat_left,
    own, ahead, behind, above, corner, parts_second,
    grad_ref, gqkv1, gout1, gqkv2, gout2,
    normed_t, dproj, cot_b, mixt_all, wsorted, block, parts_first,
    qbd, k, kt, v, qn, don, dobd, p_s, ds_s, dqt, do_rows, q_rows, cot_s, xhat_s, rstd_s,
    dk_left, dv_left, dq_left, held, other, slots_a, slots_b, slots_c, local_sem, send_sem, recv_sem, load_sem,
):
    loads = [
        pltpu.make_async_copy(
            mixt_far.at[w], mixt_all.at[:, 512 * w : 512 * (w + 1)], load_sem.at[w]
        )
        for w in range(2)
    ]
    for load in loads:
        load.start()
    here = coordinates()
    partners = {("core", 1): beside(here, "core", 1)}
    for axis in "xyz":
        for away in (1, 2, 3):
            partners[axis, away] = beside(here, axis, away)
    for a, b in ("yz", "xy"):
        for da in (1, 2, 3):
            for db in (1, 2, 3):
                partners[a, b, da, db] = device_at(
                    {**here, a: (here[a] + da) % 4, b: (here[b] + db) % 4}
                )
    barrier = pltpu.get_barrier_semaphore()
    for partner in partners.values():
        pl.semaphore_signal(barrier, inc=1, device_id=partner, device_id_type=MESH)

    def job(i):
        of_first = i < JOBS
        g = i % JOBS
        return Reduction(
            ORDERS[g % 2 * 2] if of_first else ORDERS[g % 3],
            of_first,
            here,
            partners,
            parts_first.at[g] if of_first else parts_second.at[g],
            None if of_first else local_sem.at[g],
            [ref.at[i] for ref in (held, other, slots_a, slots_b, slots_c)],
            (send_sem.at[i], recv_sem.at[i]),
        )

    def result(i):
        gqkv, gout = (gqkv1, gout1) if i < JOBS else (gqkv2, gout2)
        g = i % JOBS

        def out(total):
            for part in range(3):
                at = C * part + 128 * g
                gqkv[:, at : at + 128] = total[:, 128 * part : 128 * (part + 1)]
            gout[:, 128 * g : 128 * (g + 1)] = total[:, 384:512]

        return out

    first, second = [job(i) for i in range(JOBS)], [job(JOBS + i) for i in range(JOBS)]
    for reduction in second:
        reduction.local_copy().start()
    for ref in (qbd, dobd):
        ref[...] = jnp.zeros_like(ref)
    clear_padding((dproj, cot_b), normed_t)
    sort_columns(wsorted, wqkv_ref)
    for w in range(2):
        xhat, rstd = standardized(tiles(x_ref[7 * w : 7 * w + 7]))
        xhat_s[w] = xhat
        rstd_s[w] = rstd
        normed = (xhat * gain_ref[...] + bias_ref[...]).astype(BF16)
        normed_t[:, 512 * w : 512 * w + TOK] = normed.T
        queries = (mm(normed, wqkv_ref[:, 0:C]) * QSCALE).astype(BF16)
        qn[w] = queries
        put_diagonal(qbd.at[w], queries[0:MAIN].T, MAIN)
        keys = mm(normed, wqkv_ref[:, C : 2 * C]).astype(BF16)
        k[w] = keys
        kt[w] = keys.T
        v[w] = mm(normed, wqkv_ref[:, 2 * C :]).astype(BF16)
        if w == 0:
            pieces = [joined(above[...], corner[...]), joined(ahead[0:4], own[0:4])]
        else:
            pieces = [joined(ahead[4:7], own[4:7]), joined(own[7:11], behind[...])]
        cot = jnp.concatenate([piece.reshape(-1, C) for piece in pieces], axis=0)
        cot_s[w] = cot
        cot_h = cot.astype(BF16)
        cot_b[512 * w : 512 * w + TOK] = cot_h
        dmixed = mm_nt(cot_h, wout_ref[...]).astype(BF16)
        don[w] = dmixed
        put_diagonal(dobd.at[w], dmixed[0:MAIN].T, MAIN)
        loads[w].wait()
        q_left = left_rows(queries[MAIN:TOK]).astype(BF16)
        do_left = left_rows(dmixed[MAIN:TOK])
        mixed = mixt_all[:, 512 * w + MAIN : 512 * (w + 1)].astype(F32).T[0:LEFT]
        dsum = jnp.sum((do_left * jnp.concatenate([mixed] * HEADS, axis=0)).T, axis=0, keepdims=True)
        do_left = do_left.astype(BF16)
        p = jnp.exp2(mm(k[w], q_left.T) - stat_left[w])
        ds = (p * (mm(v[w], do_left.T) - dsum)).astype(BF16)
        dv_left[w] = mm(p.astype(BF16), do_left)
        dk_left[w] = mm(ds, q_left)
        dq_left[w] = from_left(mm(kt[w], ds))
        if w == 0:
            pl.semaphore_wait(barrier, len(partners))
            for reduction in second:
                reduction.start()

    def group(g, carry):
        for w in range(2):
            kg = k[w, :, channels_of(g)]
            vg = v[w, :, channels_of(g)]
            qg = qn[w, :, channels_of(g)]
            dog = don[w, :, channels_of(g)]
            for j in range(GROUP):
                do_rows[w, MAIN * j : MAIN * (j + 1)] = own_lanes(j, dog[0:MAIN])
                q_rows[w, MAIN * j : MAIN * (j + 1)] = own_lanes(j, qg[0:MAIN])
            for pair in range(2):
                lanes = slice(768 * pair, 768 * (pair + 1))
                scores = mm(kg, qbd[w, channels_of(g), lanes])
                p = jnp.exp2(scores - stat_ref[w, g, :, lanes]).astype(BF16)
                p_s[w, :, lanes] = p
                dsums = []
                for j in (2 * pair, 2 * pair + 1):
                    dsums.append(
                        jnp.sum(
                            mixt_all[head_channels(g, j), 512 * w : 512 * w + MAIN].astype(F32)
                            * dobd[w, head_channels(g, j), MAIN * j : MAIN * (j + 1)].astype(F32),
                            axis=0, keepdims=True,
                        )
                    )
                dp = mm(vg, dobd[w, channels_of(g), lanes]) - jnp.concatenate(dsums, axis=1)
                ds = (p.astype(F32) * dp).astype(BF16)
                ds_s[w, :, lanes] = ds
                dq = mm(kt[w, pair_channels(g, pair), :], ds)
                for i in range(2):
                    j = 2 * pair + i
                    dqt[w, HD * j : HD * (j + 1), :] = dq[HD * i : HD * (i + 1), MAIN * i : MAIN * (i + 1)]
            dk = (mm(ds_s[w], q_rows[w]) + dk_left[w, :, channels_of(g)]) * LN2
            dv = mm(p_s[w], do_rows[w]) + dv_left[w, :, channels_of(g)]
            dq = jnp.concatenate([dqt[w].T, dq_left[w, :, channels_of(g)]], axis=0) * HD ** (-0.5)
            dproj[512 * w : 512 * w + TOK, columns_of(g)] = jnp.concatenate(
                [dq.astype(BF16), dk.astype(BF16), dv.astype(BF16)], axis=1
            )
        group_gradients(scale, g, g % 2 * 2, normed_t, dproj, mixt_all, cot_b, block, parts_first.at[g])
        for now in range(JOBS):

            @pl.when(g == now)
            def _():
                first[now].start()
                for i in range(JOBS):
                    if now in SECOND_STAGES:
                        second[i].advance(SECOND_STAGES[now])
                for i in range(now):
                    first[i].advance(now - 1 - i, result(i))

        return carry

    lax.fori_loop(0, JOBS, group, 0)
    for now in range(JOBS, 2 * JOBS - 1):
        w = now - JOBS
        if w < 2:
            dnormed = mm_nt(dproj[512 * w : 512 * w + TOK], wsorted[...])
            total = cot_s[w] + norm_backward(dnormed, xhat_s[w], rstd_s[w], gain_ref[...])
            grad_ref[7 * w : 7 * w + 7] = total.reshape(7, 7, 8, C).astype(BF16)
        for i in reversed(range(JOBS)):
            if 0 <= now - 1 - i <= 2:
                first[i].advance(now - 1 - i, result(i))
        if now == JOBS:
            for i in range(JOBS):
                second[i].advance(3, result(JOBS + i))
    for reduction in first + second:
        reduction.finish()


def second_kernel(
    scale,
    y_own, y_ahead, y_behind_here, y_above, y_corner, c_own, c_ahead, c_behind_here, c_above_here, c_corner_here,
    gain_ref, bias_ref, wqkv_ref, wout_ref,
    own, ahead_there, behind_there, above_there, corner_there, parts,
    normed_t, dproj, cot_b, mixt, wsorted, block, qbd, k, kt, v, vt, qn, dot_s, dobd, dopt, dqt,
    e_a, e_b, ds_a, ds_b, do_rows, q_rows, pen, cot_s, xhat_s,
    ahead, behind, above, corner, c_behind, c_above, c_corner, y_behind, send_sem, recv_sem,
):
    exchange = Exchange(-1, send_sem, recv_sem)
    exchange.greet((1, -1))
    e_s, ds_s = (e_a, e_b), (ds_a, ds_b)
    for ref in (qbd, dobd, q_rows, cot_b, mixt):
        ref[...] = jnp.zeros_like(ref)
    clear_padding((dproj,), normed_t)
    sort_columns(wsorted, wqkv_ref)
    for w in range(2):
        base = 512 * w
        last_frames = lax.axis_index("tm") == (lax.axis_size("tm") - 1 if w == 0 else 0)
        last_rows = (lax.axis_index("rows") == lax.axis_size("rows") - 1) if w == 1 else False

        def region_of(token, segment):
            columns = 4 if segment == 0 else 3
            late = jnp.where(last_frames & (token % 8 < 4), 1, 0)
            below = jnp.where(last_rows & (token // 8 // columns >= 4), 2, 0)
            return late + below

        def gather(into, own, ahead, behind, above, corner):
            def put(rho, count, whole):
                into[32 * rho : 32 * (rho + count)] = whole[:, 3:7].reshape(-1, C)
                into[224 + 24 * rho : 224 + 24 * (rho + count)] = whole[:, 0:3].reshape(-1, C)

            if w == 0:
                put(0, 7, joined(ahead[...], own[0:7]))
            else:
                put(0, 4, joined(own[7:11], behind[...]))
                put(4, 3, joined(above[...], corner[...]))

        if w == 1:
            exchange.wait_for((0, 1, 2, 3))
        gather(xhat_s, y_own, y_ahead, y_behind, y_above, y_corner)
        gather(cot_s, c_own, c_ahead, c_behind, c_above, c_corner)
        xhat, rstd = standardized(xhat_s[...])
        xhat_s[...] = xhat
        normed = (xhat * gain_ref[...] + bias_ref[...]).astype(BF16)
        normed_t[:, base : base + TOK] = normed.T
        queries = (mm(normed, wqkv_ref[:, 0:C]) * QSCALE).astype(BF16)
        qn[...] = queries
        keys = mm(normed, wqkv_ref[:, C : 2 * C]).astype(BF16)
        k[...] = keys
        values_f = mm(normed, wqkv_ref[:, 2 * C :])
        values = values_f.astype(BF16)
        v[...] = values
        cot_h = cot_s[...].astype(BF16)
        dmixed = mm_nt(cot_h, wout_ref[...]).astype(BF16)
        for s, (start, stop) in enumerate(SPLIT):
            count = stop - start
            cot_b[512 * w + 256 * s : 512 * w + 256 * s + count] = cot_h[start:stop]
            put_diagonal(qbd, queries[start:stop].T, 256, 1024 * s)
            kt[:, 256 * s : 256 * s + count] = keys[start:stop].T
            dot_s[:, 256 * s : 256 * s + count] = dmixed[start:stop].T
            turned = values[start:stop].T
            vt[:, 256 * s : 256 * s + count] = turned
            total = jnp.sum(turned.astype(F32), axis=1, keepdims=True)
            other = 1 - s
            lane = 256 * other + SPLIT[other][1] - SPLIT[other][0]
            first = lax.broadcasted_iota(jnp.int32, (C, VIRTUAL), 1) == 0
            vt[:, lane : lane + VIRTUAL] = jnp.where(first, total, 0.0).astype(BF16)
            shape = (count, 256)
            key = region_of(lax.broadcasted_iota(jnp.int32, shape, 0), s)
            query = region_of(lax.broadcasted_iota(jnp.int32, shape, 1), s)
            pen[start:stop] = jnp.where(key == query, 0.0, 1.0)

        if w == 0:
            exchange.wait_for_others()
            exchange.send(1, y_behind_here, y_behind, 1)
            exchange.send(1, c_behind_here, c_behind, 1)
            exchange.send(2, c_above_here, c_above, 1)
            exchange.send(3, c_corner_here, c_corner, 1)

        def group(g, carry):
            virtual_dv = []
            grads = []
            for s, (start, stop) in enumerate(SPLIT):
                count = stop - start
                kg = k[start:stop, channels_of(g)]
                apart = jnp.concatenate([pen[start:stop]] * 2, axis=1) > 0.5
                sums_of, invs = [], []
                for pair in range(2):
                    lanes = slice(512 * pair, 512 * (pair + 1))
                    scores = mm(kg, qbd[channels_of(g), 1024 * s + 512 * pair : 1024 * s + 512 * (pair + 1)])
                    scores = jnp.where(apart, MASKED, scores)
                    top = jnp.maximum(jnp.max(scores, axis=0, keepdims=True), MASKED)
                    e = jnp.exp2(scores - top)
                    e_s[s][0:count, lanes] = e.astype(BF16)
                    rest = jnp.exp2(MASKED - top)
                    first = lax.broadcasted_iota(jnp.int32, (VIRTUAL, 512), 0) == 0
                    e_s[s][count : count + VIRTUAL, lanes] = jnp.where(first, rest, 0.0).astype(BF16)
                    inv = 1.0 / (jnp.sum(e, axis=0, keepdims=True) + (TOK - count) * rest)
                    invs += [inv[:, 0:256], inv[:, 256:512]]
                for j in range(GROUP):
                    lanes = slice(256 * j, 256 * (j + 1))
                    tokens = slice(256 * s, 256 * (s + 1))
                    inv = invs[j]
                    mixed = inv * mm(
                        vt[head_channels(g, j), 256 * s : 256 * s + count + VIRTUAL], e_s[s][:, lanes]
                    )
                    mixt[head_channels(g, j), 512 * w + 256 * s : 512 * w + 256 * s + count] = mixed[
                        :, 0:count
                    ].astype(BF16)
                    do = dot_s[head_channels(g, j), tokens].astype(F32) * inv
                    inside = lax.broadcasted_iota(jnp.int32, do.shape, 1) < count
                    do = jnp.where(inside, do, 0.0).astype(BF16)
                    sums_of.append(jnp.sum(mixed * do.astype(F32), axis=0, keepdims=True))
                    dopt[HD * j : HD * (j + 1), tokens] = do
                    dobd[HD * j : HD * (j + 1), 1024 * s + 256 * j : 1024 * s + 256 * (j + 1)] = do
                turned = dopt[:, 256 * s : 256 * (s + 1)].T
                qg = qn[start:stop, channels_of(g)]
                for j in range(GROUP):
                    at = 1024 * s + 256 * j
                    do_rows[at : at + 256] = own_lanes(j, turned)
                    q_rows[at : at + count] = own_lanes(j, qg)
                for pair in range(2):
                    lanes = slice(512 * pair, 512 * (pair + 1))
                    at = 1024 * s + 512 * pair
                    dsum = jnp.concatenate(sums_of[2 * pair : 2 * pair + 2], axis=1)
                    dp = mm(v[start:stop, channels_of(g)], dobd[:, at : at + 512]) - dsum
                    ds = e_s[s][0:count, lanes].astype(F32) * jnp.where(apart, 0.0, dp)
                    ds_s[s][:, lanes] = ds.astype(BF16)
                for j in range(GROUP):
                    lanes = slice(256 * j, 256 * (j + 1))
                    dq = mm(kt[head_channels(g, j), 256 * s : 256 * s + count], ds_s[s][:, lanes])
                    dqt[HD * j : HD * (j + 1), 256 * s : 256 * (s + 1)] = (dq * HD ** (-0.5)).astype(BF16)
                block = slice(1024 * s, 1024 * (s + 1))
                dv = mm(e_s[s][...], do_rows[block])
                dk = mm(ds_s[s][...], q_rows[block]) * LN2
                virtual_dv.append(dv[count : count + 1])
                grads.append((dk, dv[0:count]))
            for s, (start, stop) in enumerate(SPLIT):
                rows = slice(base + start, base + stop)
                dk, dv = grads[s]
                dproj[rows, columns_of(g)] = jnp.concatenate(
                    [
                        dqt[:, 256 * s : 256 * s + stop - start].T,
                        dk.astype(BF16),
                        (dv + virtual_dv[1 - s]).astype(BF16),
                    ],
                    axis=1,
                )
            return carry

        lax.fori_loop(0, HEADS // GROUP, group, 0)
        dnormed = mm_nt(dproj[base : base + TOK], wsorted[...])
        total = cot_s[...] + norm_backward(dnormed, xhat_s[...], rstd, gain_ref[...])
        whole = jnp.concatenate(
            [total[224:392].reshape(7, 3, 8, C), total[0:224].reshape(7, 4, 8, C)], axis=1
        )
        low, high = whole[:, :, 0:4].astype(BF16), whole[:, :, 4:8].astype(BF16)
        if w == 0:
            ahead[...] = low
            own[0:7] = high
            exchange.send(0, ahead, ahead_there)
        else:
            own[7:11] = low[0:4]
            behind[...] = high[0:4]
            above[...] = low[4:7]
            corner[...] = high[4:7]
            exchange.send(1, behind, behind_there)
            exchange.send(2, above, above_there)
            exchange.send(3, corner, corner_there)

    def gradients(g, carry):
        group_gradients(scale, g, g % 3, normed_t, dproj, mixt, cot_b, block, parts.at[g])
        return carry

    lax.fori_loop(0, JOBS, gradients, 0)
    exchange.wait((0, 1, 2, 3))


def piece_shapes():
    return [(rows, 7, 4, C) for rows in (11, 7, 4, 3, 3)]


PARTS = [(JOBS, 2, 4, 4, 4, 4, 512)]
SAVED = [
    jax.ShapeDtypeStruct((2, C, 512), BF16),
    jax.ShapeDtypeStruct((2, HEADS // GROUP, 1, 4 * MAIN), F32),
    jax.ShapeDtypeStruct((2, 1, 128), F32),
]
TOKENS = (14, 7, 8, C)
IN_VMEM = pl.BlockSpec(memory_space=pltpu.VMEM)


ANYWHERE = pl.BlockSpec(memory_space=pl.ANY)
IN_HBM = pl.BlockSpec(memory_space=pltpu.HBM)


def call(
    kernel, name, args, out_shape, scratch, vmem, there=(), far=(), semaphores=(), collective_id=None
):
    return pl.pallas_call(
        kernel,
        in_specs=[IN_HBM if i in far else IN_VMEM for i in range(len(args))],
        out_specs=[ANYWHERE if i in there else IN_VMEM for i in range(len(out_shape))],
        out_shape=out_shape,
        scratch_shapes=[pltpu.VMEM(shape, dtype) for shape, dtype in scratch]
        + [pltpu.SemaphoreType.DMA(shape) for shape in semaphores],
        compiler_params=pltpu.CompilerParams(
            vmem_limit_bytes=vmem * MIB,
            has_side_effects=collective_id is not None,
            collective_id=collective_id,
        ),
        name=name,
    )(*args)


def halves(shapes):
    return [jax.ShapeDtypeStruct(shape, BF16) for shape in shapes]


def forward_first(x, cot, weights):
    pieces = piece_shapes()
    outs = call(
        forward_kernel,
        "forward_first",
        (x, cot, *weights),
        SAVED + halves(pieces * 2),
        [(shape, BF16) for shape in (pieces[1], *pieces[3:], pieces[1])]
        + [((C, 4 * MAIN), BF16), ((TOK, C), BF16), ((C, TOK), BF16)]
        + [(x.shape, BF16), (cot.shape, BF16)]
        + [(weight.shape, weight.dtype) for weight in weights],
        vmem=52,
        far=range(6),
        there=(4, 6, 7, 9),
        semaphores=[(5,), (5,), (6,)],
        collective_id=1,
    )
    return outs[:3], outs[3:8], outs[8:]


GRADIENT_SCRATCH = [
    ((C, 1024), BF16), ((1024, 3 * C), BF16), ((1024, C), BF16), ((C, 1024), BF16), ((C, 3 * C), BF16), ((C, C), F32),
]


def backward_first(scale, x, weights, saved, pieces, parts):
    both = 2 * JOBS
    args = (x, *weights, *saved, *pieces, parts)
    return call(
        functools.partial(backward_first_kernel, scale),
        "backward_first",
        args,
        halves([TOKENS]) + [jax.ShapeDtypeStruct((4, width), F32) for width in (3 * C, C)] * 2,
        GRADIENT_SCRATCH
        + [(PARTS[0], BF16)]
        + [
            ((2, C, 4 * MAIN), BF16), ((2, TOK, C), BF16), ((2, C, TOK), BF16), ((2, TOK, C), BF16),
            ((2, TOK, C), BF16), ((2, TOK, C), BF16), ((2, C, 4 * MAIN), BF16),
            ((2, TOK, 4 * MAIN), BF16), ((2, TOK, 4 * MAIN), BF16), ((2, 128, MAIN), F32),
            ((2, 4 * MAIN, 128), BF16), ((2, 4 * MAIN, 128), BF16),
            ((2, TOK, C), F32), ((2, TOK, C), F32), ((2, TOK, 1), F32),
            ((2, TOK, C), F32), ((2, TOK, C), F32), ((2, LEFT, C), F32),
        ]
        + [((both, 4, 4, 4, 4, 512), BF16)] * 3
        + [((both, 4, 4, 4, 512), BF16), ((both, 4, 4, 512), BF16)],
        vmem=46,
        far=(5, len(args) - 1),
        semaphores=[(JOBS,), (both, 19), (both, 19), (2,)],
        collective_id=3,
    )


def hand_on_kernel(*refs):
    for source, target in zip(refs[:5], refs[5:]):
        target[...] = source[...]


def handed_on(outs):
    return call(
        hand_on_kernel,
        "hand_on",
        outs,
        [jax.ShapeDtypeStruct(out.shape, out.dtype) for out in outs],
        [],
        vmem=8,
    )


def second_block(scale, y_pieces, c_pieces, weights):
    return call(
        functools.partial(second_kernel, scale),
        "second_block",
        (*y_pieces, *c_pieces, *weights),
        halves(piece_shapes() + PARTS),
        GRADIENT_SCRATCH
        + [
            ((C, 2048), BF16), ((TOK, C), BF16), ((C, 512), BF16), ((TOK, C), BF16),
            ((C, 512), BF16), ((TOK, C), BF16), ((C, 512), BF16),
            ((128, 2048), BF16), ((128, 512), BF16), ((128, 512), BF16),
            ((224 + VIRTUAL, 1024), BF16), ((168 + VIRTUAL, 1024), BF16),
            ((224, 1024), BF16), ((168, 1024), BF16),
            ((2048, 128), BF16), ((2048, 128), BF16),
            ((TOK, 256), F32), ((TOK, C), F32), ((TOK, C), F32),
        ]
        + [(shape, BF16) for shape in piece_shapes()[1:] + piece_shapes()[2:] + piece_shapes()[2:3]],
        vmem=28,
        there=range(1, 5),
        semaphores=[(8,)] * 2,
        collective_id=2,
    )


def per_device(
    video_clip, cotangent,
    gain_first, bias_first, qkv_first, out_first,
    gain_second, bias_second, qkv_second, out_second,
):
    frames, rows_here, columns, channels = video_clip.shape
    devices = lax.axis_size("tm") * lax.axis_size("rows")
    scale = 1.0 / math.sqrt(frames * rows_here * columns * devices)
    x = video_clip.transpose(1, 2, 0, 3)
    cot = cotangent.transpose(1, 2, 0, 3)
    first = (gain_first.reshape(1, C), bias_first.reshape(1, C), qkv_first, out_first)
    second = (gain_second.reshape(1, C), bias_second.reshape(1, C), qkv_second, out_second)
    saved, y_pieces, c_pieces = forward_first(x, cot, first)
    *d_pieces, parts = second_block(scale, y_pieces, c_pieces, second)
    grad, *sums = handed_on(backward_first(scale, x, first, saved, d_pieces, parts))
    return (grad.transpose(2, 0, 1, 3), *sums)


def solution(mesh):
    clip = P("tm", "rows", None, None)
    scattered = P(("tm", "rows"), None)
    return jax.shard_map(
        per_device,
        mesh=mesh,
        in_specs=(clip, clip) + (P(),) * 8,
        out_specs=(clip,) + (scattered,) * 4,
        check_vma=False,
    )
```
